32 devices in a mesh: dp: 32 (over z, y, x, core).
Axes of the slice: x: 2, y: 2, z: 4, core: 2. Of those that a mesh axis runs over, the one named last changes fastest.
Arguments:
- tokens: bfloat16 [40960, 768], P('dp'), may hold values from -6 to 6
- cotangent: bfloat16 [40960, 768], P('dp'), may hold values from -6 to 6
- loss_mask: int32 [40960], P('dp'), may hold values from 0 to 1, as said below
- bucket_perm: int32 [32], replicated, may hold values from 0 to 31, as said below
- short_lengths: int32 [24, 3], replicated, may hold values from 1 to 512, 1024 in all within a row
- row_owner: int32 [40960], P('dp'), may hold values from 0 to 31, as said below
- row_slot: int32 [40960], P('dp'), may hold values from 0 to 2047, as said below
- first_gain: float32 [768], P('dp'), may hold values from 0.25 to 1.75
- first_shift: float32 [768], P('dp'), may hold values from -1.25 to 1.25
- second_gain: float32 [768], P('dp'), may hold values from 0.25 to 1.75
- second_shift: float32 [768], P('dp'), may hold values from -1.25 to 1.25
- project_weight: float32 [768, 2304], P('dp'), may hold values from -0.21875 to 0.21875
- project_bias: float32 [2304], P('dp'), may hold values from -1.25 to 1.25
- output_weight: float32 [768, 768], P('dp'), may hold values from -0.875 to 0.875
- output_bias: float32 [768], P('dp'), may hold values from -1.25 to 1.25
- up_weight: float32 [768, 3072], P('dp'), may hold values from -0.21875 to 0.21875
- up_bias: float32 [3072], P('dp'), may hold values from -1.25 to 1.25
- down_weight: float32 [3072, 768], P('dp'), may hold values from -0.109375 to 0.109375
- down_bias: float32 [768], P('dp'), may hold values from -1.25 to 1.25
Outputs:
- block_out: bfloat16 [40960, 768], P('dp')
- tokens_grad: bfloat16 [40960, 768], P('dp')
- first_gain_grad: float32 [768], P('dp')
- first_shift_grad: float32 [768], P('dp')
- second_gain_grad: float32 [768], P('dp')
- second_shift_grad: float32 [768], P('dp')
- project_weight_grad: float32 [768, 2304], P('dp')
- project_bias_grad: float32 [2304], P('dp')
- output_weight_grad: float32 [768, 768], P('dp')
- output_bias_grad: float32 [768], P('dp')
- up_weight_grad: float32 [768, 3072], P('dp')
- up_bias_grad: float32 [3072], P('dp')
- down_weight_grad: float32 [3072, 768], P('dp')
- down_bias_grad: float32 [768], P('dp')
The draws below stay inside these ranges and needn't reach their ends.
Inputs may be any that keep to these rules, and one draw needn't show every extreme that they name: `bucket_perm`: each device owns exactly one bucket. `row_owner`: the tokens of one device go to every device: exactly 64 to the owner of each long bucket and 32 to the owner of each short bucket. `row_slot`: with row_owner, each place 0 to 2047 of a long bucket and 0 to 1023 of a short bucket is named by exactly one token. `loss_mask`: the first token of each device carries loss.
All inputs are finite; a program needn't handle non-finite values.
Results may differ from the reference program's by a relative error of at most 0.012.
The reference program's roundings to bfloat16 on the way count: a program that leaves them out, or rounds other values in their place, can miss the bound.
Values may be sent and summed in bfloat16 or wider, within the bound.
No kernel may reach another device: no remote copies, remote signals or barrier semaphores. Data moves between devices by JAX's collectives and lax.ppermute only.
A program may use at most 320 MiB of HBM per device.

```python
import math
import jax
import jax.numpy as jnp
import numpy as np
from jax import lax

D = 768
HEADS = 12
HEAD_DIM = 64
ROT = 16
FF = 3072
LONG = 2048
SHORT = 512
SENTS = 3
SHORT_TOK = 1024
QBLK = 512
LONG_BUCKETS = 8
SHORT_BUCKETS = 24
TOK_DEV = 1280
TOKENS = 40960
N_DP = 32


def shuffle_long(key):
    return jax.random.permutation(key, LONG).astype(jnp.int32)


def shuffle_short(key):
    return jax.random.permutation(key, SHORT_TOK).astype(jnp.int32)


def arrange(key):
    devices = TOKENS // TOK_DEV
    order = jax.random.permutation(jax.random.fold_in(key, 101), devices).astype(jnp.int32)
    bucket = jnp.zeros((devices,), jnp.int32).at[order].set(jnp.arange(devices, dtype=jnp.int32))
    is_long = bucket < LONG_BUCKETS
    long_keys = jax.random.split(jax.random.fold_in(key, 102), devices)
    short_keys = jax.random.split(jax.random.fold_in(key, 103), devices)
    long_order = jax.vmap(shuffle_long)(long_keys)
    short_order = jax.vmap(shuffle_short)(short_keys)
    short_wide = jnp.concatenate([short_order, jnp.zeros((devices, LONG - SHORT_TOK), jnp.int32)], 1)
    sender = jnp.where(is_long[:, None], long_order // (LONG // devices), short_wide // (SHORT_TOK // devices))
    used = is_long[:, None] | (jnp.arange(LONG, dtype=jnp.int32)[None, :] < SHORT_TOK)
    sender = jnp.where(used, sender, devices)
    entries = devices * LONG
    tiebreak = jax.random.permutation(jax.random.fold_in(key, 104), entries).astype(jnp.int32)
    ranked = jnp.argsort(sender.reshape(-1) * entries + tiebreak)[:TOKENS].astype(jnp.int32)
    return (order, ranked // LONG, ranked % LONG)


def draw_bucket_perm(key, part):
    order, owners, slots = arrange(key)
    return order


def draw_row_owner(key, part):
    order, owners, slots = arrange(key)
    return owners


def draw_row_slot(key, part):
    order, owners, slots = arrange(key)
    return slots


def draw_loss_mask(key, part):
    key = jax.random.fold_in(key, 5)
    devices = TOKENS // TOK_DEV
    spots = jnp.arange(TOKENS, dtype=jnp.int32)
    device = spots // TOK_DEV
    level = jax.random.randint(key, (TOKENS,), 0, 4 * devices)
    picked = (level < devices + 2 * device).astype(jnp.int32)
    return jnp.where(spots % TOK_DEV == 0, 1, picked).astype(jnp.int32)


def block_levels(key, dims, shards, least, largest):
    def one(axis_at, shards_of):
        steps = jax.random.uniform(jax.random.fold_in(jax.random.fold_in(key, 6), axis_at), (shards_of,), jnp.float32, least / len(shards), largest / len(shards))
        return jnp.repeat(jnp.exp(steps), dims[axis_at] // shards_of).reshape((-1,) + (1,) * (len(dims) - axis_at - 1))

    loudness = one(*shards[0])
    for cut in shards[1:]:
        loudness = loudness * one(*cut)
    return loudness


def profile(count, total, reach, slope):
    loads = [(1 << 20) // math.isqrt(grade ** slope) + 1 for grade in range(2, count + 1)]
    spare, holding = total - reach - (count - 1), [1] * (count - 1)
    while spare > 0:
        free = [i for i in range(count - 1) if holding[i] < reach]
        pool, left = sum([loads[i] for i in free]), spare
        for i in free:
            extra = min(reach - holding[i], max(1, left * loads[i] // pool), spare)
            holding[i] = holding[i] + extra
            spare = spare - extra
    return np.array([reach] + holding)


def uneven_parts(stream_key, amount, total, most, slope):
    if amount == 2:
        one = jax.random.randint(stream_key, (), max(1, total - most), min(most, total - 1) + 1)
        return jnp.stack([one, total - one])
    tallies = jnp.asarray(profile(amount, total, most, slope), jnp.int32)
    pairs = (amount - 1) // 2
    source_of, receiver = tallies[1:1 + 2 * pairs:2], tallies[2:2 + 2 * pairs:2]
    margin = jnp.minimum(source_of - 1, most - receiver)
    moved = jax.random.randint(jax.random.fold_in(stream_key, 1), (pairs,), 0, 1 << 20) % (margin + 1)
    tallies = tallies.at[1:1 + 2 * pairs:2].set(source_of - moved).at[2:2 + 2 * pairs:2].set(receiver + moved)
    return tallies[jax.random.permutation(jax.random.fold_in(stream_key, 2), amount)]


def scatter_about(own_key, extent, width, limit, shards=(), kind=jnp.bfloat16):
    array = width * jax.random.normal(own_key, extent, jnp.float32)
    if shards:
        array = array * block_levels(own_key, extent, shards, -0.22, 0.18)
    return jnp.clip(array, -limit, limit).astype(kind)


def setup_inputs(seed: int = 0) -> dict:
    key_list = jax.random.split(jax.random.key(seed), 20)
    tokens = scatter_about(key_list[0], (TOKENS, D), 1.0, 6.0, ((0, 32),))
    cotangent = scatter_about(key_list[1], (TOKENS, D), 1.0, 6.0, ((0, 32),))
    loss_mask = draw_loss_mask(jax.random.fold_in(key_list[19], 71), 0)
    bucket_perm = draw_bucket_perm(jax.random.fold_in(key_list[19], 71), 0)
    short_lengths = jax.vmap(lambda own: uneven_parts(own, SENTS, SHORT_TOK, SHORT, 0))(jax.random.split(key_list[4], SHORT_BUCKETS)).reshape((SHORT_BUCKETS, SENTS)).astype(jnp.int32)
    row_owner = draw_row_owner(jax.random.fold_in(key_list[19], 71), 0)
    row_slot = draw_row_slot(jax.random.fold_in(key_list[19], 71), 0)
    first_gain = jnp.clip(1.0 + 0.15 * jax.random.normal(key_list[7], (D,), jnp.float32), 0.25, 1.75)
    first_shift = scatter_about(key_list[8], (D,), 0.2, 1.25, ((0, 32),), jnp.float32)
    second_gain = jnp.clip(1.0 + 0.15 * jax.random.normal(key_list[9], (D,), jnp.float32), 0.25, 1.75)
    second_shift = scatter_about(key_list[10], (D,), 0.2, 1.25, ((0, 32),), jnp.float32)
    project_weight = scatter_about(key_list[11], (D, 3 * D), D ** -0.5, 0.21875, ((0, 32),), jnp.float32)
    project_bias = scatter_about(key_list[12], (3 * D,), 0.2, 1.25, ((0, 32),), jnp.float32)
    output_weight = scatter_about(key_list[13], (D, D), (D * 128 // LONG) ** -0.5, 0.875, ((0, 32),), jnp.float32)
    output_bias = scatter_about(key_list[14], (D,), 0.2, 1.25, ((0, 32),), jnp.float32)
    up_weight = scatter_about(key_list[15], (D, FF), D ** -0.5, 0.21875, ((0, 32),), jnp.float32)
    up_bias = scatter_about(key_list[16], (FF,), 0.2, 1.25, ((0, 32),), jnp.float32)
    down_weight = scatter_about(key_list[17], (FF, D), FF ** -0.5, 0.109375, ((0, 32),), jnp.float32)
    down_bias = scatter_about(key_list[18], (D,), 0.2, 1.25, ((0, 32),), jnp.float32)
    return dict(tokens=tokens, cotangent=cotangent, loss_mask=loss_mask, bucket_perm=bucket_perm, short_lengths=short_lengths, row_owner=row_owner, row_slot=row_slot, first_gain=first_gain, first_shift=first_shift, second_gain=second_gain, second_shift=second_shift, project_weight=project_weight, project_bias=project_bias, output_weight=output_weight, output_bias=output_bias, up_weight=up_weight, up_bias=up_bias, down_weight=down_weight, down_bias=down_bias)


@jax.custom_vjp
def low(v):
    return lax.optimization_barrier(v.astype(jnp.bfloat16)).astype(jnp.float32)

@jax.custom_vjp
def low_back(v):
    return v

def low_keep(v):
    return (low(v), None)

def low_pass(kept, grad):
    return (grad,)

def back_keep(v):
    return (v, None)

def back_low(kept, grad):
    return (low(grad),)
low.defvjp(low_keep, low_pass)
low_back.defvjp(back_keep, back_low)
epsilon = 1e-05
highest = lax.Precision.HIGHEST

def product(left, right):
    return jnp.dot(left, right, precision=highest, preferred_element_type=jnp.float32)

def layer_norm(values, gain, shift):
    mean = lax.optimization_barrier(jnp.mean(values, -1, keepdims=True))
    centred = values - mean
    spread = lax.optimization_barrier(jnp.mean(centred * centred, -1, keepdims=True))
    return centred * lax.rsqrt(spread + epsilon) * gain + shift

def angles(position):
    freq = 10000.0 ** (-2.0 * jnp.arange(ROT // 2).astype(jnp.float32) / ROT)
    phase = position.astype(jnp.float32)[:, None] * freq[None, :]
    return (jnp.cos(phase), jnp.sin(phase))

def turn(values, cosine, sine):
    count = values.shape[0]
    heads = values.reshape(count, HEADS, HEAD_DIM)
    half = ROT // 2
    first = heads[..., :half]
    second = heads[..., half:ROT]
    cosine = cosine[:, None]
    sine = sine[:, None]
    turned = jnp.concatenate([first * cosine - second * sine, second * cosine + first * sine, heads[..., ROT:]], -1)
    return turned.reshape(count, D)

def attend(queries, keys, values, docs):
    count = queries.shape[0]
    blocks = count // QBLK
    head_q = queries.reshape(blocks, QBLK, HEADS, HEAD_DIM)
    head_k = keys.reshape(count, HEADS, HEAD_DIM)
    head_v = values.reshape(count, HEADS, HEAD_DIM)
    spots = jnp.arange(count, dtype=jnp.int32)

    @jax.checkpoint
    def one_block(parts):
        block_q, block_doc, block_spot = parts
        score = jnp.einsum('qhd,khd->hqk', block_q, head_k, precision=highest, preferred_element_type=jnp.float32) * HEAD_DIM ** (-0.5)
        score = low_back(score)
        allowed = (block_doc[:, None] == docs[None, :]) & (block_spot[:, None] >= spots[None, :])
        score = jnp.where(allowed[None], score, -jnp.inf)
        peak = lax.optimization_barrier(jnp.max(score, -1, keepdims=True))
        expo = jnp.exp(score - peak)
        probs = low(expo / lax.optimization_barrier(jnp.sum(expo, -1, keepdims=True)))
        return jnp.einsum('hqk,khd->qhd', probs, head_v, precision=highest, preferred_element_type=jnp.float32)
    out = lax.map(one_block, (head_q, docs.reshape(blocks, QBLK), spots.reshape(blocks, QBLK)))
    return out.reshape(count, D)

def sentence(rows, docs, position, weights):
    first_gain, first_shift, second_gain, second_shift, project_weight, project_bias, output_weight, output_bias, up_weight, up_bias, down_weight, down_bias = weights
    cosine, sine = angles(position)
    normed = low(layer_norm(rows, first_gain, first_shift))
    mixed = low_back(product(normed, project_weight) + project_bias)
    queries = low(turn(mixed[:, :D], cosine, sine))
    keys = low(turn(mixed[:, D:2 * D], cosine, sine))
    values = low(mixed[:, 2 * D:])
    context = low_back(low(attend(queries, keys, values, docs)))
    attended = product(context, output_weight) + output_bias
    second = low(layer_norm(rows, second_gain, second_shift))
    hidden = low_back(product(second, up_weight) + up_bias)
    active = low(jax.nn.gelu(hidden, approximate=False))
    return rows + attended + (product(active, down_weight) + down_bias)

def reference(tokens, cotangent, loss_mask, bucket_perm, short_lengths, row_owner, row_slot, first_gain, first_shift, second_gain, second_shift, project_weight, project_bias, output_weight, output_bias, up_weight, up_bias, down_weight, down_bias):
    long_count = N_DP // 4
    flat = (row_owner * LONG + row_slot).astype(jnp.int32)
    source = jnp.full((N_DP * LONG,), TOKENS, jnp.int32).at[flat].set(jnp.arange(TOKENS, dtype=jnp.int32)).reshape(N_DP, LONG)
    long_rows = source[bucket_perm[:long_count]]
    short_rows = source[bucket_perm[long_count:], :SHORT_TOK]
    ends = jnp.cumsum(short_lengths, -1).astype(jnp.int32)
    spots = jnp.arange(SHORT_TOK, dtype=jnp.int32)
    short_docs = lax.optimization_barrier(jnp.sum((spots[None, :, None] >= ends[:, None, :]).astype(jnp.int32), -1))
    starts = (ends - short_lengths).astype(jnp.int32)
    short_pos = spots[None, :] - jnp.take_along_axis(starts, short_docs, 1)
    long_docs = jnp.zeros((LONG,), jnp.int32)
    long_pos = jnp.arange(LONG, dtype=jnp.int32)
    step = jax.checkpoint(sentence)

    def forward(inputs, weights):
        rounded = tuple((low(w) for w in weights))

        def long_step(carry, picks):
            return (carry, step(inputs[picks], long_docs, long_pos, rounded))

        def short_step(carry, parts):
            picks, docs, position = parts
            return (carry, step(inputs[picks], docs, position, rounded))
        zero = jnp.zeros((), jnp.float32)
        unused, long_out = lax.scan(long_step, zero, long_rows)
        unused, short_out = lax.scan(short_step, zero, (short_rows, short_docs, short_pos))
        out = jnp.zeros((TOKENS, D), jnp.float32)
        out = out.at[long_rows.reshape(-1)].set(long_out.reshape(-1, D))
        return out.at[short_rows.reshape(-1)].set(short_out.reshape(-1, D))
    inputs = tokens.astype(jnp.float32)
    weights = (first_gain.astype(jnp.float32), first_shift.astype(jnp.float32), second_gain.astype(jnp.float32), second_shift.astype(jnp.float32), project_weight.astype(jnp.float32), project_bias.astype(jnp.float32), output_weight.astype(jnp.float32), output_bias.astype(jnp.float32), up_weight.astype(jnp.float32), up_bias.astype(jnp.float32), down_weight.astype(jnp.float32), down_bias.astype(jnp.float32))
    out, pull = jax.vjp(forward, inputs, weights)
    tangent = cotangent.astype(jnp.float32) * loss_mask.astype(jnp.float32)[:, None]
    scale = lax.rsqrt(jnp.sum(loss_mask.astype(jnp.float32)))
    input_grad, grads = pull(tangent)
    return (out.astype(jnp.bfloat16), input_grad.astype(jnp.bfloat16), grads[0] * scale, grads[1] * scale, grads[2] * scale, grads[3] * scale, grads[4] * scale, grads[5] * scale, grads[6] * scale, grads[7] * scale, grads[8] * scale, grads[9] * scale, grads[10] * scale, grads[11] * scale)
```

```python
import functools
import math

import jax
import jax.numpy as jnp
from jax import lax
from jax.experimental import pallas as pl
from jax.experimental.pallas import tpu as pltpu
from jax.sharding import PartitionSpec as P

D = 768
HEADS = 12
HEAD_DIM = 64
ROT = 16
FF = 3072
LONG = 2048
SHORT_TOK = 1024
TOTAL = 3 * SHORT_TOK
BLK = 256
NH = HEADS // 2
HW = NH * HEAD_DIM
PART = SHORT_TOK // 2
MIB = 2**20

epsilon = 1e-05
bfloat = jnp.bfloat16
single = jnp.float32


def dot(left, right):
    return jnp.dot(left, right, preferred_element_type=single)


def over_rows(left, right):
    return lax.dot_general(left, right, (((0,), (0,)), ((), ())), preferred_element_type=single)


def against(left, right):
    return lax.dot_general(left, right, (((1,), (1,)), ((), ())), preferred_element_type=single)


def norm_stats(values):
    mean = jnp.mean(values, -1, keepdims=True)
    centred = values - mean
    spread = jnp.mean(centred * centred, -1, keepdims=True)
    factor = lax.rsqrt(spread + epsilon)
    return (centred * factor, factor)


def norm_back(upper, scaled, factor, gain):
    gain_grad = jnp.sum(upper * scaled, 0)
    shift_grad = jnp.sum(upper, 0)
    inner = upper * gain
    lower = factor * (
        inner
        - jnp.mean(inner, -1, keepdims=True)
        - scaled * jnp.mean(inner * scaled, -1, keepdims=True)
    )
    return (lower, gain_grad, shift_grad)


def params(mib):
    return pltpu.CompilerParams(vmem_limit_bytes=mib * MIB)


def whole(shape):
    return pl.BlockSpec(shape, lambda *_: (0,) * len(shape))


def feed_kernel(
    tok, tan, gain, shift, up, up_add, down, feed, lower, g_up, g_up_add, g_down, normed, act, slope
):
    step = pl.program_id(0)
    rows = tok.shape[0]
    chunk = rows // 2
    root = 1.0 / math.sqrt(2.0)
    dens = 1.0 / math.sqrt(2.0 * math.pi)

    @pl.when(step == 0)
    def _():
        def one(i, carry):
            r = pl.ds(pl.multiple_of(i * BLK, BLK), BLK)
            scaled, _ = norm_stats(tok[r, :].astype(single))
            normed[r, :] = (scaled * gain[...] + shift[...]).astype(bfloat)
            return carry

        lax.fori_loop(0, rows // BLK, one, 0)

    bias_sum = jnp.zeros(g_up_add.shape, single)
    for i in range(2):
        r = pl.ds(i * chunk, chunk)
        hidden = dot(normed[r, :], up[...]) + up_add[...]
        above = against(tan[r, :], down[...])
        phi = 0.5 * (1.0 + lax.erf(hidden * root))
        active = (hidden * phi).astype(bfloat)
        sl = (above * (phi + hidden * (dens * jnp.exp(-0.5 * hidden * hidden)))).astype(bfloat)
        act[r, :] = active
        slope[r, :] = sl
        bias_sum = bias_sum + jnp.sum(sl.astype(single), 0, keepdims=True)
        part_feed = dot(active, down[...])
        part_lower = against(sl, up[...])

        @pl.when(step == 0)
        def _():
            feed[r, :] = part_feed
            lower[r, :] = part_lower

        @pl.when(step > 0)
        def _():
            feed[r, :] += part_feed
            lower[r, :] += part_lower

    g_up_add[...] = bias_sum
    g_up[...] = over_rows(normed[...], slope[...])
    g_down[...] = over_rows(act[...], tan[...])


def feed_forward(tok, tan, gain, shift, up, up_add, down):
    rows = tok.shape[0]
    width = 768
    cols = pl.BlockSpec((D, width), lambda j: (0, j))
    line = pl.BlockSpec((1, width), lambda j: (0, j))
    tall = pl.BlockSpec((width, D), lambda j: (j, 0))
    return pl.pallas_call(
        feed_kernel,
        grid=(FF // width,),
        in_specs=[whole((rows, D)), whole((rows, D)), whole((1, D)), whole((1, D)), cols, line, tall],
        out_specs=[whole((rows, D)), whole((rows, D)), cols, line, tall],
        out_shape=[
            jax.ShapeDtypeStruct((rows, D), single),
            jax.ShapeDtypeStruct((rows, D), single),
            jax.ShapeDtypeStruct((D, FF), single),
            jax.ShapeDtypeStruct((1, FF), single),
            jax.ShapeDtypeStruct((FF, D), single),
        ],
        scratch_shapes=[
            pltpu.VMEM((rows, D), bfloat),
            pltpu.VMEM((rows, width), bfloat),
            pltpu.VMEM((rows, width), bfloat),
        ],
        compiler_params=params(56),
        cost_estimate=pl.CostEstimate(
            flops=12 * rows * D * FF, bytes_accessed=50 * MIB, transcendentals=2 * rows * FF
        ),
        name="feed_forward",
    )(tok, tan, gain, shift, up, up_add, down)


def pick_rows(places, own, other, low, span, first):
    spot = lax.broadcasted_iota(jnp.int32, (BLK, PART), 0) + first

    def part(k):
        mine = jnp.where(places[k] == spot, 1.0, 0.0).astype(bfloat)
        theirs = jnp.where(places[k + 3] == spot, 1.0, 0.0).astype(bfloat)
        return dot(mine, own[k]) + dot(theirs, other[k])

    return part


def turn_lanes(values, cosine, sine):
    lane = lax.broadcasted_iota(jnp.int32, values.shape, 1)
    swapped = jnp.where(
        lax.rem(lane, ROT) < ROT // 2, pltpu.roll(values, 128 - ROT // 2, 1), pltpu.roll(values, ROT // 2, 1)
    )
    return values * cosine + swapped * sine


def front_kernel(
    meta, places, own, other, gain, shift, weight, add, cosine, sine, normed, q, k, kt, v, vt, rows
):
    i = pl.program_id(0)
    active = meta[2, i]

    @pl.when(active > 0)
    def _():
        part = pick_rows(places, own, other, None, None, i * BLK)
        low = meta[3, i]
        rows[...] = part(low)

        @pl.when(meta[4, i] > 1)
        def _():
            rows[...] += part(low + 1)

        scaled, _ = norm_stats(rows[...])
        n = (scaled * gain[...] + shift[...]).astype(bfloat)
        normed[...] = n
        for s in range(3):
            c = slice(s * HW, (s + 1) * HW)
            mixed = dot(n, weight[:, c]) + add[:, c]
            if s < 2:
                mixed = jnp.concatenate(
                    [
                        turn_lanes(mixed[:, p : p + 128], cosine[...], sine[...])
                        for p in range(0, HW, 128)
                    ],
                    1,
                )
            low_mixed = mixed.astype(bfloat)
            if s == 0:
                q[...] = low_mixed * HEAD_DIM ** (-0.5)
            elif s == 1:
                k[...] = low_mixed
                kt[...] = low_mixed.T
            else:
                v[...] = low_mixed
                vt[...] = low_mixed.T

    @pl.when(active == 0)
    def _():
        for ref in (normed, q, k, kt, v, vt):
            ref[...] = jnp.zeros_like(ref)


def front(meta, places, own, other, gain, shift, weight, add, cosine, sine):
    tall = lambda width: pl.BlockSpec((BLK, width), lambda i, m: (i, 0))
    flat = pl.BlockSpec((HW, BLK), lambda i, m: (0, i))
    out = lambda *shape: jax.ShapeDtypeStruct(shape, bfloat)
    return pl.pallas_call(
        front_kernel,
        grid_spec=pltpu.PrefetchScalarGridSpec(
            num_scalar_prefetch=1,
            grid=(TOTAL // BLK,),
            in_specs=[
                whole((6, 1, PART)),
                whole((3, PART, D)),
                whole((3, PART, D)),
                whole((1, D)),
                whole((1, D)),
                whole((D, 3 * HW)),
                whole((1, 3 * HW)),
                tall(128),
                tall(128),
            ],
            out_specs=[tall(D), tall(HW), tall(HW), flat, tall(HW), flat],
            scratch_shapes=[pltpu.VMEM((BLK, D), single)],
        ),
        out_shape=[
            out(TOTAL, D),
            out(TOTAL, HW),
            out(TOTAL, HW),
            out(HW, TOTAL),
            out(TOTAL, HW),
            out(HW, TOTAL),
        ],
        compiler_params=params(40),
        cost_estimate=pl.CostEstimate(
            flops=2 * TOTAL * D * (3 * HW + 1024), bytes_accessed=24 * MIB, transcendentals=0
        ),
        name="front",
    )(meta, places, own, other, gain, shift, weight, add, cosine, sine)


def settle_kernel(meta, places, own, other, out, rows):
    i = pl.program_id(0)

    @pl.when(meta[2, i] > 0)
    def _():
        part = pick_rows(places, own, other, None, None, i * BLK)
        low = meta[3, i]
        rows[...] = part(low)

        @pl.when(meta[4, i] > 1)
        def _():
            rows[...] += part(low + 1)

        out[...] = rows[...].astype(bfloat)

    @pl.when(meta[2, i] == 0)
    def _():
        out[...] = jnp.zeros_like(out)


def settle(meta, places, own, other):
    width = own.shape[-1]
    return pl.pallas_call(
        settle_kernel,
        grid_spec=pltpu.PrefetchScalarGridSpec(
            num_scalar_prefetch=1,
            grid=(TOTAL // BLK,),
            in_specs=[whole((6, 1, PART)), whole((3, PART, width)), whole((3, PART, width))],
            out_specs=pl.BlockSpec((BLK, width), lambda i, m: (i, 0)),
            scratch_shapes=[pltpu.VMEM((BLK, width), single)],
        ),
        out_shape=jax.ShapeDtypeStruct((TOTAL, width), bfloat),
        compiler_params=params(32),
        name="settle",
    )(meta, places, own, other)


def unsettle_kernel(meta, spots, values, out, acc):
    b = pl.program_id(0)
    low, high = meta[5, b], meta[6, b]
    acc[...] = jnp.zeros_like(acc)
    lane = lax.broadcasted_iota(jnp.int32, (PART, PART), 1)

    def one(c, carry):
        hot = jnp.where(spots[:, 0:1] == lane + c * PART, 1.0, 0.0).astype(bfloat)
        r = pl.ds(pl.multiple_of(c * PART, PART), PART)
        acc[...] += dot(hot, values[r, :].astype(bfloat))
        return carry

    lax.fori_loop(low, high, one, 0)
    out[0] = acc[...].astype(bfloat)


def unsettle(meta, spots, values):
    width = values.shape[-1]
    return pl.pallas_call(
        unsettle_kernel,
        grid_spec=pltpu.PrefetchScalarGridSpec(
            num_scalar_prefetch=1,
            grid=(6,),
            in_specs=[
                pl.BlockSpec((PART, 128), lambda b, m: (b, 0)),
                whole((TOTAL, width)),
            ],
            out_specs=pl.BlockSpec((1, PART, width), lambda b, m: (b, 0, 0)),
            scratch_shapes=[pltpu.VMEM((PART, width), single)],
        ),
        out_shape=jax.ShapeDtypeStruct((6, PART, width), bfloat),
        compiler_params=params(40),
        name="unsettle",
    )(meta, spots, values)


def of_head(values, h):
    lane = lax.broadcasted_iota(jnp.int32, values.shape, 1)
    return jnp.where((lane < HEAD_DIM) == (h % 2 == 0), values, jnp.zeros_like(values))


def lanes_of(h):
    return slice((h // 2) * 128, (h // 2) * 128 + 128)


def rows_of(h):
    return slice(h * HEAD_DIM, (h + 1) * HEAD_DIM)


def allowed_of(start, j, diagonal):
    row = lax.broadcasted_iota(jnp.int32, (BLK, BLK), 0)
    allowed = row + j * BLK >= start[...]
    if diagonal:
        allowed &= row <= lax.broadcasted_iota(jnp.int32, (BLK, BLK), 1)
    return allowed


def over_blocks(meta, i, step):
    def masked(j, carry):
        step(j, True, False)
        return carry

    def plain(j, carry):
        step(j, False, False)
        return carry

    lax.fori_loop(meta[0, i], meta[1, i], masked, 0)
    lax.fori_loop(meta[1, i], i, plain, 0)
    step(i, True, True)


def attend_kernel(meta, q, k, vt, start, context, logsum, score, peak, total, acc):
    i = pl.program_id(0)

    @pl.when(meta[2, i] > 0)
    def _():
        first = meta[0, i]
        queries = [of_head(q[:, lanes_of(h)], h) for h in range(NH)]
        peak[...] = jnp.full(peak.shape, -jnp.inf, single)

        def step(j, masked, diagonal):
            r = pl.ds(pl.multiple_of(j * BLK, BLK), BLK)
            o = pl.ds(pl.multiple_of((j - first) * BLK, BLK), BLK)
            if masked:
                allowed = allowed_of(start, j, diagonal)
            for h in range(NH):
                s = against(k[r, lanes_of(h)], queries[h])
                if masked:
                    s = jnp.where(allowed, s, -jnp.inf)
                score[h, o, :] = s
                peak[h] = jnp.maximum(peak[h], jnp.max(s.reshape(BLK // 8, 8, BLK), 0))

        over_blocks(meta, i, step)
        tops = [jnp.max(peak[h], 0, keepdims=True) for h in range(NH)]
        total[...] = jnp.zeros_like(total)
        acc[...] = jnp.zeros_like(acc)

        def add(j, carry):
            r = pl.ds(pl.multiple_of(j * BLK, BLK), BLK)
            o = pl.ds(pl.multiple_of((j - first) * BLK, BLK), BLK)
            for h in range(NH):
                p = jnp.exp(score[h, o, :] - tops[h])
                total[h] += jnp.sum(p.reshape(BLK // 8, 8, BLK), 0)
                acc[rows_of(h), :] += dot(vt[rows_of(h), r], p.astype(bfloat))
            return carry

        lax.fori_loop(first, i + 1, add, 0)
        for h in range(NH):
            whole_sum = jnp.sum(total[h], 0, keepdims=True)
            acc[rows_of(h), :] = acc[rows_of(h), :] / whole_sum
            logsum[h : h + 1, :] = tops[h] + jnp.log(whole_sum)
        context[...] = acc[...].T

    @pl.when(meta[2, i] == 0)
    def _():
        context[...] = jnp.zeros_like(context)
        logsum[...] = jnp.zeros_like(logsum)


def attend(meta, q, k, vt, start):
    block = pl.BlockSpec((BLK, HW), lambda i, m: (i, 0))
    line = lambda rows: pl.BlockSpec((rows, BLK), lambda i, m: (0, i))
    return pl.pallas_call(
        attend_kernel,
        grid_spec=pltpu.PrefetchScalarGridSpec(
            num_scalar_prefetch=1,
            grid=(TOTAL // BLK,),
            in_specs=[block, whole((TOTAL, HW)), whole((HW, TOTAL)), line(1)],
            out_specs=[block, line(8)],
            scratch_shapes=[
                pltpu.VMEM((NH, LONG, BLK), single),
                pltpu.VMEM((NH, 8, BLK), single),
                pltpu.VMEM((NH, 8, BLK), single),
                pltpu.VMEM((HW, BLK), single),
            ],
        ),
        out_shape=[
            jax.ShapeDtypeStruct((TOTAL, HW), single),
            jax.ShapeDtypeStruct((8, TOTAL), single),
        ],
        compiler_params=params(40),
        cost_estimate=pl.CostEstimate(
            flops=NH * LONG * LONG * 512, bytes_accessed=12 * MIB, transcendentals=NH * LONG * LONG // 2
        ),
        name="attend",
    )(meta, q, k, vt, start)


def attend_back_kernel(meta, q, k, kt, v, start, upper, context, logsum, dq, dk, dv, dqt, probs, slopes):
    i = pl.program_id(0)

    @pl.when(i == 0)
    def _():
        dk[...] = jnp.zeros_like(dk)
        dv[...] = jnp.zeros_like(dv)

    @pl.when(meta[2, i] > 0)
    def _():
        queries = [of_head(q[:, lanes_of(h)], h) for h in range(NH)]
        uppers = [of_head(upper[:, lanes_of(h)], h) for h in range(NH)]
        both = (upper[...].astype(single) * context[...]).T
        delta = [jnp.sum(both[rows_of(h), :], 0, keepdims=True) for h in range(NH)]
        dqt[...] = jnp.zeros_like(dqt)

        def step(j, masked, diagonal):
            r = pl.ds(pl.multiple_of(j * BLK, BLK), BLK)
            if masked:
                allowed = allowed_of(start, j, diagonal)
            for h in range(NH):
                s = against(k[r, lanes_of(h)], queries[h])
                p = jnp.exp(s - logsum[h : h + 1, :])
                if masked:
                    p = jnp.where(allowed, p, 0.0)
                dp = against(v[r, lanes_of(h)], uppers[h])
                c = slice((h % 2) * BLK, (h % 2) * BLK + BLK)
                probs[h // 2, :, c] = p.astype(bfloat)
                slopes[h // 2, :, c] = (p * (dp - delta[h])).astype(bfloat)
            for g in range(NH // 2):
                c = slice(g * 128, g * 128 + 128)
                dv[r, c] += dot(probs[g], jnp.concatenate(uppers[2 * g : 2 * g + 2], 0))
                dk[r, c] += dot(slopes[g], jnp.concatenate(queries[2 * g : 2 * g + 2], 0))
                for h in (2 * g, 2 * g + 1):
                    e = slice((h % 2) * BLK, (h % 2) * BLK + BLK)
                    dqt[rows_of(h), :] += dot(kt[rows_of(h), r], slopes[g, :, e])

        over_blocks(meta, i, step)
        dq[...] = dqt[...].T * HEAD_DIM ** (-0.5)

    @pl.when(meta[2, i] == 0)
    def _():
        dq[...] = jnp.zeros_like(dq)


def attend_back(meta, q, k, kt, v, start, upper, context, logsum):
    block = pl.BlockSpec((BLK, HW), lambda i, m: (i, 0))
    line = lambda rows: pl.BlockSpec((rows, BLK), lambda i, m: (0, i))
    full = whole((TOTAL, HW))
    return pl.pallas_call(
        attend_back_kernel,
        grid_spec=pltpu.PrefetchScalarGridSpec(
            num_scalar_prefetch=1,
            grid=(TOTAL // BLK,),
            in_specs=[block, full, whole((HW, TOTAL)), full, line(1), block, block, line(8)],
            out_specs=[block, full, full],
            scratch_shapes=[
                pltpu.VMEM((HW, BLK), single),
                pltpu.VMEM((NH // 2, BLK, 2 * BLK), bfloat),
                pltpu.VMEM((NH // 2, BLK, 2 * BLK), bfloat),
            ],
        ),
        out_shape=[jax.ShapeDtypeStruct((TOTAL, HW), single)] * 3,
        compiler_params=params(48),
        cost_estimate=pl.CostEstimate(
            flops=5 * NH * LONG * LONG * 256, bytes_accessed=24 * MIB, transcendentals=NH * LONG * LONG // 2
        ),
        name="attend_back",
    )(meta, q, k, kt, v, start, upper, context, logsum)


def back_kernel(meta, dq, dk, dv, normed, weight, cosine, sine, lower, g_weight, g_add):
    i = pl.program_id(0)

    @pl.when(i == 0)
    def _():
        g_weight[...] = jnp.zeros_like(g_weight)
        g_add[...] = jnp.zeros_like(g_add)

    @pl.when(meta[2, i] > 0)
    def _():
        turned = []
        for ref in (dq, dk):
            for p in range(0, HW, 128):
                turned.append(turn_lanes(ref[:, p : p + 128], cosine[...], -sine[...]))
        turned.append(dv[...])
        mixed = jnp.concatenate(turned, 1).astype(bfloat)
        g_add[...] += jnp.sum(mixed.astype(single), 0, keepdims=True)
        lower[...] = against(mixed, weight[...]).astype(bfloat)
        g_weight[...] += over_rows(normed[...], mixed)

    @pl.when(meta[2, i] == 0)
    def _():
        lower[...] = jnp.zeros_like(lower)


def back(meta, dq, dk, dv, normed, weight, cosine, sine):
    tall = lambda width: pl.BlockSpec((BLK, width), lambda i, m: (i, 0))
    return pl.pallas_call(
        back_kernel,
        grid_spec=pltpu.PrefetchScalarGridSpec(
            num_scalar_prefetch=1,
            grid=(TOTAL // BLK,),
            in_specs=[
                tall(HW),
                tall(HW),
                tall(HW),
                tall(D),
                whole((D, 3 * HW)),
                tall(128),
                tall(128),
            ],
            out_specs=[tall(D), whole((D, 3 * HW)), whole((1, 3 * HW))],
        ),
        out_shape=[
            jax.ShapeDtypeStruct((TOTAL, D), bfloat),
            jax.ShapeDtypeStruct((D, 3 * HW), single),
            jax.ShapeDtypeStruct((1, 3 * HW), single),
        ],
        compiler_params=params(40),
        cost_estimate=pl.CostEstimate(
            flops=4 * TOTAL * D * 3 * HW, bytes_accessed=32 * MIB, transcendentals=0
        ),
        name="back",
    )(meta, dq, dk, dv, normed, weight, cosine, sine)


def gather_all(x):
    return lax.all_gather(x, "dp", axis=0, tiled=True)


def scatter_sum(x):
    return lax.psum_scatter(x, "dp", scatter_dimension=0, tiled=True)


def body(
    tokens,
    cotangent,
    loss_mask,
    bucket_perm,
    short_lengths,
    row_owner,
    row_slot,
    first_gain,
    first_shift,
    second_gain,
    second_shift,
    project_weight,
    project_bias,
    output_weight,
    output_bias,
    up_weight,
    up_bias,
    down_weight,
    down_bias,
):
    devices = lax.axis_size("dp")
    me = lax.axis_index("dp")
    core = me % 2
    chip = me // 2
    rows = tokens.shape[0]
    share = LONG // devices // 4
    room = 3 * share
    long_count = devices // 4
    swap = [(i, i ^ 1) for i in range(devices)]

    def exchange(x):
        return lax.ppermute(x, "dp", swap)

    small = jnp.concatenate(
        [
            first_gain,
            first_shift,
            second_gain,
            second_shift,
            output_bias,
            down_bias,
            project_bias,
            up_bias,
        ]
    ).astype(bfloat)
    small_all = gather_all(small[None])
    project_full = gather_all(project_weight.astype(bfloat))
    output_full = gather_all(output_weight.astype(bfloat))
    up_full = gather_all(up_weight.astype(bfloat))
    down_full = gather_all(down_weight.astype(bfloat))
    piece = D // devices

    def vector(first, width):
        return small_all[:, first : first + width].astype(single).reshape(1, devices * width)

    gain_one, shift_one, gain_two, shift_two, output_add, down_add = (
        vector(i * piece, piece) for i in range(6)
    )
    project_add = vector(6 * piece, 3 * piece)
    up_add = vector(9 * piece, 4 * piece)
    project_half = lax.dynamic_index_in_dim(
        project_full.reshape(D, 3, 2, HW), core, 2, keepdims=False
    ).reshape(D, 3 * HW)
    project_add_half = lax.dynamic_index_in_dim(
        project_add.reshape(1, 3, 2, HW), core, 2, keepdims=False
    ).reshape(1, 3 * HW)

    spread = jnp.arange(devices, dtype=jnp.int32)
    bucket = jnp.sum(jnp.where(bucket_perm[None, :] == row_owner[:, None], spread[None, :], 0), -1)
    hot = (row_owner[:, None] == spread[None, :]).astype(bfloat)
    line = jnp.arange(rows, dtype=jnp.int32)
    before = (line[None, :] < line[:, None]).astype(bfloat)
    rank = jnp.sum(dot(before, hot) * hot.astype(single), -1).astype(jnp.int32)
    is_long = bucket < long_count
    short = bucket - long_count
    part = jnp.where(is_long, 0, short % 3)
    to_chip = jnp.where(is_long, 2 * bucket, 2 * (short // 3) + 1)
    held = jnp.where(is_long, 2 * share, share)
    to_core = rank // held
    place = (2 * to_chip + to_core) * room + part * share + rank % held
    slot = part * SHORT_TOK + row_slot
    spots = jnp.arange(devices * room, dtype=jnp.int32)
    slot_at = jnp.sum(
        jnp.where(place[None, :] == spots[:, None], slot[None, :] + 1, 0), -1
    ) - 1
    slot_send = slot_at.reshape(devices // 2, 1, 2 * room)
    slot_send = jnp.broadcast_to(slot_send, (devices // 2, 2, 2 * room)).reshape(devices, 2 * room)
    sender = (place[None, :] == spots[:, None]).astype(bfloat)
    keeper = (place[:, None] == spots[None, :]).astype(bfloat)

    def swap_all(x):
        return lax.all_to_all(x, "dp", split_axis=0, concat_axis=0, tiled=True)

    def dispatch(x):
        moved = swap_all(dot(sender, x).astype(bfloat).reshape(devices, room, D))
        return moved.reshape(devices, 3, share, D).transpose(1, 0, 2, 3).reshape(3, PART, D)

    def give_back(x):
        moved = x.reshape(3, devices, share, D).transpose(1, 0, 2, 3).reshape(devices, room, D)
        return dot(keeper, swap_all(moved).reshape(devices * room, D))

    slot_recv = swap_all(slot_send).reshape(devices, 2, 3, share).transpose(1, 2, 0, 3)
    slot_recv = slot_recv.reshape(2, 3, PART)
    slot_recv = jnp.where(core == 0, slot_recv, slot_recv[::-1])
    places = slot_recv.reshape(6, 1, PART)
    places_wide = jnp.broadcast_to(slot_recv.reshape(6 * PART, 1), (6 * PART, 128))

    self_long = chip % 2 == 0
    lengths = lax.dynamic_slice_in_dim(short_lengths, 3 * (chip // 2), 3, 0)
    ends = jnp.cumsum(lengths, -1)
    at = jnp.arange(TOTAL, dtype=jnp.int32).reshape(3, SHORT_TOK)
    inside = jnp.arange(SHORT_TOK, dtype=jnp.int32)
    begun = jnp.max(
        jnp.where(ends[:, None, :] <= inside[None, :, None], ends[:, None, :], 0), -1
    )
    start = jnp.where(self_long, 0, begun + at - inside[None, :]).reshape(TOTAL)
    position = jnp.arange(TOTAL, dtype=jnp.int32) - start
    blocks = jnp.arange(TOTAL // BLK, dtype=jnp.int32)
    low_start = start[::BLK] // BLK
    high_start = (start[BLK - 1 :: BLK] + BLK - 1) // BLK
    zero = jnp.zeros_like(blocks)
    meta = jnp.stack(
        [
            low_start,
            jnp.minimum(blocks, jnp.maximum(low_start, high_start)),
            jnp.where(self_long & (blocks >= LONG // BLK), 0, 1),
            jnp.where(self_long, 0, blocks // (SHORT_TOK // BLK)),
            jnp.where(self_long, 2, 1) + zero,
            jnp.where(self_long, 0, 2 * (blocks % 3)),
            jnp.where(self_long, jnp.where(blocks % 3 == 2, 0, 4), 2 * (blocks % 3) + 2),
        ]
    ).astype(jnp.int32)
    freq = 10000.0 ** (-2.0 * jnp.arange(ROT // 2).astype(single) / ROT)
    phase = position.astype(single)[:, None] * freq[None, :]
    cos8, sin8 = jnp.cos(phase), jnp.sin(phase)
    rest = HEAD_DIM - ROT
    cosine = jnp.tile(
        jnp.concatenate([cos8, cos8, jnp.ones((TOTAL, rest), single)], 1), (1, 2)
    )
    sine = jnp.tile(jnp.concatenate([-sin8, sin8, jnp.zeros((TOTAL, rest), single)], 1), (1, 2))
    starts = start.reshape(1, TOTAL)

    def half(x, which):
        return lax.dynamic_slice_in_dim(x, which * HW, HW, x.ndim - 1)

    tangent = cotangent * loss_mask.astype(bfloat)[:, None]
    own = dispatch(tokens)
    other = exchange(own)
    upper_rows = dispatch(against(tangent, output_full).astype(bfloat))
    upper_other = exchange(half(upper_rows, 1 - core))
    normed_one, q, k, kt, v, vt = front(
        meta, places, own, other, gain_one, shift_one, project_half, project_add_half, cosine, sine
    )
    context, logsum = attend(meta, q, k, vt, starts)
    context_rows = unsettle(meta, places_wide, context)
    mine, theirs = context_rows[:3], exchange(context_rows[3:])
    context_back = give_back(
        jnp.concatenate(
            [jnp.where(core == 0, mine, theirs), jnp.where(core == 0, theirs, mine)], -1
        )
    ).astype(bfloat)

    feed, lower_two_up, up_grad, up_add_grad, down_grad = feed_forward(
        tokens, tangent, gain_two, shift_two, up_full, up_add, down_full
    )

    upper = settle(meta, places, half(upper_rows, core), upper_other)
    dq, dk, dv = attend_back(meta, q, k, kt, v, starts, upper, context, logsum)
    lower_rows, project_grad_half, project_add_half_grad = back(
        meta, dq, dk, dv, normed_one, project_half, cosine, sine
    )
    lower_moved = unsettle(meta, places_wide, lower_rows)
    lower_sum = lower_moved[:3].astype(single) + exchange(lower_moved[3:]).astype(single)
    upper_one = give_back(lower_sum.astype(bfloat))

    rows_in = tokens.astype(single)
    scaled, factor = norm_stats(rows_in)
    block_out = (
        rows_in + (dot(context_back, output_full) + output_add) + (feed + down_add)
    ).astype(bfloat)
    lower_one, gain_one_grad, shift_one_grad = norm_back(upper_one, scaled, factor, gain_one)
    lower_two, gain_two_grad, shift_two_grad = norm_back(lower_two_up, scaled, factor, gain_two)
    tokens_grad = (tangent.astype(single) + lower_one + lower_two).astype(bfloat)
    output_grad = over_rows(context_back, tangent)
    bias_grad = jnp.sum(tangent.astype(single), 0)

    def spread_half(x):
        lead = x.shape[0]
        x = x.reshape(lead, 3, 1, HW)
        empty = jnp.zeros_like(x)
        pair = jnp.where(
            core == 0, jnp.concatenate([x, empty], 2), jnp.concatenate([empty, x], 2)
        )
        return pair.reshape(lead, 3 * D)

    scale = lax.rsqrt(lax.psum(jnp.sum(loss_mask.astype(single)), "dp"))
    vectors = jnp.concatenate(
        [
            x.reshape(devices, -1)
            for x in (
                gain_one_grad,
                shift_one_grad,
                gain_two_grad,
                shift_two_grad,
                bias_grad,
                spread_half(project_add_half_grad),
                up_add_grad,
            )
        ],
        1,
    )
    vector_sum = scatter_sum(vectors)[0] * scale
    gains = [vector_sum[i * piece : (i + 1) * piece] for i in range(5)]
    return (
        block_out,
        tokens_grad,
        gains[0],
        gains[1],
        gains[2],
        gains[3],
        scatter_sum(spread_half(project_grad_half)) * scale,
        vector_sum[5 * piece : 8 * piece],
        scatter_sum(output_grad) * scale,
        gains[4],
        scatter_sum(up_grad) * scale,
        vector_sum[8 * piece : 12 * piece],
        scatter_sum(down_grad) * scale,
        gains[4],
    )


def solution(mesh):
    tall, flat = P("dp", None), P("dp")
    return jax.shard_map(
        body,
        mesh=mesh,
        in_specs=(
            tall,
            tall,
            flat,
            P(),
            P(),
            flat,
            flat,
            flat,
            flat,
            flat,
            flat,
            tall,
            flat,
            tall,
            flat,
            tall,
            flat,
            tall,
            flat,
        ),
        out_specs=(
            tall,
            tall,
            flat,
            flat,
            flat,
            flat,
            tall,
            flat,
            tall,
            flat,
            tall,
            flat,
            tall,
            flat,
        ),
        check_vma=False,
    )
```

```python
import functools
import math

import jax
import jax.numpy as jnp
from jax import lax
from jax.experimental import pallas as pl
from jax.experimental.pallas import tpu as pltpu
from jax.sharding import PartitionSpec as P

D = 768
HEADS = 12
HEAD_DIM = 64
ROT = 16
FF = 3072
LONG = 2048
SHORT_TOK = 1024
TOTAL = 3 * SHORT_TOK
BLK = 256
BLOCKS = TOTAL // BLK
NH = HEADS // 2
HW = NH * HEAD_DIM
PART = SHORT_TOK // 2
MIB = 2**20

epsilon = 1e-05
bfloat = jnp.bfloat16
single = jnp.float32


def dot(left, right):
    return jnp.dot(left, right, preferred_element_type=single)


def over_rows(left, right):
    return lax.dot_general(left, right, (((0,), (0,)), ((), ())), preferred_element_type=single)


def against(left, right):
    return lax.dot_general(left, right, (((1,), (1,)), ((), ())), preferred_element_type=single)


def norm_stats(values):
    mean = jnp.mean(values, -1, keepdims=True)
    centred = values - mean
    spread = jnp.mean(centred * centred, -1, keepdims=True)
    factor = lax.rsqrt(spread + epsilon)
    return (centred * factor, factor)


def params(mib):
    return pltpu.CompilerParams(vmem_limit_bytes=mib * MIB)


def whole(shape):
    return pl.BlockSpec(shape, lambda *_: (0,) * len(shape))


def feed_kernel(
    tok, tan, lines, up, up_add, down, feed, lower, grad, g_up_add, normed, act, slope
):
    step = pl.program_id(0)
    rows = tok.shape[0]
    chunk = rows // 2
    root = 1.0 / math.sqrt(2.0)
    dens = 1.0 / math.sqrt(2.0 * math.pi)

    @pl.when(step == 0)
    def _():
        def one(i, carry):
            r = pl.ds(pl.multiple_of(i * BLK, BLK), BLK)
            scaled, _ = norm_stats(tok[r, :].astype(single))
            normed[r, :] = (scaled * lines[2:3, :] + lines[3:4, :]).astype(bfloat)
            return carry

        lax.fori_loop(0, rows // BLK, one, 0)

    bias_sum = jnp.zeros((1, D), single)
    for i in range(2):
        r = pl.ds(i * chunk, chunk)
        hidden = dot(normed[r, :], up[...]) + up_add[0]
        above = against(tan[r, :], down[...])
        phi = 0.5 * (1.0 + lax.erf(hidden * root))
        active = (hidden * phi).astype(bfloat)
        sl = (above * (phi + hidden * (dens * jnp.exp(-0.5 * hidden * hidden)))).astype(bfloat)
        act[r, :] = active
        slope[r, :] = sl
        bias_sum = bias_sum + jnp.sum(sl.astype(single), 0, keepdims=True)
        part_feed = dot(active, down[...])
        part_lower = against(sl, up[...])

        @pl.when(step == 0)
        def _():
            feed[r, :] = part_feed
            lower[r, :] = part_lower

        @pl.when(step > 0)
        def _():
            feed[r, :] += part_feed
            lower[r, :] += part_lower

    g_up_add[0] = bias_sum
    grad[:, :D] = over_rows(normed[...], slope[...]).astype(bfloat)
    grad[:, D:] = over_rows(act[...], tan[...]).astype(bfloat)


def feed_forward(tok, tan, lines, weights, up_add):
    rows, count = tok.shape[0], FF // D
    wide = lambda where: pl.BlockSpec((D, D), lambda j: (0, where + j))
    one = lambda shape: pl.BlockSpec(shape, lambda j: (0, 0), pipeline_mode=pl.Buffered(1))
    line = pl.BlockSpec((1, 1, D), lambda j: (j, 0, 0))
    pair = pl.BlockSpec((D, 2 * D), lambda j: (0, j))
    return pl.pallas_call(
        feed_kernel,
        grid=(count,),
        in_specs=[one((rows, D)), one((rows, D)), one((16, D)), wide(0), line, wide(count)],
        out_specs=[one((rows, D)), one((rows, D)), pair, line],
        out_shape=[
            jax.ShapeDtypeStruct((rows, D), single),
            jax.ShapeDtypeStruct((rows, D), single),
            jax.ShapeDtypeStruct((D, 2 * count * D), bfloat),
            jax.ShapeDtypeStruct((count, 1, D), single),
        ],
        scratch_shapes=[
            pltpu.VMEM((rows, D), bfloat),
            pltpu.VMEM((rows, D), bfloat),
            pltpu.VMEM((rows, D), bfloat),
        ],
        compiler_params=params(60),
        cost_estimate=pl.CostEstimate(
            flops=12 * rows * D * D * count, bytes_accessed=count * 12 * MIB, transcendentals=2 * rows * D * count
        ),
        name="feed_forward",
    )(tok, tan, lines, weights, up_add, weights)


def gather_rows(meta, i, places, own, other, rows):
    spot = lax.broadcasted_iota(jnp.int32, (BLK, PART), 0) + i * BLK

    def part(k):
        mine = jnp.where(places[k] == spot, 1.0, 0.0).astype(bfloat)
        theirs = jnp.where(places[k + 3] == spot, 1.0, 0.0).astype(bfloat)
        return dot(mine, own[k]) + dot(theirs, other[k])

    low = meta[3, i]
    rows[...] = part(low)

    @pl.when(meta[4, i] > 1)
    def _():
        rows[...] += part(low + 1)


def column(line):
    return jnp.broadcast_to(line, (128, line.shape[1])).T[:, 0:1]


def return_rows(meta, at, places, values, mine, theirs, acc):
    b = lax.rem(at + 3, 6)
    acc[...] = jnp.zeros_like(acc)
    lane = lax.broadcasted_iota(jnp.int32, (PART, PART), 1)
    spots = column(places[b])

    def one(c, carry):
        hot = jnp.where(spots == lane + c * PART, 1.0, 0.0).astype(bfloat)
        r = pl.ds(pl.multiple_of(c * PART, PART), PART)
        acc[...] += dot(hot, values[r, :])
        return carry

    lax.fori_loop(meta[5, b], meta[6, b], one, 0)

    @pl.when(at < 3)
    def _():
        theirs[0] = acc[...].astype(bfloat)

    @pl.when(at >= 3)
    def _():
        mine[0] = acc[...].astype(bfloat)


def turn_lanes(values, cosine, sine):
    lane = lax.broadcasted_iota(jnp.int32, values.shape, 1)
    swapped = jnp.where(
        lax.rem(lane, ROT) < ROT // 2, pltpu.roll(values, 128 - ROT // 2, 1), pltpu.roll(values, ROT // 2, 1)
    )
    return values * cosine + swapped * sine


def of_head(values, h):
    lane = lax.broadcasted_iota(jnp.int32, values.shape, 1)
    return jnp.where((lane < HEAD_DIM) == (h % 2 == 0), values, jnp.zeros_like(values))


def lanes_of(h):
    return slice((h // 2) * 128, (h // 2) * 128 + 128)


def rows_of(h):
    return slice(h * HEAD_DIM, (h + 1) * HEAD_DIM)


def block_of(j):
    return pl.ds(pl.multiple_of(j * BLK, BLK), BLK)


def allowed_of(start, j, diagonal):
    row = lax.broadcasted_iota(jnp.int32, (BLK, BLK), 0)
    allowed = row + j * BLK >= start[...]
    if diagonal:
        allowed &= row <= lax.broadcasted_iota(jnp.int32, (BLK, BLK), 1)
    return allowed


def over_blocks(meta, i, step):
    def masked(j, carry):
        step(j, True, False)
        return carry

    def plain(j, carry):
        step(j, False, False)
        return carry

    lax.fori_loop(meta[0, i], meta[1, i], masked, 0)
    lax.fori_loop(meta[1, i], i, plain, 0)
    step(i, True, True)


def forward_kernel(
    meta,
    places,
    own,
    other,
    lines,
    weight_q,
    weight_k,
    weight_v,
    add,
    cosine,
    sine,
    start,
    kept,
    q,
    k,
    kt,
    v,
    context,
    logsum,
    mine,
    theirs,
    rows,
    keys,
    values,
    score,
    peak,
    total,
    acc,
    done,
    back_acc,
):
    step_at = pl.program_id(0)
    i = jnp.minimum(step_at, BLOCKS - 1)
    here = block_of(i)
    live = (step_at < BLOCKS) & (meta[2, i] > 0)

    @pl.when(live)
    def _():
        gather_rows(meta, i, places, own, other, rows)
        scaled, _ = norm_stats(rows[...])
        n = (scaled * lines[0:1, :] + lines[1:2, :]).astype(bfloat)
        kept[...] = rows[...].astype(bfloat)
        for s, weight in enumerate((weight_q, weight_k, weight_v)):
            mixed = dot(n, weight[...]) + add[:, s * HW : (s + 1) * HW]
            if s < 2:
                mixed = jnp.concatenate(
                    [
                        turn_lanes(mixed[:, p : p + 128], cosine[...], sine[...])
                        for p in range(0, HW, 128)
                    ],
                    1,
                )
            narrow = mixed.astype(bfloat)
            if s == 0:
                q[...] = narrow * HEAD_DIM ** (-0.5)
            elif s == 1:
                k[...] = narrow
                keys[here, :] = narrow
                kt[...] = narrow.T
            else:
                v[...] = narrow
                values[:, here] = narrow.T

        first = meta[0, i]
        queries = [of_head(q[:, lanes_of(h)], h) for h in range(NH)]
        peak[...] = jnp.full(peak.shape, -jnp.inf, single)

        def step(j, masked, diagonal):
            if masked:
                allowed = allowed_of(start, j, diagonal)
            for h in range(NH):
                s = against(keys[block_of(j), lanes_of(h)], queries[h])
                if masked:
                    s = jnp.where(allowed, s, -jnp.inf)
                score[h, block_of(j - first), :] = s
                peak[h] = jnp.maximum(peak[h], jnp.max(s.reshape(BLK // 8, 8, BLK), 0))

        over_blocks(meta, i, step)
        tops = [jnp.max(peak[h], 0, keepdims=True) for h in range(NH)]
        total[...] = jnp.zeros_like(total)
        acc[...] = jnp.zeros_like(acc)

        def gain(j, carry):
            for h in range(NH):
                p = jnp.exp(score[h, block_of(j - first), :] - tops[h])
                total[h] += jnp.sum(p.reshape(BLK // 8, 8, BLK), 0)
                acc[rows_of(h), :] += dot(values[rows_of(h), block_of(j)], p.astype(bfloat))
            return carry

        lax.fori_loop(first, i + 1, gain, 0)
        for h in range(NH):
            whole_sum = jnp.sum(total[h], 0, keepdims=True)
            acc[rows_of(h), :] = acc[rows_of(h), :] / whole_sum
            logsum[h : h + 1, :] = tops[h] + jnp.log(whole_sum)
        turned = acc[...].T
        context[...] = turned
        done[here, :] = turned.astype(bfloat)

    @pl.when((step_at < BLOCKS) & (meta[2, i] == 0))
    def _():
        for ref in (kept, q, k, kt, v, context, logsum):
            ref[...] = jnp.zeros_like(ref)

    @pl.when(step_at >= BLOCKS)
    def _():
        return_rows(meta, jnp.maximum(step_at - BLOCKS, 0), places, done, mine, theirs, back_acc)


def columns():
    return [
        pl.BlockSpec((D, HW), lambda i, m, s=s: (0, 2 * s + m[7, 0]), pipeline_mode=pl.Buffered(1))
        for s in range(3)
    ]


def held(*shape):
    return pl.BlockSpec(shape, lambda i, m: (0,) * len(shape), pipeline_mode=pl.Buffered(1))


def tall_at(width, first):
    return pl.BlockSpec((BLK, width), lambda i, m: (jnp.clip(i - first, 0, BLOCKS - 1), 0))


def flat_at(height, first):
    return pl.BlockSpec((height, BLK), lambda i, m: (0, jnp.clip(i - first, 0, BLOCKS - 1)))


def parts_at(first, width):
    return [
        pl.BlockSpec((1, PART, width), lambda i, m, f=f: (jnp.clip(i - f, 0, 2), 0, 0))
        for f in (first + 3, first)
    ]


def forward(meta, places, own, other, lines, weight, add, cosine, sine, start):
    out = lambda *shape: jax.ShapeDtypeStruct(shape, bfloat)
    return pl.pallas_call(
        forward_kernel,
        grid_spec=pltpu.PrefetchScalarGridSpec(
            num_scalar_prefetch=1,
            grid=(BLOCKS + 6,),
            in_specs=[
                held(6, 1, PART),
                held(3, PART, D),
                held(3, PART, D),
                held(16, D),
                *columns(),
                held(1, 3 * HW),
                tall_at(128, 0),
                tall_at(128, 0),
                flat_at(1, 0),
            ],
            out_specs=[
                tall_at(D, 0),
                tall_at(HW, 0),
                tall_at(HW, 0),
                flat_at(HW, 0),
                tall_at(HW, 0),
                tall_at(HW, 0),
                flat_at(8, 0),
                *parts_at(BLOCKS, HW),
            ],
            scratch_shapes=[
                pltpu.VMEM((BLK, D), single),
                pltpu.VMEM((TOTAL, HW), bfloat),
                pltpu.VMEM((HW, TOTAL), bfloat),
                pltpu.VMEM((NH, LONG, BLK), single),
                pltpu.VMEM((NH, 8, BLK), single),
                pltpu.VMEM((NH, 8, BLK), single),
                pltpu.VMEM((HW, BLK), single),
                pltpu.VMEM((TOTAL, HW), bfloat),
                pltpu.VMEM((PART, HW), single),
            ],
        ),
        out_shape=[
            out(TOTAL, D),
            out(TOTAL, HW),
            out(TOTAL, HW),
            out(HW, TOTAL),
            out(TOTAL, HW),
            jax.ShapeDtypeStruct((TOTAL, HW), single),
            jax.ShapeDtypeStruct((8, TOTAL), single),
            out(3, PART, HW),
            out(3, PART, HW),
        ],
        compiler_params=params(60),
        cost_estimate=pl.CostEstimate(
            flops=60 * 10**9, bytes_accessed=40 * MIB, transcendentals=NH * LONG * LONG // 2
        ),
        name="forward",
    )(meta, places, own, other, lines, weight, weight, weight, add, cosine, sine, start)


def backward_kernel(
    meta,
    places,
    own,
    other,
    weight_out,
    q,
    k,
    kt,
    v,
    start,
    context,
    logsum,
    kept,
    lines,
    weight_q,
    weight_k,
    weight_v,
    cosine,
    sine,
    mine,
    theirs,
    g_weight,
    g_add,
    g_gain,
    g_shift,
    rows,
    upper,
    dq,
    dk,
    dv,
    dqt,
    probs,
    slopes,
    g_acc,
    lower,
    back_acc,
):
    step_at = pl.program_id(0)
    i = jnp.minimum(step_at, BLOCKS - 1)
    b = jnp.clip(step_at - BLOCKS, 0, BLOCKS - 1)

    @pl.when(step_at == 0)
    def _():
        for ref in (g_acc, g_add, g_gain, g_shift):
            ref[...] = jnp.zeros_like(ref)

    @pl.when((step_at < BLOCKS) & (meta[2, i] > 0))
    def _():
        gather_rows(meta, i, places, own, other, rows)
        upper[...] = against(rows[...].astype(bfloat), weight_out[...]).astype(bfloat)
        queries = [of_head(q[:, lanes_of(h)], h) for h in range(NH)]
        uppers = [of_head(upper[:, lanes_of(h)], h) for h in range(NH)]
        both = (upper[...].astype(single) * context[...]).T
        delta = [jnp.sum(both[rows_of(h), :], 0, keepdims=True) for h in range(NH)]
        dqt[...] = jnp.zeros_like(dqt)

        def step(j, masked, diagonal):
            r = block_of(j)
            if masked:
                allowed = allowed_of(start, j, diagonal)
            for h in range(NH):
                s = against(k[r, lanes_of(h)], queries[h])
                p = jnp.exp(s - logsum[h : h + 1, :])
                if masked:
                    p = jnp.where(allowed, p, 0.0)
                dp = against(v[r, lanes_of(h)], uppers[h])
                c = slice((h % 2) * BLK, (h % 2) * BLK + BLK)
                probs[h // 2, :, c] = p.astype(bfloat)
                slopes[h // 2, :, c] = (p * (dp - delta[h])).astype(bfloat)
            for g in range(NH // 2):
                c = slice(g * 128, g * 128 + 128)
                part_v = dot(probs[g], jnp.concatenate(uppers[2 * g : 2 * g + 2], 0))
                part_k = dot(slopes[g], jnp.concatenate(queries[2 * g : 2 * g + 2], 0))
                if diagonal:
                    dv[r, c] = part_v
                    dk[r, c] = part_k
                else:
                    dv[r, c] += part_v
                    dk[r, c] += part_k
                for h in (2 * g, 2 * g + 1):
                    e = slice((h % 2) * BLK, (h % 2) * BLK + BLK)
                    dqt[rows_of(h), :] += dot(kt[rows_of(h), r], slopes[g, :, e])

        over_blocks(meta, i, step)
        dq[block_of(i), :] = dqt[...].T * HEAD_DIM ** (-0.5)

    @pl.when((step_at >= BLOCKS) & (step_at < 2 * BLOCKS) & (meta[2, b] > 0))
    def _():
        r = block_of(b)
        turned = []
        for ref in (dq, dk):
            for p in range(0, HW, 128):
                turned.append(turn_lanes(ref[r, p : p + 128], cosine[...], -sine[...]))
        turned.append(dv[r, :])
        mixed = jnp.concatenate(turned, 1).astype(bfloat)
        g_add[...] += jnp.sum(mixed.astype(single), 0, keepdims=True)
        up = (
            against(mixed[:, :HW], weight_q[...])
            + against(mixed[:, HW : 2 * HW], weight_k[...])
            + against(mixed[:, 2 * HW :], weight_v[...])
        )
        lower[r, :] = up.astype(bfloat)
        scaled, _ = norm_stats(kept[...].astype(single))
        g_gain[...] += jnp.sum(up * scaled, 0, keepdims=True)
        g_shift[...] += jnp.sum(up, 0, keepdims=True)
        normed = (scaled * lines[0:1, :] + lines[1:2, :]).astype(bfloat)
        g_acc[...] += over_rows(normed, mixed)

    @pl.when(step_at == 2 * BLOCKS)
    def _():
        for s in range(3):
            g_weight[s] = g_acc[:, s * HW : (s + 1) * HW].astype(bfloat)

    @pl.when(step_at >= 2 * BLOCKS)
    def _():
        return_rows(
            meta, jnp.maximum(step_at - 2 * BLOCKS, 0), places, lower, mine, theirs, back_acc
        )


def backward(
    meta, places, own, other, q, k, kt, v, start, context, logsum, kept, lines, weight, cosine, sine
):
    return pl.pallas_call(
        backward_kernel,
        grid_spec=pltpu.PrefetchScalarGridSpec(
            num_scalar_prefetch=1,
            grid=(2 * BLOCKS + 6,),
            in_specs=[
                held(6, 1, PART),
                held(3, PART, D),
                held(3, PART, D),
                pl.BlockSpec((HW, D), lambda i, m: (m[7, 0], 3), pipeline_mode=pl.Buffered(1)),
                tall_at(HW, 0),
                held(TOTAL, HW),
                held(HW, TOTAL),
                held(TOTAL, HW),
                flat_at(1, 0),
                tall_at(HW, 0),
                flat_at(8, 0),
                tall_at(D, BLOCKS),
                held(16, D),
                *columns(),
                tall_at(128, BLOCKS),
                tall_at(128, BLOCKS),
            ],
            out_specs=[
                *parts_at(2 * BLOCKS, D),
                held(3, D, HW),
                held(1, 3 * HW),
                held(1, D),
                held(1, D),
            ],
            scratch_shapes=[
                pltpu.VMEM((BLK, D), single),
                pltpu.VMEM((BLK, HW), bfloat),
                pltpu.VMEM((TOTAL, HW), single),
                pltpu.VMEM((TOTAL, HW), single),
                pltpu.VMEM((TOTAL, HW), single),
                pltpu.VMEM((HW, BLK), single),
                pltpu.VMEM((NH // 2, BLK, 2 * BLK), bfloat),
                pltpu.VMEM((NH // 2, BLK, 2 * BLK), bfloat),
                pltpu.VMEM((D, 3 * HW), single),
                pltpu.VMEM((TOTAL, D), bfloat),
                pltpu.VMEM((PART, D), single),
            ],
        ),
        out_shape=[
            jax.ShapeDtypeStruct((3, PART, D), bfloat),
            jax.ShapeDtypeStruct((3, PART, D), bfloat),
            jax.ShapeDtypeStruct((3, D, HW), bfloat),
            jax.ShapeDtypeStruct((1, 3 * HW), single),
            jax.ShapeDtypeStruct((1, D), single),
            jax.ShapeDtypeStruct((1, D), single),
        ],
        compiler_params=params(60),
        cost_estimate=pl.CostEstimate(
            flops=90 * 10**9, bytes_accessed=40 * MIB, transcendentals=NH * LONG * LONG // 2
        ),
        name="backward",
    )(
        meta,
        places,
        own,
        other,
        weight,
        q,
        k,
        kt,
        v,
        start,
        context,
        logsum,
        kept,
        lines,
        weight,
        weight,
        weight,
        cosine,
        sine,
    )


def placed_rows(place, moved):
    lane = lax.broadcasted_iota(jnp.int32, (BLK, moved.shape[0]), 1)
    return dot(jnp.where(column(place[...]) == lane, 1.0, 0.0).astype(bfloat), moved[...])


def lower_norm(upper, scaled, factor, gain):
    inner = upper * gain
    return factor * (
        inner
        - jnp.mean(inner, -1, keepdims=True)
        - scaled * jnp.mean(inner * scaled, -1, keepdims=True)
    )


def close_kernel(
    place, moved, weight, lines, tok, tan, feed, feed_back, out, lower, g_weight, sums, g_acc
):
    i = pl.program_id(0)

    @pl.when(i == 0)
    def _():
        g_acc[...] = jnp.zeros_like(g_acc)
        sums[...] = jnp.zeros_like(sums)

    rows = tok[...].astype(single)
    tangent = tan[...]
    context = placed_rows(place, moved).astype(bfloat)
    attended = dot(context, weight[...]) + lines[4:5, :]
    out[...] = (rows + attended + (feed[...] + lines[5:6, :])).astype(bfloat)
    g_acc[...] += over_rows(context, tangent)
    scaled, factor = norm_stats(rows)
    upper = feed_back[...]
    wide = tangent.astype(single)
    lower[...] = wide + lower_norm(upper, scaled, factor, lines[2:3, :])
    sums[0:1, :] += jnp.sum(upper * scaled, 0, keepdims=True)
    sums[1:2, :] += jnp.sum(upper, 0, keepdims=True)
    sums[2:3, :] += jnp.sum(wide, 0, keepdims=True)

    @pl.when(i == pl.num_programs(0) - 1)
    def _():
        g_weight[...] = g_acc[...].astype(bfloat)


def close(place, moved, weights, lines, tok, tan, feed, feed_back):
    rows = tok.shape[0]
    tall = lambda width: pl.BlockSpec((BLK, width), lambda i: (i, 0))
    return pl.pallas_call(
        close_kernel,
        grid=(rows // BLK,),
        in_specs=[
            pl.BlockSpec((1, BLK), lambda i: (0, i)),
            whole(moved.shape),
            pl.BlockSpec((D, D), lambda i: (0, 3)),
            whole((16, D)),
            tall(D),
            tall(D),
            tall(D),
            tall(D),
        ],
        out_specs=[tall(D), tall(D), whole((D, D)), whole((8, D))],
        out_shape=[
            jax.ShapeDtypeStruct((rows, D), bfloat),
            jax.ShapeDtypeStruct((rows, D), single),
            jax.ShapeDtypeStruct((D, D), bfloat),
            jax.ShapeDtypeStruct((8, D), single),
        ],
        scratch_shapes=[pltpu.VMEM((D, D), single)],
        compiler_params=params(60),
        cost_estimate=pl.CostEstimate(
            flops=2 * rows * D * (moved.shape[0] + 2 * D), bytes_accessed=20 * MIB, transcendentals=0
        ),
        name="close",
    )(place, moved, weights, lines, tok, tan, feed, feed_back)


def finish_kernel(place, moved, lines, tok, lower, out):
    scaled, factor = norm_stats(tok[...].astype(single))
    upper = placed_rows(place, moved)
    out[...] = (lower[...] + lower_norm(upper, scaled, factor, lines[0:1, :])).astype(bfloat)


def finish(place, moved, lines, tok, lower):
    rows = tok.shape[0]
    tall = lambda width: pl.BlockSpec((BLK, width), lambda i: (i, 0))
    return pl.pallas_call(
        finish_kernel,
        grid=(rows // BLK,),
        in_specs=[
            pl.BlockSpec((1, BLK), lambda i: (0, i)),
            whole(moved.shape),
            whole((16, D)),
            tall(D),
            tall(D),
        ],
        out_specs=tall(D),
        out_shape=jax.ShapeDtypeStruct((rows, D), bfloat),
        compiler_params=params(60),
        cost_estimate=pl.CostEstimate(
            flops=2 * rows * D * moved.shape[0], bytes_accessed=12 * MIB, transcendentals=0
        ),
        name="finish",
    )(place, moved, lines, tok, lower)


def gather_all(x):
    return lax.all_gather(x, "dp", axis=0, tiled=True)


def body(
    tokens,
    cotangent,
    loss_mask,
    bucket_perm,
    short_lengths,
    row_owner,
    row_slot,
    first_gain,
    first_shift,
    second_gain,
    second_shift,
    project_weight,
    project_bias,
    output_weight,
    output_bias,
    up_weight,
    up_bias,
    down_weight,
    down_bias,
):
    devices = lax.axis_size("dp")
    me = lax.axis_index("dp")
    core = me % 2
    chip = me // 2
    rows = tokens.shape[0]
    share = LONG // devices // 4
    room = 3 * share
    long_count = devices // 4
    swap = [(i, i ^ 1) for i in range(devices)]

    def exchange(x):
        return lax.ppermute(x, "dp", swap)

    chips = devices // 2
    across = math.isqrt(chips // 4)
    sizes = {"core": 2, "x": across, "y": across, "z": 4}
    strides = {"core": 1, "x": 2, "y": 2 * across, "z": 2 * across * across}

    def shifted(x, name, shift):
        n, stride = sizes[name], strides[name]
        hop = []
        for d in range(devices):
            c = (d // stride) % n
            hop.append((d, d + ((c + shift) % n - c) * stride))
        return lax.ppermute(x, "dp", hop)

    def reduce_along(x, name, dim, kind=bfloat):
        n = sizes[name]
        at = (me // strides[name]) % n
        total = lax.dynamic_index_in_dim(x, at, dim, keepdims=False).astype(single)
        for shift in range(1, n):
            sent = lax.dynamic_index_in_dim(x, (at + shift) % n, dim, keepdims=False)
            total = total + shifted(sent, name, shift).astype(single)
        return total.astype(kind)

    def after(x, *others):
        return lax.optimization_barrier((x, *others))[0]

    piece = D // devices
    fours = FF // D
    count = jnp.sum(loss_mask)
    count_column = jnp.where(
        jnp.arange(piece) == 0, count // 256, jnp.where(jnp.arange(piece) == 1, count % 256, 0)
    )
    small = jnp.concatenate(
        [
            jnp.stack([first_gain, first_shift, second_gain, second_shift, output_bias, down_bias], 1),
            project_bias.reshape(3, piece).T,
            up_bias.reshape(piece, fours),
            count_column[:, None].astype(single),
        ],
        1,
    )
    small = jnp.pad(small, ((0, 0), (0, 128 - small.shape[1])))
    spread = jnp.arange(devices, dtype=jnp.int32)
    bucket = jnp.sum(jnp.where(bucket_perm[None, :] == row_owner[:, None], spread[None, :], 0), -1)
    hot = (row_owner[:, None] == spread[None, :]).astype(bfloat)
    line = jnp.arange(rows, dtype=jnp.int32)
    before = (line[None, :] < line[:, None]).astype(bfloat)
    rank = jnp.sum(dot(before, hot) * hot.astype(single), -1).astype(jnp.int32)
    is_long = bucket < long_count
    short = bucket - long_count
    third = jnp.where(is_long, 0, short % 3)
    to_chip = jnp.where(is_long, 2 * bucket, 2 * (short // 3) + 1)
    held = jnp.where(is_long, 2 * share, share)
    to_core = rank // held
    place = (2 * to_chip + to_core) * room + third * share + rank % held
    slot = third * SHORT_TOK + row_slot
    spots = jnp.arange(devices * room, dtype=jnp.int32)
    slot_at = jnp.sum(
        jnp.where(place[None, :] == spots[:, None], slot[None, :] + 1, 0), -1
    ) - 1
    slot_code = jnp.concatenate([(slot_at + 1) // 256, (slot_at + 1) % 256])
    slot_code = slot_code.astype(single).reshape(piece, 2 * devices * room // piece)
    first_all = gather_all(
        jnp.concatenate([project_weight, output_weight, small, slot_code], 1).astype(bfloat)
    )
    lines = first_all[:, 4 * D : 4 * D + 16].astype(single).T
    project_add = lines[6:9].reshape(3, devices, piece).transpose(1, 0, 2).reshape(1, 3, 2, HW)
    project_add_half = lax.dynamic_index_in_dim(project_add, core, 2, keepdims=False).reshape(
        1, 3 * HW
    )
    up_add = lines[9:13].reshape(fours, 1, D)
    counts = lines[13].reshape(devices, piece)
    scale = lax.rsqrt(jnp.sum(counts[:, 0]) * 256.0 + jnp.sum(counts[:, 1]))

    sender = (place[None, :] == spots[:, None]).astype(bfloat)
    place_line = place[None]

    def swap_all(x):
        return lax.all_to_all(x, "dp", split_axis=0, concat_axis=0, tiled=True)

    def outgoing(x):
        return dot(sender, x).astype(bfloat).reshape(devices, room, D)

    def arrange(moved):
        return moved.reshape(devices, 3, share, D).transpose(1, 0, 2, 3).reshape(3, PART, D)

    def send_back(x):
        moved = x.reshape(3, devices, share, D).transpose(1, 0, 2, 3).reshape(devices, room, D)
        return swap_all(moved).reshape(devices * room, D)

    code = first_all[:, 4 * D + 128 :].reshape(devices, 2, chips, 2 * room)
    code = lax.dynamic_index_in_dim(code, chip, 2, keepdims=False).astype(jnp.int32)
    slot_recv = (code[:, 0] * 256 + code[:, 1] - 1).reshape(devices, 2, 3, share)
    slot_recv = slot_recv.transpose(1, 2, 0, 3).reshape(2, 3, PART)
    slot_recv = jnp.where(core == 0, slot_recv, slot_recv[::-1])
    places = slot_recv.reshape(6, 1, PART)

    self_long = chip % 2 == 0
    lengths = lax.dynamic_slice_in_dim(short_lengths, 3 * (chip // 2), 3, 0)
    ends = jnp.cumsum(lengths, -1)
    at = jnp.arange(TOTAL, dtype=jnp.int32).reshape(3, SHORT_TOK)
    inside = jnp.arange(SHORT_TOK, dtype=jnp.int32)
    begun = jnp.max(
        jnp.where(ends[:, None, :] <= inside[None, :, None], ends[:, None, :], 0), -1
    )
    start = jnp.where(self_long, 0, begun + at - inside[None, :]).reshape(TOTAL)
    position = jnp.arange(TOTAL, dtype=jnp.int32) - start
    blocks = jnp.arange(TOTAL // BLK, dtype=jnp.int32)
    low_start = start[::BLK] // BLK
    high_start = (start[BLK - 1 :: BLK] + BLK - 1) // BLK
    zero = jnp.zeros_like(blocks)
    meta = jnp.stack(
        [
            low_start,
            jnp.minimum(blocks, jnp.maximum(low_start, high_start)),
            jnp.where(self_long & (blocks >= LONG // BLK), 0, 1),
            jnp.where(self_long, 0, blocks // (SHORT_TOK // BLK)),
            jnp.where(self_long, 2, 1) + zero,
            jnp.where(self_long, 0, 2 * (blocks % 3)),
            jnp.where(self_long, jnp.where(blocks % 3 == 2, 0, 4), 2 * (blocks % 3) + 2),
            core + zero,
        ]
    ).astype(jnp.int32)
    lane = jnp.arange(128, dtype=jnp.int32) % HEAD_DIM
    freq = 10000.0 ** (-2.0 * (lane % (ROT // 2)).astype(single) / ROT)
    phase = position.astype(single)[:, None] * freq[None, :]
    turning = (lane < ROT)[None, :]
    cosine = jnp.where(turning, jnp.cos(phase), 1.0)
    sine = jnp.where(turning, jnp.sin(phase) * jnp.where(lane < ROT // 2, -1.0, 1.0)[None, :], 0.0)
    starts = start.reshape(1, TOTAL)

    tangent = cotangent * loss_mask.astype(bfloat)[:, None]
    tokens_out = outgoing(tokens)
    tangent_out = outgoing(tangent)
    tokens_out, late_up, late_down = lax.optimization_barrier((tokens_out, up_weight, down_weight))
    up_mixed = late_up.astype(bfloat).reshape(piece, D, fours).transpose(0, 2, 1)
    down_mixed = late_down.astype(bfloat).reshape(piece, fours, D)
    feed_weights = gather_all(
        jnp.concatenate([up_mixed.reshape(piece, FF), down_mixed.reshape(piece, FF)], 1)
    )
    tokens_in = swap_all(tokens_out)
    tokens_in, places, meta, cosine, sine, starts, tangent_out = lax.optimization_barrier(
        (tokens_in, places, meta, cosine, sine, starts, tangent_out)
    )
    own = arrange(tokens_in)
    other = exchange(own)
    kept, q, k, kt, v, context, logsum, context_mine, context_theirs = forward(
        meta,
        places,
        own,
        other,
        lines,
        first_all,
        project_add_half,
        cosine,
        sine,
        starts,
    )

    tangent_in = swap_all(after(tangent_out, context_mine))

    feed, feed_back, wide, up_add_grad = feed_forward(
        after(tokens, context_mine), tangent, lines, feed_weights, up_add
    )
    wide_sum = lax.psum_scatter(wide, "dp", scatter_dimension=0, tiled=True).astype(single)

    mine, theirs = context_mine, exchange(context_theirs)
    context_out = jnp.concatenate(
        [jnp.where(core == 0, mine, theirs), jnp.where(core == 0, theirs, mine)], -1
    )
    context_moved = send_back(context_out)

    upper_own = arrange(after(tangent_in, feed))
    upper_other = exchange(upper_own)
    lower_mine, lower_theirs, *project_parts = backward(
        meta,
        places,
        upper_own,
        upper_other,
        q,
        k,
        kt,
        v,
        starts,
        context,
        logsum,
        kept,
        lines,
        first_all,
        cosine,
        sine,
    )
    lower_sum = (
        lower_mine.astype(single) + exchange(lower_theirs).astype(single)
    ).astype(bfloat)
    upper_moved = send_back(lower_sum)
    project_grad_half, project_add_half_grad, gain_one_grad, shift_one_grad = project_parts

    block_out, lower_two, output_grad, sums = close(
        place_line,
        after(context_moved, lower_sum),
        first_all,
        lines,
        tokens,
        tangent,
        feed,
        feed_back,
    )

    def pair_up(one, two):
        return jnp.where(
            core == 0, jnp.concatenate([one, two], -1), jnp.concatenate([two, one], -1)
        )

    add_half = project_add_half_grad.reshape(3, HW)
    project_add_grad = pair_up(add_half, jnp.zeros_like(add_half)).reshape(devices, 3, piece)
    vectors = jnp.concatenate(
        [
            gain_one_grad,
            shift_one_grad,
            sums[:3],
            project_add_grad.transpose(1, 0, 2).reshape(3, D),
            up_add_grad.reshape(fours, D),
            jnp.zeros((4, D), single),
        ],
        0,
    )
    def over_chips(x):
        return x.reshape((4, across, across) + x.shape[1:])

    extra = vectors.reshape(16, devices, piece).transpose(1, 0, 2).reshape(devices, 1, 16 * piece)
    extra = jnp.pad(extra, ((0, 0), (0, 7), (0, D - 16 * piece))).astype(bfloat)
    output_part = jnp.concatenate([output_grad.reshape(devices, piece, D), extra], 1)
    output_half = reduce_along(output_part.reshape(chips, 2, piece + 8, D), "core", 1)
    projects = project_grad_half.reshape(3, chips, 2 * piece, HW)
    one = over_chips(jnp.concatenate([projects[0], projects[1]], 1))
    two = over_chips(
        jnp.concatenate([projects[2], output_half[..., :HW], output_half[..., HW:]], 1)
    )
    one = reduce_along(reduce_along(one, "x", 2), "y", 1)
    two = reduce_along(reduce_along(two, "y", 1), "x", 1)
    narrow = reduce_along(jnp.concatenate([one, two], 1), "z", 0, single)

    by_core = narrow[: 6 * piece].reshape(3, 2, piece, HW)
    for_me = lax.dynamic_index_in_dim(by_core, core, 1, keepdims=False)
    for_other = lax.dynamic_index_in_dim(by_core, 1 - core, 1, keepdims=False)
    project_grad = pair_up(for_me, exchange(for_other)).transpose(1, 0, 2).reshape(piece, 3 * D)
    low_half, high_half = narrow[6 * piece : 7 * piece + 8], narrow[7 * piece + 8 :]
    output_sum = jnp.concatenate([low_half[:piece], high_half[:piece]], -1)
    vector_sum = jnp.concatenate([low_half[piece], high_half[piece]])[: 16 * piece]
    vector_sum = vector_sum.reshape(16, piece) * scale
    wide_sum = wide_sum.reshape(piece, fours, 2, D)
    up_sum = wide_sum[:, :, 0].transpose(0, 2, 1).reshape(piece, FF)
    down_sum = wide_sum[:, :, 1].reshape(fours * piece, D)
    scaled = lax.optimization_barrier(
        (upper_moved, vector_sum, project_grad * scale, output_sum * scale, up_sum * scale, down_sum * scale)
    )
    tokens_grad = finish(place_line, scaled[0], lines, tokens, lower_two)
    vector_sum, project_sum, output_sum, up_sum, down_sum = scaled[1:]
    return (
        block_out,
        tokens_grad,
        vector_sum[0],
        vector_sum[1],
        vector_sum[2],
        vector_sum[3],
        project_sum,
        vector_sum[5:8].reshape(3 * piece),
        output_sum,
        vector_sum[4],
        up_sum,
        vector_sum[8:12].T.reshape(fours * piece),
        down_sum,
        vector_sum[4],
    )


def solution(mesh):
    tall, flat = P("dp", None), P("dp")
    return jax.shard_map(
        body,
        mesh=mesh,
        in_specs=(
            tall,
            tall,
            flat,
            P(),
            P(),
            flat,
            flat,
            flat,
            flat,
            flat,
            flat,
            tall,
            flat,
            tall,
            flat,
            tall,
            flat,
            tall,
            flat,
        ),
        out_specs=(
            tall,
            tall,
            flat,
            flat,
            flat,
            flat,
            tall,
            flat,
            tall,
            flat,
            tall,
            flat,
            tall,
            flat,
        ),
        check_vma=False,
    )
```

```python
import functools
import math

import jax
import jax.numpy as jnp
from jax import lax
from jax.experimental import pallas as pl
from jax.experimental.pallas import tpu as pltpu
from jax.sharding import PartitionSpec as P

D = 768
HEADS = 12
HEAD_DIM = 64
ROT = 16
FF = 3072
LONG = 2048
SHORT_TOK = 1024
TOTAL = 3 * SHORT_TOK
BLK = 256
BLOCKS = TOTAL // BLK
NH = HEADS // 2
HW = NH * HEAD_DIM
PART = SHORT_TOK // 2
MIB = 2**20

epsilon = 1e-05
bfloat = jnp.bfloat16
single = jnp.float32


def dot(left, right):
    return jnp.dot(left, right, preferred_element_type=single)


def over_rows(left, right):
    return lax.dot_general(left, right, (((0,), (0,)), ((), ())), preferred_element_type=single)


def against(left, right):
    return lax.dot_general(left, right, (((1,), (1,)), ((), ())), preferred_element_type=single)


def norm_stats(values):
    mean = jnp.mean(values, -1, keepdims=True)
    centred = values - mean
    spread = jnp.mean(centred * centred, -1, keepdims=True)
    factor = lax.rsqrt(spread + epsilon)
    return (centred * factor, factor)


def lower_norm(upper, scaled, factor, gain):
    inner = upper * gain
    return factor * (
        inner
        - jnp.mean(inner, -1, keepdims=True)
        - scaled * jnp.mean(inner * scaled, -1, keepdims=True)
    )


def params(mib):
    return pltpu.CompilerParams(vmem_limit_bytes=mib * MIB)


def whole(shape):
    return pl.BlockSpec(shape, lambda *_: (0,) * len(shape))


def feed_kernel(
    tok, tan, lines, up, up_add, down, feed, lower, grad, g_up_add, sums, normed, act, slope
):
    step = pl.program_id(0)
    rows = tok.shape[0]
    chunk = rows // 2
    root = 1.0 / math.sqrt(2.0)
    dens = 1.0 / math.sqrt(2.0 * math.pi)

    @pl.when(step == 0)
    def _():
        def one(i, carry):
            r = pl.ds(pl.multiple_of(i * BLK, BLK), BLK)
            scaled, _ = norm_stats(tok[r, :].astype(single))
            normed[r, :] = (scaled * lines[2:3, :] + lines[3:4, :]).astype(bfloat)
            return carry

        lax.fori_loop(0, rows // BLK, one, 0)

    bias_sum = jnp.zeros((1, D), single)
    for i in range(2):
        r = pl.ds(i * chunk, chunk)
        hidden = dot(normed[r, :], up[...]) + up_add[0]
        above = against(tan[r, :], down[...])
        phi = 0.5 * (1.0 + lax.erf(hidden * root))
        active = (hidden * phi).astype(bfloat)
        sl = (above * (phi + hidden * (dens * jnp.exp(-0.5 * hidden * hidden)))).astype(bfloat)
        act[r, :] = active
        slope[r, :] = sl
        bias_sum = bias_sum + jnp.sum(sl.astype(single), 0, keepdims=True)
        part_feed = dot(active, down[...])
        part_lower = against(sl, up[...])

        @pl.when(step == 0)
        def _():
            feed[r, :] = part_feed
            lower[r, :] = part_lower

        @pl.when(step > 0)
        def _():
            feed[r, :] += part_feed
            lower[r, :] += part_lower

    g_up_add[0] = bias_sum
    grad[:, :D] = over_rows(normed[...], slope[...]).astype(bfloat)
    grad[:, D:] = over_rows(act[...], tan[...]).astype(bfloat)

    @pl.when(step == pl.num_programs(0) - 1)
    def _():
        def one(i, carry):
            r = pl.ds(pl.multiple_of(i * BLK, BLK), BLK)
            scaled, factor = norm_stats(tok[r, :].astype(single))
            upper, wide = lower[r, :], tan[r, :].astype(single)
            lower[r, :] = wide + lower_norm(upper, scaled, factor, lines[2:3, :])
            terms = (upper * scaled, upper, wide)
            return tuple(c + jnp.sum(t, 0, keepdims=True) for c, t in zip(carry, terms))

        parts = lax.fori_loop(0, rows // BLK, one, (jnp.zeros((1, D), single),) * 3)
        sums[...] = jnp.zeros_like(sums)
        for i in range(3):
            sums[i : i + 1, :] = parts[i]


def feed_forward(tok, tan, lines, weights, up_add):
    rows, count = tok.shape[0], FF // D
    wide = lambda where: pl.BlockSpec((D, D), lambda j: (0, where + j))
    one = lambda shape: pl.BlockSpec(shape, lambda j: (0, 0), pipeline_mode=pl.Buffered(1))
    line = pl.BlockSpec((1, 1, D), lambda j: (j, 0, 0))
    pair = pl.BlockSpec((D, 2 * D), lambda j: (0, j))
    return pl.pallas_call(
        feed_kernel,
        grid=(count,),
        in_specs=[one((rows, D)), one((rows, D)), one((16, D)), wide(0), line, wide(count)],
        out_specs=[one((rows, D)), one((rows, D)), pair, line, one((8, D))],
        out_shape=[
            jax.ShapeDtypeStruct((rows, D), single),
            jax.ShapeDtypeStruct((rows, D), single),
            jax.ShapeDtypeStruct((D, 2 * count * D), bfloat),
            jax.ShapeDtypeStruct((count, 1, D), single),
            jax.ShapeDtypeStruct((8, D), single),
        ],
        scratch_shapes=[
            pltpu.VMEM((rows, D), bfloat),
            pltpu.VMEM((rows, D), bfloat),
            pltpu.VMEM((rows, D), bfloat),
        ],
        compiler_params=params(60),
        cost_estimate=pl.CostEstimate(
            flops=12 * rows * D * D * count, bytes_accessed=count * 12 * MIB, transcendentals=2 * rows * D * count
        ),
        name="feed_forward",
    )(tok, tan, lines, weights, up_add, weights)


def gather_rows(meta, i, places, own, other, rows):
    spot = lax.broadcasted_iota(jnp.int32, (BLK, PART), 0) + i * BLK

    def part(k):
        mine = jnp.where(places[k] == spot, 1.0, 0.0).astype(bfloat)
        theirs = jnp.where(places[k + 3] == spot, 1.0, 0.0).astype(bfloat)
        return dot(mine, own[k]) + dot(theirs, other[k])

    low = meta[3, i]
    rows[...] = part(low)

    @pl.when(meta[4, i] > 1)
    def _():
        rows[...] += part(low + 1)


def column(line):
    return jnp.broadcast_to(line, (128, line.shape[1])).T[:, 0:1]


def return_rows(meta, at, places, values, mine, theirs, acc):
    b = lax.rem(at + 3, 6)
    acc[...] = jnp.zeros_like(acc)
    lane = lax.broadcasted_iota(jnp.int32, (PART, PART), 1)
    spots = column(places[b])

    def one(c, carry):
        hot = jnp.where(spots == lane + c * PART, 1.0, 0.0).astype(bfloat)
        r = pl.ds(pl.multiple_of(c * PART, PART), PART)
        acc[...] += dot(hot, values[r, :])
        return carry

    lax.fori_loop(meta[5, b], meta[6, b], one, 0)

    @pl.when(at < 3)
    def _():
        theirs[0] = acc[...].astype(bfloat)

    @pl.when(at >= 3)
    def _():
        mine[0] = acc[...].astype(bfloat)


def turn_lanes(values, cosine, sine):
    lane = lax.broadcasted_iota(jnp.int32, values.shape, 1)
    swapped = jnp.where(
        (lane & (ROT - 1)) < ROT // 2, pltpu.roll(values, 128 - ROT // 2, 1), pltpu.roll(values, ROT // 2, 1)
    )
    return values * cosine + swapped * sine


def of_head(values, h):
    lane = lax.broadcasted_iota(jnp.int32, values.shape, 1)
    return jnp.where((lane < HEAD_DIM) == (h % 2 == 0), values, jnp.zeros_like(values))


def lanes_of(h):
    return slice((h // 2) * 128, (h // 2) * 128 + 128)


def rows_of(h):
    return slice(h * HEAD_DIM, (h + 1) * HEAD_DIM)


def block_of(j):
    return pl.ds(pl.multiple_of(j * BLK, BLK), BLK)


def allowed_of(start, j, diagonal):
    row = lax.broadcasted_iota(jnp.int32, (BLK, BLK), 0)
    allowed = row + j * BLK >= start[...]
    if diagonal:
        allowed &= row <= lax.broadcasted_iota(jnp.int32, (BLK, BLK), 1)
    return allowed


def over_blocks(meta, i, step):
    def masked(j, carry):
        step(j, True, False)
        return carry

    def plain(j, carry):
        step(j, False, False)
        return carry

    lax.fori_loop(meta[0, i], meta[1, i], masked, 0)
    lax.fori_loop(meta[1, i], i, plain, 0)
    step(i, True, True)


def forward_kernel(
    meta,
    places,
    own,
    other,
    lines,
    weight_q,
    weight_k,
    weight_v,
    add,
    cosine,
    sine,
    start,
    kept,
    q,
    k,
    kt,
    v,
    context,
    logsum,
    mine,
    theirs,
    rows,
    keys,
    values,
    score,
    peak,
    total,
    acc,
    done,
    back_acc,
):
    step_at = pl.program_id(0)
    i = jnp.minimum(step_at, BLOCKS - 1)
    here = block_of(i)
    live = (step_at < BLOCKS) & (meta[2, i] > 0)

    @pl.when(live)
    def _():
        gather_rows(meta, i, places, own, other, rows)
        scaled, _ = norm_stats(rows[...])
        n = (scaled * lines[0:1, :] + lines[1:2, :]).astype(bfloat)
        kept[...] = rows[...].astype(bfloat)
        for s, weight in enumerate((weight_q, weight_k, weight_v)):
            mixed = dot(n, weight[...]) + add[:, s * HW : (s + 1) * HW]
            if s < 2:
                mixed = jnp.concatenate(
                    [
                        turn_lanes(mixed[:, p : p + 128], cosine[...], sine[...])
                        for p in range(0, HW, 128)
                    ],
                    1,
                )
            narrow = mixed.astype(bfloat)
            if s == 0:
                q[...] = narrow * HEAD_DIM ** (-0.5)
            elif s == 1:
                k[...] = narrow
                keys[here, :] = narrow
                kt[...] = narrow.T
            else:
                v[...] = narrow
                values[:, here] = narrow.T

        first = meta[0, i]
        queries = [of_head(q[:, lanes_of(h)], h) for h in range(NH)]
        peak[...] = jnp.full(peak.shape, -jnp.inf, single)

        def step(j, masked, diagonal):
            if masked:
                allowed = allowed_of(start, j, diagonal)
            for h in range(NH):
                s = against(keys[block_of(j), lanes_of(h)], queries[h])
                if masked:
                    s = jnp.where(allowed, s, -jnp.inf)
                score[h, block_of(j - first), :] = s
                peak[h] = jnp.maximum(peak[h], jnp.max(s.reshape(BLK // 8, 8, BLK), 0))

        over_blocks(meta, i, step)
        tops = [jnp.max(peak[h], 0, keepdims=True) for h in range(NH)]
        total[...] = jnp.zeros_like(total)
        acc[...] = jnp.zeros_like(acc)

        def gain(j, carry):
            for h in range(NH):
                p = jnp.exp(score[h, block_of(j - first), :] - tops[h])
                total[h] += jnp.sum(p.reshape(BLK // 8, 8, BLK), 0)
                acc[rows_of(h), :] += dot(values[rows_of(h), block_of(j)], p.astype(bfloat))
            return carry

        lax.fori_loop(first, i + 1, gain, 0)
        for h in range(NH):
            whole_sum = jnp.sum(total[h], 0, keepdims=True)
            acc[rows_of(h), :] = acc[rows_of(h), :] / whole_sum
            logsum[h : h + 1, :] = tops[h] + jnp.log(whole_sum)
        turned = acc[...].T
        context[...] = turned
        done[here, :] = turned.astype(bfloat)

    @pl.when((step_at < BLOCKS) & (meta[2, i] == 0))
    def _():
        for ref in (kept, q, k, kt, v, context, logsum):
            ref[...] = jnp.zeros_like(ref)

    @pl.when(step_at >= BLOCKS)
    def _():
        return_rows(meta, jnp.maximum(step_at - BLOCKS, 0), places, done, mine, theirs, back_acc)


def columns():
    return [
        pl.BlockSpec((D, HW), lambda i, m, s=s: (0, 2 * s + m[7, 0]), pipeline_mode=pl.Buffered(1))
        for s in range(3)
    ]


def held(*shape):
    return pl.BlockSpec(shape, lambda i, m: (0,) * len(shape), pipeline_mode=pl.Buffered(1))


def tall_at(width, first):
    return pl.BlockSpec((BLK, width), lambda i, m: (jnp.clip(i - first, 0, BLOCKS - 1), 0))


def flat_at(height, first):
    return pl.BlockSpec((height, BLK), lambda i, m: (0, jnp.clip(i - first, 0, BLOCKS - 1)))


def parts_at(first, width):
    return [
        pl.BlockSpec((1, PART, width), lambda i, m, f=f: (jnp.clip(i - f, 0, 2), 0, 0))
        for f in (first + 3, first)
    ]


def forward(meta, places, own, other, lines, weight, add, cosine, sine, start):
    out = lambda *shape: jax.ShapeDtypeStruct(shape, bfloat)
    return pl.pallas_call(
        forward_kernel,
        grid_spec=pltpu.PrefetchScalarGridSpec(
            num_scalar_prefetch=1,
            grid=(BLOCKS + 6,),
            in_specs=[
                held(6, 1, PART),
                held(3, PART, D),
                held(3, PART, D),
                held(16, D),
                *columns(),
                held(1, 3 * HW),
                tall_at(128, 0),
                tall_at(128, 0),
                flat_at(1, 0),
            ],
            out_specs=[
                tall_at(D, 0),
                tall_at(HW, 0),
                tall_at(HW, 0),
                flat_at(HW, 0),
                tall_at(HW, 0),
                tall_at(HW, 0),
                flat_at(8, 0),
                *parts_at(BLOCKS, HW),
            ],
            scratch_shapes=[
                pltpu.VMEM((BLK, D), single),
                pltpu.VMEM((TOTAL, HW), bfloat),
                pltpu.VMEM((HW, TOTAL), bfloat),
                pltpu.VMEM((NH, LONG, BLK), single),
                pltpu.VMEM((NH, 8, BLK), single),
                pltpu.VMEM((NH, 8, BLK), single),
                pltpu.VMEM((HW, BLK), single),
                pltpu.VMEM((TOTAL, HW), bfloat),
                pltpu.VMEM((PART, HW), single),
            ],
        ),
        out_shape=[
            out(TOTAL, D),
            out(TOTAL, HW),
            out(TOTAL, HW),
            out(HW, TOTAL),
            out(TOTAL, HW),
            jax.ShapeDtypeStruct((TOTAL, HW), single),
            jax.ShapeDtypeStruct((8, TOTAL), single),
            out(3, PART, HW),
            out(3, PART, HW),
        ],
        compiler_params=params(60),
        cost_estimate=pl.CostEstimate(
            flops=75 * 10**9, bytes_accessed=40 * MIB, transcendentals=NH * LONG * LONG // 2
        ),
        name="forward",
    )(meta, places, own, other, lines, weight, weight, weight, add, cosine, sine, start)


def backward_kernel(
    meta,
    places,
    own,
    other,
    weight_out,
    q,
    k,
    kt,
    v,
    start,
    context,
    logsum,
    kept,
    lines,
    weight_q,
    weight_k,
    weight_v,
    cosine,
    sine,
    mine,
    theirs,
    g_out,
    g_weight,
    g_add,
    g_gain,
    g_shift,
    rows,
    upper,
    dq,
    dk,
    dv,
    dqt,
    probs,
    slopes,
    out_acc,
    g_acc,
    lower,
    back_acc,
):
    step_at = pl.program_id(0)
    i = jnp.minimum(step_at, BLOCKS - 1)
    b = jnp.clip(step_at - BLOCKS, 0, BLOCKS - 1)

    @pl.when(step_at == 0)
    def _():
        for ref in (out_acc, g_acc, g_add, g_gain, g_shift):
            ref[...] = jnp.zeros_like(ref)

    @pl.when((step_at < BLOCKS) & (meta[2, i] > 0))
    def _():
        gather_rows(meta, i, places, own, other, rows)
        tangent = rows[...].astype(bfloat)
        upper[...] = against(tangent, weight_out[...]).astype(bfloat)
        out_acc[...] += over_rows(context[...].astype(bfloat), tangent)
        queries = [of_head(q[:, lanes_of(h)], h) for h in range(NH)]
        uppers = [of_head(upper[:, lanes_of(h)], h) for h in range(NH)]
        both = (upper[...].astype(single) * context[...]).T
        delta = [jnp.sum(both[rows_of(h), :], 0, keepdims=True) for h in range(NH)]
        dqt[...] = jnp.zeros_like(dqt)

        def step(j, masked, diagonal):
            r = block_of(j)
            if masked:
                allowed = allowed_of(start, j, diagonal)
            for h in range(NH):
                s = against(k[r, lanes_of(h)], queries[h])
                p = jnp.exp(s - logsum[h : h + 1, :])
                if masked:
                    p = jnp.where(allowed, p, 0.0)
                dp = against(v[r, lanes_of(h)], uppers[h])
                c = slice((h % 2) * BLK, (h % 2) * BLK + BLK)
                probs[h // 2, :, c] = p.astype(bfloat)
                slopes[h // 2, :, c] = (p * (dp - delta[h])).astype(bfloat)
            for g in range(NH // 2):
                c = slice(g * 128, g * 128 + 128)
                part_v = dot(probs[g], jnp.concatenate(uppers[2 * g : 2 * g + 2], 0))
                part_k = dot(slopes[g], jnp.concatenate(queries[2 * g : 2 * g + 2], 0))
                if diagonal:
                    dv[r, c] = part_v
                    dk[r, c] = part_k
                else:
                    dv[r, c] += part_v
                    dk[r, c] += part_k
                for h in (2 * g, 2 * g + 1):
                    e = slice((h % 2) * BLK, (h % 2) * BLK + BLK)
                    dqt[rows_of(h), :] += dot(kt[rows_of(h), r], slopes[g, :, e])

        over_blocks(meta, i, step)
        dq[block_of(i), :] = dqt[...].T * HEAD_DIM ** (-0.5)

    @pl.when((step_at >= BLOCKS) & (step_at < 2 * BLOCKS) & (meta[2, b] > 0))
    def _():
        r = block_of(b)
        turned = []
        for ref in (dq, dk):
            for p in range(0, HW, 128):
                turned.append(turn_lanes(ref[r, p : p + 128], cosine[...], -sine[...]))
        turned.append(dv[r, :])
        mixed = jnp.concatenate(turned, 1).astype(bfloat)
        g_add[...] += jnp.sum(mixed.astype(single), 0, keepdims=True)
        up = (
            against(mixed[:, :HW], weight_q[...])
            + against(mixed[:, HW : 2 * HW], weight_k[...])
            + against(mixed[:, 2 * HW :], weight_v[...])
        )
        lower[r, :] = up.astype(bfloat)
        scaled, _ = norm_stats(kept[...].astype(single))
        g_gain[...] += jnp.sum(up * scaled, 0, keepdims=True)
        g_shift[...] += jnp.sum(up, 0, keepdims=True)
        normed = (scaled * lines[0:1, :] + lines[1:2, :]).astype(bfloat)
        g_acc[...] += over_rows(normed, mixed)

    @pl.when(step_at == 2 * BLOCKS)
    def _():
        g_out[...] = out_acc[...].astype(bfloat)
        for s in range(3):
            g_weight[s] = g_acc[:, s * HW : (s + 1) * HW].astype(bfloat)

    @pl.when(step_at >= 2 * BLOCKS)
    def _():
        return_rows(
            meta, jnp.maximum(step_at - 2 * BLOCKS, 0), places, lower, mine, theirs, back_acc
        )


def backward(
    meta, places, own, other, q, k, kt, v, start, context, logsum, kept, lines, weight, cosine, sine
):
    return pl.pallas_call(
        backward_kernel,
        grid_spec=pltpu.PrefetchScalarGridSpec(
            num_scalar_prefetch=1,
            grid=(2 * BLOCKS + 6,),
            in_specs=[
                held(6, 1, PART),
                held(3, PART, D),
                held(3, PART, D),
                pl.BlockSpec((HW, D), lambda i, m: (m[7, 0], 3), pipeline_mode=pl.Buffered(1)),
                tall_at(HW, 0),
                held(TOTAL, HW),
                held(HW, TOTAL),
                held(TOTAL, HW),
                flat_at(1, 0),
                tall_at(HW, 0),
                flat_at(8, 0),
                tall_at(D, BLOCKS),
                held(16, D),
                *columns(),
                tall_at(128, BLOCKS),
                tall_at(128, BLOCKS),
            ],
            out_specs=[
                *parts_at(2 * BLOCKS, D),
                held(HW, D),
                held(3, D, HW),
                held(1, 3 * HW),
                held(1, D),
                held(1, D),
            ],
            scratch_shapes=[
                pltpu.VMEM((BLK, D), single),
                pltpu.VMEM((BLK, HW), bfloat),
                pltpu.VMEM((TOTAL, HW), single),
                pltpu.VMEM((TOTAL, HW), single),
                pltpu.VMEM((TOTAL, HW), single),
                pltpu.VMEM((HW, BLK), single),
                pltpu.VMEM((NH // 2, BLK, 2 * BLK), bfloat),
                pltpu.VMEM((NH // 2, BLK, 2 * BLK), bfloat),
                pltpu.VMEM((HW, D), single),
                pltpu.VMEM((D, 3 * HW), single),
                pltpu.VMEM((TOTAL, D), bfloat),
                pltpu.VMEM((PART, D), single),
            ],
        ),
        out_shape=[
            jax.ShapeDtypeStruct((3, PART, D), bfloat),
            jax.ShapeDtypeStruct((3, PART, D), bfloat),
            jax.ShapeDtypeStruct((HW, D), bfloat),
            jax.ShapeDtypeStruct((3, D, HW), bfloat),
            jax.ShapeDtypeStruct((1, 3 * HW), single),
            jax.ShapeDtypeStruct((1, D), single),
            jax.ShapeDtypeStruct((1, D), single),
        ],
        compiler_params=params(60),
        cost_estimate=pl.CostEstimate(
            flops=90 * 10**9, bytes_accessed=40 * MIB, transcendentals=NH * LONG * LONG // 2
        ),
        name="backward",
    )(
        meta,
        places,
        own,
        other,
        weight,
        q,
        k,
        kt,
        v,
        start,
        context,
        logsum,
        kept,
        lines,
        weight,
        weight,
        weight,
        cosine,
        sine,
    )


def placed_rows(place, moved):
    lane = lax.broadcasted_iota(jnp.int32, (BLK, moved.shape[0]), 1)
    return dot(jnp.where(column(place[...]) == lane, 1.0, 0.0).astype(bfloat), moved[...])


def close_kernel(place, moved, weight, lines, tok, feed, out):
    context = placed_rows(place, moved).astype(bfloat)
    attended = dot(context, weight[...]) + lines[4:5, :]
    out[...] = (tok[...].astype(single) + attended + (feed[...] + lines[5:6, :])).astype(bfloat)


def close(place, moved, weights, lines, tok, feed):
    rows = tok.shape[0]
    tall = lambda width: pl.BlockSpec((BLK, width), lambda i: (i, 0))
    return pl.pallas_call(
        close_kernel,
        grid=(rows // BLK,),
        in_specs=[
            pl.BlockSpec((1, BLK), lambda i: (0, i)),
            whole(moved.shape),
            pl.BlockSpec((D, D), lambda i: (0, 3)),
            whole((16, D)),
            tall(D),
            tall(D),
        ],
        out_specs=tall(D),
        out_shape=jax.ShapeDtypeStruct((rows, D), bfloat),
        compiler_params=params(60),
        cost_estimate=pl.CostEstimate(
            flops=12 * 10**9, bytes_accessed=12 * MIB, transcendentals=0
        ),
        name="close",
    )(place, moved, weights, lines, tok, feed)


def finish_kernel(place, moved, lines, tok, lower, out):
    scaled, factor = norm_stats(tok[...].astype(single))
    upper = placed_rows(place, moved)
    out[...] = (lower[...] + lower_norm(upper, scaled, factor, lines[0:1, :])).astype(bfloat)


def finish(place, moved, lines, tok, lower):
    rows = tok.shape[0]
    tall = lambda width: pl.BlockSpec((BLK, width), lambda i: (i, 0))
    return pl.pallas_call(
        finish_kernel,
        grid=(rows // BLK,),
        in_specs=[
            pl.BlockSpec((1, BLK), lambda i: (0, i)),
            whole(moved.shape),
            whole((16, D)),
            tall(D),
            tall(D),
        ],
        out_specs=tall(D),
        out_shape=jax.ShapeDtypeStruct((rows, D), bfloat),
        compiler_params=params(60),
        cost_estimate=pl.CostEstimate(
            flops=2 * rows * D * moved.shape[0], bytes_accessed=12 * MIB, transcendentals=0
        ),
        name="finish",
    )(place, moved, lines, tok, lower)


def gather_all(x):
    return lax.all_gather(x, "dp", axis=0, tiled=True)


def body(
    tokens,
    cotangent,
    loss_mask,
    bucket_perm,
    short_lengths,
    row_owner,
    row_slot,
    first_gain,
    first_shift,
    second_gain,
    second_shift,
    project_weight,
    project_bias,
    output_weight,
    output_bias,
    up_weight,
    up_bias,
    down_weight,
    down_bias,
):
    devices = lax.axis_size("dp")
    me = lax.axis_index("dp")
    core = me % 2
    chip = me // 2
    rows = tokens.shape[0]
    share = LONG // devices // 4
    room = 3 * share
    long_count = devices // 4
    swap = [(i, i ^ 1) for i in range(devices)]

    def exchange(x):
        return lax.ppermute(x, "dp", swap)

    chips = devices // 2
    across = math.isqrt(chips // 4)
    sizes = {"core": 2, "x": across, "y": across, "z": 4}
    strides = {"core": 1, "x": 2, "y": 2 * across, "z": 2 * across * across}

    def shifted(x, name, shift):
        n, stride = sizes[name], strides[name]
        hop = []
        for d in range(devices):
            c = (d // stride) % n
            hop.append((d, d + ((c + shift) % n - c) * stride))
        return lax.ppermute(x, "dp", hop)

    def after(x, *others):
        return lax.optimization_barrier((x, *others))[0]

    def reduce_along(x, name, dim, kind=bfloat, late=None):
        n = sizes[name]
        at = (me // strides[name]) % n
        total = lax.dynamic_index_in_dim(x, at, dim, keepdims=False).astype(single)
        for shift in range(1, n):
            sent = lax.dynamic_index_in_dim(x, (at + shift) % n, dim, keepdims=False)
            got = shifted(sent, name, shift)
            total = total + (got if late is None else after(got, late)).astype(single)
        return total.astype(kind)

    piece = D // devices
    fours = FF // D
    count = jnp.sum(loss_mask)
    count_column = jnp.where(
        jnp.arange(piece) == 0, count // 256, jnp.where(jnp.arange(piece) == 1, count % 256, 0)
    )
    small = jnp.concatenate(
        [
            jnp.stack([first_gain, first_shift, second_gain, second_shift, output_bias, down_bias], 1),
            project_bias.reshape(3, piece).T,
            up_bias.reshape(piece, fours),
            count_column[:, None].astype(single),
        ],
        1,
    )
    small = jnp.pad(small, ((0, 0), (0, 128 - small.shape[1])))
    spread = jnp.arange(devices, dtype=jnp.int32)
    bucket = jnp.sum(jnp.where(bucket_perm[None, :] == row_owner[:, None], spread[None, :], 0), -1)
    hot = (row_owner[:, None] == spread[None, :]).astype(bfloat)
    line = jnp.arange(rows, dtype=jnp.int32)
    before = (line[None, :] < line[:, None]).astype(bfloat)
    rank = jnp.sum(dot(before, hot) * hot.astype(single), -1).astype(jnp.int32)
    is_long = bucket < long_count
    short = bucket - long_count
    third = jnp.where(is_long, 0, short % 3)
    to_chip = jnp.where(is_long, 2 * bucket, 2 * (short // 3) + 1)
    held = jnp.where(is_long, 2 * share, share)
    to_core = rank // held
    place = (2 * to_chip + to_core) * room + third * share + rank % held
    slot = third * SHORT_TOK + row_slot
    spots = jnp.arange(devices * room, dtype=jnp.int32)
    slot_at = jnp.sum(
        jnp.where(place[None, :] == spots[:, None], slot[None, :] + 1, 0), -1
    ) - 1
    slot_code = jnp.concatenate([(slot_at + 1) // 256, (slot_at + 1) % 256])
    slot_code = slot_code.astype(single).reshape(piece, 2 * devices * room // piece)
    first_all = gather_all(
        jnp.concatenate([project_weight, output_weight, small, slot_code], 1).astype(bfloat)
    )
    lines = first_all[:, 4 * D : 4 * D + 16].astype(single).T
    project_add = lines[6:9].reshape(3, devices, piece).transpose(1, 0, 2).reshape(1, 3, 2, HW)
    project_add_half = lax.dynamic_index_in_dim(project_add, core, 2, keepdims=False).reshape(
        1, 3 * HW
    )
    up_add = lines[9:13].reshape(fours, 1, D)
    counts = lines[13].reshape(devices, piece)
    scale = lax.rsqrt(jnp.sum(counts[:, 0]) * 256.0 + jnp.sum(counts[:, 1]))

    sender = (place[None, :] == spots[:, None]).astype(bfloat)
    place_line = place[None]

    def swap_all(x):
        return lax.all_to_all(x, "dp", split_axis=0, concat_axis=0, tiled=True)

    def outgoing(x):
        return dot(sender, x).astype(bfloat).reshape(devices, room, D)

    def arrange(moved):
        return moved.reshape(devices, 3, share, D).transpose(1, 0, 2, 3).reshape(3, PART, D)

    def send_back(x):
        moved = x.reshape(3, devices, share, D).transpose(1, 0, 2, 3).reshape(devices, room, D)
        return swap_all(moved).reshape(devices * room, D)

    code = first_all[:, 4 * D + 128 :].reshape(devices, 2, chips, 2 * room)
    code = lax.dynamic_index_in_dim(code, chip, 2, keepdims=False).astype(jnp.int32)
    slot_recv = (code[:, 0] * 256 + code[:, 1] - 1).reshape(devices, 2, 3, share)
    slot_recv = slot_recv.transpose(1, 2, 0, 3).reshape(2, 3, PART)
    slot_recv = jnp.where(core == 0, slot_recv, slot_recv[::-1])
    places = slot_recv.reshape(6, 1, PART)

    self_long = chip % 2 == 0
    lengths = lax.dynamic_slice_in_dim(short_lengths, 3 * (chip // 2), 3, 0)
    ends = jnp.cumsum(lengths, -1)
    at = jnp.arange(TOTAL, dtype=jnp.int32).reshape(3, SHORT_TOK)
    inside = jnp.arange(SHORT_TOK, dtype=jnp.int32)
    begun = jnp.max(
        jnp.where(ends[:, None, :] <= inside[None, :, None], ends[:, None, :], 0), -1
    )
    start = jnp.where(self_long, 0, begun + at - inside[None, :]).reshape(TOTAL)
    position = jnp.arange(TOTAL, dtype=jnp.int32) - start
    blocks = jnp.arange(TOTAL // BLK, dtype=jnp.int32)
    low_start = start[::BLK] // BLK
    high_start = (start[BLK - 1 :: BLK] + BLK - 1) // BLK
    zero = jnp.zeros_like(blocks)
    meta = jnp.stack(
        [
            low_start,
            jnp.minimum(blocks, jnp.maximum(low_start, high_start)),
            jnp.where(self_long & (blocks >= LONG // BLK), 0, 1),
            jnp.where(self_long, 0, blocks // (SHORT_TOK // BLK)),
            jnp.where(self_long, 2, 1) + zero,
            jnp.where(self_long, 0, 2 * (blocks % 3)),
            jnp.where(self_long, jnp.where(blocks % 3 == 2, 0, 4), 2 * (blocks % 3) + 2),
            core + zero,
        ]
    ).astype(jnp.int32)
    lane = jnp.arange(128, dtype=jnp.int32) % HEAD_DIM
    freq = 10000.0 ** (-2.0 * (lane % (ROT // 2)).astype(single) / ROT)
    phase = position.astype(single)[:, None] * freq[None, :]
    turning = (lane < ROT)[None, :]
    cosine = jnp.where(turning, jnp.cos(phase), 1.0)
    sine = jnp.where(turning, jnp.sin(phase) * jnp.where(lane < ROT // 2, -1.0, 1.0)[None, :], 0.0)
    starts = start.reshape(1, TOTAL)

    tangent = cotangent * loss_mask.astype(bfloat)[:, None]
    tokens_out = outgoing(tokens)
    tangent_out = outgoing(tangent)
    tokens_out, late_up, late_down = lax.optimization_barrier((tokens_out, up_weight, down_weight))
    up_mixed = late_up.astype(bfloat).reshape(piece, D, fours).transpose(0, 2, 1)
    down_mixed = late_down.astype(bfloat).reshape(piece, fours, D)
    feed_weights = gather_all(
        jnp.concatenate([up_mixed.reshape(piece, FF), down_mixed.reshape(piece, FF)], 1)
    )
    tokens_in = swap_all(tokens_out)
    tokens_in, places, meta, cosine, sine, starts, tangent_out = lax.optimization_barrier(
        (tokens_in, places, meta, cosine, sine, starts, tangent_out)
    )
    own = arrange(tokens_in)
    other = exchange(own)
    kept, q, k, kt, v, context, logsum, context_mine, context_theirs = forward(
        meta,
        places,
        own,
        other,
        lines,
        first_all,
        project_add_half,
        cosine,
        sine,
        starts,
    )

    tangent_in = swap_all(after(tangent_out, context_mine))

    mine, theirs = context_mine, exchange(context_theirs)
    context_out = jnp.concatenate(
        [jnp.where(core == 0, mine, theirs), jnp.where(core == 0, theirs, mine)], -1
    )
    feed, lower_two, wide, up_add_grad, sums = feed_forward(
        after(tokens, context_out), tangent, lines, feed_weights, up_add
    )
    wide_sum = lax.psum_scatter(wide, "dp", scatter_dimension=0, tiled=True).astype(single)

    context_moved = send_back(context_out)

    upper_own = arrange(after(tangent_in, feed))
    upper_other = exchange(upper_own)
    lower_mine, lower_theirs, *project_parts = backward(
        meta,
        places,
        upper_own,
        upper_other,
        q,
        k,
        kt,
        v,
        starts,
        context,
        logsum,
        kept,
        lines,
        first_all,
        cosine,
        sine,
    )
    lower_sum = (
        lower_mine.astype(single) + exchange(lower_theirs).astype(single)
    ).astype(bfloat)
    upper_moved = send_back(lower_sum)
    output_half_grad, project_grad_half, project_add_half_grad, gain_one_grad, shift_one_grad = (
        project_parts
    )

    block_out = close(
        place_line, after(context_moved, lower_sum), first_all, lines, tokens, feed
    )

    def pair_up(one, two):
        return jnp.where(
            core == 0, jnp.concatenate([one, two], -1), jnp.concatenate([two, one], -1)
        )

    add_half = project_add_half_grad.reshape(3, HW)
    project_add_grad = pair_up(add_half, jnp.zeros_like(add_half)).reshape(devices, 3, piece)
    vectors = jnp.concatenate(
        [
            gain_one_grad,
            shift_one_grad,
            sums[:3],
            project_add_grad.transpose(1, 0, 2).reshape(3, D),
            up_add_grad.reshape(fours, D),
            jnp.zeros((4, D), single),
        ],
        0,
    )
    def over_chips(x):
        return x.reshape((4, across, across) + x.shape[1:])

    extra = vectors.reshape(16, devices, piece).transpose(1, 0, 2).reshape(devices, 1, 16 * piece)
    extra = jnp.pad(extra, ((0, 0), (0, 7), (0, D - 16 * piece))).astype(bfloat)
    empty = jnp.zeros_like(output_half_grad)
    output_grad = jnp.where(
        core == 0,
        jnp.concatenate([output_half_grad, empty], 0),
        jnp.concatenate([empty, output_half_grad], 0),
    )
    output_part = jnp.concatenate([output_grad.reshape(devices, piece, D), extra], 1)
    output_half = reduce_along(output_part.reshape(chips, 2, piece + 8, D), "core", 1)
    by_core = project_grad_half.reshape(3, chips, 2, piece, HW)
    for_me = lax.dynamic_index_in_dim(by_core, core, 2, keepdims=False)
    for_other = lax.dynamic_index_in_dim(by_core, 1 - core, 2, keepdims=False)
    projects = pair_up(for_me, exchange(for_other))
    narrow = over_chips(
        jnp.concatenate([projects[0], projects[1], projects[2], output_half], 1)
    )
    cut = narrow.shape[3] // 16 * 8
    one = reduce_along(narrow[..., :cut, :], "x", 2, late=block_out)
    two = reduce_along(narrow[..., cut:, :], "y", 1, late=block_out)
    one = reduce_along(one, "y", 1)
    two = reduce_along(two, "x", 1)
    wide_sum = wide_sum.reshape(piece, fours, 2, D)
    up_sum = wide_sum[:, :, 0].transpose(0, 2, 1).reshape(piece, FF)
    down_sum = wide_sum[:, :, 1].reshape(fours * piece, D)
    upper_moved, up_sum, down_sum = lax.optimization_barrier(
        (upper_moved, up_sum * scale, down_sum * scale)
    )
    tokens_grad = finish(place_line, upper_moved, lines, tokens, lower_two)
    narrow = reduce_along(jnp.concatenate([one, two], 1), "z", 0, single, tokens_grad) * scale
    project_sum = narrow[: 3 * piece].reshape(3, piece, D).transpose(1, 0, 2).reshape(piece, 3 * D)
    output_sum = narrow[3 * piece : 4 * piece]
    vector_sum = narrow[4 * piece, : 16 * piece].reshape(16, piece)
    return (
        block_out,
        tokens_grad,
        vector_sum[0],
        vector_sum[1],
        vector_sum[2],
        vector_sum[3],
        project_sum,
        vector_sum[5:8].reshape(3 * piece),
        output_sum,
        vector_sum[4],
        up_sum,
        vector_sum[8:12].T.reshape(fours * piece),
        down_sum,
        vector_sum[4],
    )


def solution(mesh):
    tall, flat = P("dp", None), P("dp")
    return jax.shard_map(
        body,
        mesh=mesh,
        in_specs=(
            tall,
            tall,
            flat,
            P(),
            P(),
            flat,
            flat,
            flat,
            flat,
            flat,
            flat,
            tall,
            flat,
            tall,
            flat,
            tall,
            flat,
            tall,
            flat,
        ),
        out_specs=(
            tall,
            tall,
            flat,
            flat,
            flat,
            flat,
            tall,
            flat,
            tall,
            flat,
            tall,
            flat,
            tall,
            flat,
        ),
        check_vma=False,
    )
```

```python
import functools
import math

import jax
import jax.numpy as jnp
from jax import lax
from jax.experimental import pallas as pl
from jax.experimental.pallas import tpu as pltpu
from jax.sharding import PartitionSpec as P

D = 768
HEADS = 12
HEAD_DIM = 64
ROT = 16
FF = 3072
LONG = 2048
SHORT_TOK = 1024
TOTAL = 3 * SHORT_TOK
BLK = 256
BLOCKS = TOTAL // BLK
WIDE = 512
STEPS = TOTAL // WIDE
NH = HEADS // 2
HW = NH * HEAD_DIM
PART = SHORT_TOK // 2
MIB = 2**20

epsilon = 1e-05
bfloat = jnp.bfloat16
single = jnp.float32


def dot(left, right):
    return jnp.dot(left, right, preferred_element_type=single)


def over_rows(left, right):
    return lax.dot_general(left, right, (((0,), (0,)), ((), ())), preferred_element_type=single)


def against(left, right):
    return lax.dot_general(left, right, (((1,), (1,)), ((), ())), preferred_element_type=single)


def norm_stats(values):
    mean = jnp.mean(values, -1, keepdims=True)
    centred = values - mean
    spread = jnp.mean(centred * centred, -1, keepdims=True)
    factor = lax.rsqrt(spread + epsilon)
    return (centred * factor, factor)


def lower_norm(upper, scaled, factor, gain):
    inner = upper * gain
    return factor * (
        inner
        - jnp.mean(inner, -1, keepdims=True)
        - scaled * jnp.mean(inner * scaled, -1, keepdims=True)
    )


def params(mib):
    return pltpu.CompilerParams(vmem_limit_bytes=mib * MIB)


def whole(shape):
    return pl.BlockSpec(shape, lambda *_: (0,) * len(shape))


def feed_kernel(
    tok, tan, lines, up, up_add, down, feed, lower, grad, g_up_add, sums, normed, act, slope
):
    step = pl.program_id(0)
    rows = tok.shape[0]
    chunk = rows // 2
    root = 1.0 / math.sqrt(2.0)
    dens = 1.0 / math.sqrt(2.0 * math.pi)

    @pl.when(step == 0)
    def _():
        def one(i, carry):
            r = pl.ds(pl.multiple_of(i * BLK, BLK), BLK)
            scaled, _ = norm_stats(tok[r, :].astype(single))
            normed[r, :] = (scaled * lines[2:3, :] + lines[3:4, :]).astype(bfloat)
            return carry

        lax.fori_loop(0, rows // BLK, one, 0)

    bias_sum = jnp.zeros((1, D), single)
    for i in range(2):
        r = pl.ds(i * chunk, chunk)
        hidden = dot(normed[r, :], up[...]) + up_add[0]
        above = against(tan[r, :], down[...])
        phi = 0.5 * (1.0 + lax.erf(hidden * root))
        active = (hidden * phi).astype(bfloat)
        sl = (above * (phi + hidden * (dens * jnp.exp(-0.5 * hidden * hidden)))).astype(bfloat)
        act[r, :] = active
        slope[r, :] = sl
        bias_sum = bias_sum + jnp.sum(sl.astype(single), 0, keepdims=True)
        part_feed = dot(active, down[...])
        part_lower = against(sl, up[...])

        feed[r, :] = jnp.where(step > 0, feed[r, :], 0.0) + part_feed
        lower[r, :] = jnp.where(step > 0, lower[r, :], 0.0) + part_lower

    g_up_add[0] = bias_sum
    grad[:, :D] = over_rows(normed[...], slope[...]).astype(bfloat)
    grad[:, D:] = over_rows(act[...], tan[...]).astype(bfloat)

    @pl.when(step == pl.num_programs(0) - 1)
    def _():
        def one(i, carry):
            r = pl.ds(pl.multiple_of(i * BLK, BLK), BLK)
            scaled, factor = norm_stats(tok[r, :].astype(single))
            upper, wide = lower[r, :], tan[r, :].astype(single)
            lower[r, :] = wide + lower_norm(upper, scaled, factor, lines[2:3, :])
            terms = (upper * scaled, upper, wide)
            return tuple(c + jnp.sum(t, 0, keepdims=True) for c, t in zip(carry, terms))

        parts = lax.fori_loop(0, rows // BLK, one, (jnp.zeros((1, D), single),) * 3)
        sums[...] = jnp.zeros_like(sums)
        for i in range(3):
            sums[i : i + 1, :] = parts[i]


def feed_forward(tok, tan, lines, weights, up_add):
    rows, count = tok.shape[0], FF // D
    wide = lambda where: pl.BlockSpec((D, D), lambda j: (0, where + j))
    one = lambda shape: pl.BlockSpec(shape, lambda j: (0, 0), pipeline_mode=pl.Buffered(1))
    line = pl.BlockSpec((1, 1, D), lambda j: (j, 0, 0))
    pair = pl.BlockSpec((D, 2 * D), lambda j: (0, j))
    return pl.pallas_call(
        feed_kernel,
        grid=(count,),
        in_specs=[one((rows, D)), one((rows, D)), one((16, D)), wide(0), line, wide(count)],
        out_specs=[one((rows, D)), one((rows, D)), pair, line, one((8, D))],
        out_shape=[
            jax.ShapeDtypeStruct((rows, D), single),
            jax.ShapeDtypeStruct((rows, D), single),
            jax.ShapeDtypeStruct((D, 2 * count * D), bfloat),
            jax.ShapeDtypeStruct((count, 1, D), single),
            jax.ShapeDtypeStruct((8, D), single),
        ],
        scratch_shapes=[
            pltpu.VMEM((rows, D), bfloat),
            pltpu.VMEM((rows, D), bfloat),
            pltpu.VMEM((rows, D), bfloat),
        ],
        compiler_params=params(60),
        cost_estimate=pl.CostEstimate(
            flops=12 * rows * D * D * count, bytes_accessed=count * 12 * MIB, transcendentals=2 * rows * D * count
        ),
        name="feed_forward",
    )(tok, tan, lines, weights, up_add, weights)


def gather_rows(meta, i, places, own, other, rows):
    spot = lax.broadcasted_iota(jnp.int32, (BLK, PART), 0) + i * BLK

    def part(k):
        mine = jnp.where(places[k] == spot, 1.0, 0.0).astype(bfloat)
        theirs = jnp.where(places[k + 3] == spot, 1.0, 0.0).astype(bfloat)
        return dot(mine, own[k]) + dot(theirs, other[k])

    low = meta[3, i]
    rows[...] = part(low)

    @pl.when(meta[4, i] > 1)
    def _():
        rows[...] += part(low + 1)


def column(line):
    return jnp.broadcast_to(line, (128, line.shape[1])).T[:, 0:1]


def return_rows(meta, at, places, values, mine, theirs, acc):
    b = lax.rem(at + 3, 6)
    acc[...] = jnp.zeros_like(acc)
    lane = lax.broadcasted_iota(jnp.int32, (PART, PART), 1)
    spots = column(places[b])

    def one(c, carry):
        hot = jnp.where(spots == lane + c * PART, 1.0, 0.0).astype(bfloat)
        r = pl.ds(pl.multiple_of(c * PART, PART), PART)
        acc[...] += dot(hot, values[r, :])
        return carry

    lax.fori_loop(meta[5, b], meta[6, b], one, 0)

    @pl.when(at < 3)
    def _():
        theirs[0] = acc[...].astype(bfloat)

    @pl.when(at >= 3)
    def _():
        mine[0] = acc[...].astype(bfloat)


def turn_lanes(values, cosine, sine):
    lane = lax.broadcasted_iota(jnp.int32, values.shape, 1)
    swapped = jnp.where(
        (lane & (ROT - 1)) < ROT // 2, pltpu.roll(values, 128 - ROT // 2, 1), pltpu.roll(values, ROT // 2, 1)
    )
    return values * cosine + swapped * sine


def of_head(values, h):
    lane = lax.broadcasted_iota(jnp.int32, values.shape, 1)
    return jnp.where((lane < HEAD_DIM) == (h % 2 == 0), values, jnp.zeros_like(values))


def lanes_of(h):
    return slice((h // 2) * 128, (h // 2) * 128 + 128)


def rows_of(h):
    return slice(h * HEAD_DIM, (h + 1) * HEAD_DIM)


def block_of(j):
    return pl.ds(pl.multiple_of(j * BLK, BLK), BLK)


def allowed_of(start, j, diagonal):
    row = lax.broadcasted_iota(jnp.int32, (BLK, BLK), 0)
    allowed = row + j * BLK >= start[...]
    if diagonal:
        allowed &= row <= lax.broadcasted_iota(jnp.int32, (BLK, BLK), 1)
    return allowed


def over_blocks(meta, i, step):
    def masked(j, carry):
        step(j, True, False)
        return carry

    def plain(j, carry):
        step(j, False, False)
        return carry

    lax.fori_loop(meta[0, i], meta[1, i], masked, 0)
    lax.fori_loop(meta[1, i], i, plain, 0)
    step(i, True, True)


def forward_kernel(
    meta,
    places,
    own,
    other,
    lines,
    weight_q,
    weight_k,
    weight_v,
    add,
    cosine,
    sine,
    start,
    kept,
    q,
    k,
    kt,
    v,
    context,
    logsum,
    mine,
    theirs,
    rows,
    keys,
    values,
    score,
    peak,
    total,
    acc,
    done,
    back_acc,
):
    step_at = pl.program_id(0)
    i = jnp.minimum(step_at, BLOCKS - 1)
    here = block_of(i)
    live = (step_at < BLOCKS) & (meta[2, i] > 0)

    @pl.when(live)
    def _():
        gather_rows(meta, i, places, own, other, rows)
        scaled, _ = norm_stats(rows[...])
        n = (scaled * lines[0:1, :] + lines[1:2, :]).astype(bfloat)
        kept[...] = rows[...].astype(bfloat)
        for s, weight in enumerate((weight_q, weight_k, weight_v)):
            mixed = dot(n, weight[...]) + add[:, s * HW : (s + 1) * HW]
            if s < 2:
                mixed = jnp.concatenate(
                    [
                        turn_lanes(mixed[:, p : p + 128], cosine[...], sine[...])
                        for p in range(0, HW, 128)
                    ],
                    1,
                )
            narrow = mixed.astype(bfloat)
            if s == 0:
                q[...] = narrow * HEAD_DIM ** (-0.5)
            elif s == 1:
                k[...] = narrow
                keys[here, :] = narrow
                kt[...] = narrow.T
            else:
                v[...] = narrow
                values[:, here] = narrow.T

        first = meta[0, i]
        queries = [of_head(q[:, lanes_of(h)], h) for h in range(NH)]
        peak[...] = jnp.full(peak.shape, -jnp.inf, single)

        def step(j, masked, diagonal):
            if masked:
                allowed = allowed_of(start, j, diagonal)
            for h in range(NH):
                s = against(keys[block_of(j), lanes_of(h)], queries[h])
                if masked:
                    s = jnp.where(allowed, s, -jnp.inf)
                score[h, block_of(j - first), :] = s
                peak[h] = jnp.maximum(peak[h], jnp.max(s.reshape(BLK // 8, 8, BLK), 0))

        over_blocks(meta, i, step)
        tops = [jnp.max(peak[h], 0, keepdims=True) for h in range(NH)]
        total[...] = jnp.zeros_like(total)
        acc[...] = jnp.zeros_like(acc)

        def gain(j, carry):
            for h in range(NH):
                p = jnp.exp(score[h, block_of(j - first), :] - tops[h])
                total[h] += jnp.sum(p.reshape(BLK // 8, 8, BLK), 0)
                acc[rows_of(h), :] += dot(values[rows_of(h), block_of(j)], p.astype(bfloat))
            return carry

        lax.fori_loop(first, i + 1, gain, 0)
        for h in range(NH):
            whole_sum = jnp.sum(total[h], 0, keepdims=True)
            acc[rows_of(h), :] = acc[rows_of(h), :] / whole_sum
            logsum[h : h + 1, :] = tops[h] + jnp.log(whole_sum)
        turned = acc[...].T
        context[...] = turned
        done[here, :] = turned.astype(bfloat)

    @pl.when(step_at >= BLOCKS)
    def _():
        return_rows(meta, jnp.maximum(step_at - BLOCKS, 0), places, done, mine, theirs, back_acc)


def columns():
    return [
        pl.BlockSpec((D, HW), lambda i, m, s=s: (0, 2 * s + m[7, 0]), pipeline_mode=pl.Buffered(1))
        for s in range(3)
    ]


def held(*shape):
    return pl.BlockSpec(shape, lambda i, m: (0,) * len(shape), pipeline_mode=pl.Buffered(1))


def tall_at(width):
    return pl.BlockSpec((BLK, width), lambda i, m: (jnp.minimum(i, m[8, 0]), 0))


def flat_at(height):
    return pl.BlockSpec((height, BLK), lambda i, m: (0, jnp.minimum(i, m[8, 0])))


def wide_at(width):
    return pl.BlockSpec((WIDE, width), lambda i, m: (jnp.clip(i - BLOCKS, 0, m[8, 0] // 2), 0))


def parts_at(first, width):
    return [
        pl.BlockSpec((1, PART, width), lambda i, m, f=f: (jnp.clip(i - f, 0, 2), 0, 0))
        for f in (first + 3, first)
    ]


def forward(meta, places, own, other, lines, weight, add, cosine, sine, start):
    out = lambda *shape: jax.ShapeDtypeStruct(shape, bfloat)
    return pl.pallas_call(
        forward_kernel,
        grid_spec=pltpu.PrefetchScalarGridSpec(
            num_scalar_prefetch=1,
            grid=(BLOCKS + 6,),
            in_specs=[
                held(6, 1, PART),
                held(3, PART, D),
                held(3, PART, D),
                held(16, D),
                *columns(),
                held(1, 3 * HW),
                tall_at(128),
                tall_at(128),
                flat_at(1),
            ],
            out_specs=[
                tall_at(D),
                tall_at(HW),
                tall_at(HW),
                flat_at(HW),
                tall_at(HW),
                tall_at(HW),
                flat_at(8),
                *parts_at(BLOCKS, HW),
            ],
            scratch_shapes=[
                pltpu.VMEM((BLK, D), single),
                pltpu.VMEM((TOTAL, HW), bfloat),
                pltpu.VMEM((HW, TOTAL), bfloat),
                pltpu.VMEM((NH, LONG, BLK), single),
                pltpu.VMEM((NH, 8, BLK), single),
                pltpu.VMEM((NH, 8, BLK), single),
                pltpu.VMEM((HW, BLK), single),
                pltpu.VMEM((TOTAL, HW), bfloat),
                pltpu.VMEM((PART, HW), single),
            ],
        ),
        out_shape=[
            out(TOTAL, D),
            out(TOTAL, HW),
            out(TOTAL, HW),
            out(HW, TOTAL),
            out(TOTAL, HW),
            jax.ShapeDtypeStruct((TOTAL, HW), single),
            jax.ShapeDtypeStruct((8, TOTAL), single),
            out(3, PART, HW),
            out(3, PART, HW),
        ],
        compiler_params=params(60),
        cost_estimate=pl.CostEstimate(
            flops=75 * 10**9, bytes_accessed=40 * MIB, transcendentals=NH * LONG * LONG // 2
        ),
        name="forward",
    )(meta, places, own, other, lines, weight, weight, weight, add, cosine, sine, start)


def backward_kernel(
    meta,
    places,
    own,
    other,
    weight_out,
    q,
    k,
    kt,
    v,
    start,
    context,
    logsum,
    kept,
    lines,
    weight_q,
    weight_k,
    weight_v,
    cosine,
    sine,
    mine,
    theirs,
    g_out,
    g_weight,
    g_add,
    g_gain,
    g_shift,
    rows,
    upper,
    dq,
    dk,
    dv,
    dqt,
    probs,
    slopes,
    out_acc,
    g_acc,
    lower,
    back_acc,
):
    step_at = pl.program_id(0)
    i = jnp.minimum(step_at, BLOCKS - 1)
    b = jnp.clip(step_at - BLOCKS, 0, STEPS - 1)

    @pl.when(step_at == 0)
    def _():
        for ref in (out_acc, g_acc, g_add, g_gain, g_shift):
            ref[...] = jnp.zeros_like(ref)

    @pl.when((step_at < BLOCKS) & (meta[2, i] > 0))
    def _():
        gather_rows(meta, i, places, own, other, rows)
        tangent = rows[...].astype(bfloat)
        upper[...] = against(tangent, weight_out[...]).astype(bfloat)
        out_acc[...] += over_rows(context[...].astype(bfloat), tangent)
        queries = [of_head(q[:, lanes_of(h)], h) for h in range(NH)]
        uppers = [of_head(upper[:, lanes_of(h)], h) for h in range(NH)]
        both = (upper[...].astype(single) * context[...]).T
        delta = [jnp.sum(both[rows_of(h), :], 0, keepdims=True) for h in range(NH)]
        dqt[...] = jnp.zeros_like(dqt)

        def step(j, masked, diagonal):
            r = block_of(j)
            if masked:
                allowed = allowed_of(start, j, diagonal)
            for h in range(NH):
                s = against(k[r, lanes_of(h)], queries[h])
                p = jnp.exp(s - logsum[h : h + 1, :])
                if masked:
                    p = jnp.where(allowed, p, 0.0)
                dp = against(v[r, lanes_of(h)], uppers[h])
                c = slice((h % 2) * BLK, (h % 2) * BLK + BLK)
                probs[h // 2, :, c] = p.astype(bfloat)
                slopes[h // 2, :, c] = (p * (dp - delta[h])).astype(bfloat)
            for g in range(NH // 2):
                c = slice(g * 128, g * 128 + 128)
                part_v = dot(probs[g], jnp.concatenate(uppers[2 * g : 2 * g + 2], 0))
                part_k = dot(slopes[g], jnp.concatenate(queries[2 * g : 2 * g + 2], 0))
                if diagonal:
                    dv[r, c] = part_v
                    dk[r, c] = part_k
                else:
                    dv[r, c] += part_v
                    dk[r, c] += part_k
                for h in (2 * g, 2 * g + 1):
                    e = slice((h % 2) * BLK, (h % 2) * BLK + BLK)
                    dqt[rows_of(h), :] += dot(kt[rows_of(h), r], slopes[g, :, e])

        over_blocks(meta, i, step)
        dq[block_of(i), :] = dqt[...].T * HEAD_DIM ** (-0.5)

    @pl.when((step_at >= BLOCKS) & (step_at < BLOCKS + STEPS) & (meta[2, 2 * b] > 0))
    def _():
        r = pl.ds(pl.multiple_of(b * WIDE, WIDE), WIDE)
        turned = []
        for ref in (dq, dk):
            for p in range(0, HW, 128):
                turned.append(turn_lanes(ref[r, p : p + 128], cosine[...], -sine[...]))
        turned.append(dv[r, :])
        mixed = jnp.concatenate(turned, 1).astype(bfloat)
        g_add[...] += jnp.sum(mixed.astype(single), 0, keepdims=True)
        up = (
            against(mixed[:, :HW], weight_q[...])
            + against(mixed[:, HW : 2 * HW], weight_k[...])
            + against(mixed[:, 2 * HW :], weight_v[...])
        )
        lower[r, :] = up.astype(bfloat)
        scaled, _ = norm_stats(kept[...].astype(single))
        g_gain[...] += jnp.sum(up * scaled, 0, keepdims=True)
        g_shift[...] += jnp.sum(up, 0, keepdims=True)
        normed = (scaled * lines[0:1, :] + lines[1:2, :]).astype(bfloat)
        g_acc[...] += over_rows(normed, mixed)

    @pl.when(step_at == BLOCKS + STEPS)
    def _():
        g_out[...] = out_acc[...].astype(bfloat)
        for s in range(3):
            g_weight[s] = g_acc[:, s * HW : (s + 1) * HW].astype(bfloat)

    @pl.when(step_at >= BLOCKS + STEPS)
    def _():
        return_rows(
            meta, jnp.maximum(step_at - BLOCKS - STEPS, 0), places, lower, mine, theirs, back_acc
        )


def backward(
    meta, places, own, other, q, k, kt, v, start, context, logsum, kept, lines, weight, cosine, sine
):
    return pl.pallas_call(
        backward_kernel,
        grid_spec=pltpu.PrefetchScalarGridSpec(
            num_scalar_prefetch=1,
            grid=(BLOCKS + STEPS + 6,),
            in_specs=[
                held(6, 1, PART),
                held(3, PART, D),
                held(3, PART, D),
                pl.BlockSpec((HW, D), lambda i, m: (m[7, 0], 3), pipeline_mode=pl.Buffered(1)),
                tall_at(HW),
                held(TOTAL, HW),
                held(HW, TOTAL),
                held(TOTAL, HW),
                flat_at(1),
                tall_at(HW),
                flat_at(8),
                wide_at(D),
                held(16, D),
                *columns(),
                wide_at(128),
                wide_at(128),
            ],
            out_specs=[
                *parts_at(BLOCKS + STEPS, D),
                held(HW, D),
                held(3, D, HW),
                held(1, 3 * HW),
                held(1, D),
                held(1, D),
            ],
            scratch_shapes=[
                pltpu.VMEM((BLK, D), single),
                pltpu.VMEM((BLK, HW), bfloat),
                pltpu.VMEM((TOTAL, HW), single),
                pltpu.VMEM((TOTAL, HW), single),
                pltpu.VMEM((TOTAL, HW), single),
                pltpu.VMEM((HW, BLK), single),
                pltpu.VMEM((NH // 2, BLK, 2 * BLK), bfloat),
                pltpu.VMEM((NH // 2, BLK, 2 * BLK), bfloat),
                pltpu.VMEM((HW, D), single),
                pltpu.VMEM((D, 3 * HW), single),
                pltpu.VMEM((TOTAL, D), bfloat),
                pltpu.VMEM((PART, D), single),
            ],
        ),
        out_shape=[
            jax.ShapeDtypeStruct((3, PART, D), bfloat),
            jax.ShapeDtypeStruct((3, PART, D), bfloat),
            jax.ShapeDtypeStruct((HW, D), bfloat),
            jax.ShapeDtypeStruct((3, D, HW), bfloat),
            jax.ShapeDtypeStruct((1, 3 * HW), single),
            jax.ShapeDtypeStruct((1, D), single),
            jax.ShapeDtypeStruct((1, D), single),
        ],
        compiler_params=params(60),
        cost_estimate=pl.CostEstimate(
            flops=90 * 10**9, bytes_accessed=40 * MIB, transcendentals=NH * LONG * LONG // 2
        ),
        name="backward",
    )(
        meta,
        places,
        own,
        other,
        weight,
        q,
        k,
        kt,
        v,
        start,
        context,
        logsum,
        kept,
        lines,
        weight,
        weight,
        weight,
        cosine,
        sine,
    )


def placed_rows(place, moved):
    lane = lax.broadcasted_iota(jnp.int32, (BLK, moved.shape[0]), 1)
    return dot(jnp.where(column(place[...]) == lane, 1.0, 0.0).astype(bfloat), moved[...])


def close_kernel(place, moved, weight, lines, tok, feed, out):
    context = placed_rows(place, moved).astype(bfloat)
    attended = dot(context, weight[...]) + lines[4:5, :]
    out[...] = (tok[...].astype(single) + attended + (feed[...] + lines[5:6, :])).astype(bfloat)


def close(place, moved, weights, lines, tok, feed):
    rows = tok.shape[0]
    tall = lambda width: pl.BlockSpec((BLK, width), lambda i: (i, 0))
    return pl.pallas_call(
        close_kernel,
        grid=(rows // BLK,),
        in_specs=[
            pl.BlockSpec((1, BLK), lambda i: (0, i)),
            whole(moved.shape),
            pl.BlockSpec((D, D), lambda i: (0, 3)),
            whole((16, D)),
            tall(D),
            tall(D),
        ],
        out_specs=tall(D),
        out_shape=jax.ShapeDtypeStruct((rows, D), bfloat),
        compiler_params=params(60),
        cost_estimate=pl.CostEstimate(
            flops=12 * 10**9, bytes_accessed=12 * MIB, transcendentals=0
        ),
        name="close",
    )(place, moved, weights, lines, tok, feed)


def finish_kernel(place, moved, lines, tok, lower, out):
    scaled, factor = norm_stats(tok[...].astype(single))
    upper = placed_rows(place, moved)
    out[...] = (lower[...] + lower_norm(upper, scaled, factor, lines[0:1, :])).astype(bfloat)


def finish(place, moved, lines, tok, lower):
    rows = tok.shape[0]
    tall = lambda width: pl.BlockSpec((BLK, width), lambda i: (i, 0))
    return pl.pallas_call(
        finish_kernel,
        grid=(rows // BLK,),
        in_specs=[
            pl.BlockSpec((1, BLK), lambda i: (0, i)),
            whole(moved.shape),
            whole((16, D)),
            tall(D),
            tall(D),
        ],
        out_specs=tall(D),
        out_shape=jax.ShapeDtypeStruct((rows, D), bfloat),
        compiler_params=params(60),
        cost_estimate=pl.CostEstimate(
            flops=2 * rows * D * moved.shape[0], bytes_accessed=12 * MIB, transcendentals=0
        ),
        name="finish",
    )(place, moved, lines, tok, lower)


def gather_all(x):
    return lax.all_gather(x, "dp", axis=0, tiled=True)


def body(
    tokens,
    cotangent,
    loss_mask,
    bucket_perm,
    short_lengths,
    row_owner,
    row_slot,
    first_gain,
    first_shift,
    second_gain,
    second_shift,
    project_weight,
    project_bias,
    output_weight,
    output_bias,
    up_weight,
    up_bias,
    down_weight,
    down_bias,
):
    devices = lax.axis_size("dp")
    me = lax.axis_index("dp")
    core = me % 2
    chip = me // 2
    rows = tokens.shape[0]
    share = LONG // devices // 4
    room = 3 * share
    long_count = devices // 4
    swap = [(i, i ^ 1) for i in range(devices)]

    def exchange(x):
        return lax.ppermute(x, "dp", swap)

    chips = devices // 2
    across = math.isqrt(chips // 4)
    sizes = {"core": 2, "x": across, "y": across, "z": 4}
    strides = {"core": 1, "x": 2, "y": 2 * across, "z": 2 * across * across}

    def shifted(x, name, shift):
        n, stride = sizes[name], strides[name]
        hop = []
        for d in range(devices):
            c = (d // stride) % n
            hop.append((d, d + ((c + shift) % n - c) * stride))
        return lax.ppermute(x, "dp", hop)

    def after(x, *others):
        return lax.optimization_barrier((x, *others))[0]

    def reduce_along(x, name, dim, kind=bfloat, late=None):
        n = sizes[name]
        at = (me // strides[name]) % n
        total = lax.dynamic_index_in_dim(x, at, dim, keepdims=False).astype(single)
        for shift in range(1, n):
            sent = lax.dynamic_index_in_dim(x, (at + shift) % n, dim, keepdims=False)
            got = shifted(sent, name, shift)
            total = total + (got if late is None else after(got, late)).astype(single)
        return total.astype(kind)

    piece = D // devices
    fours = FF // D
    count = jnp.sum(loss_mask)
    count_column = jnp.where(
        jnp.arange(piece) == 0, count // 256, jnp.where(jnp.arange(piece) == 1, count % 256, 0)
    )
    small = jnp.concatenate(
        [
            jnp.stack([first_gain, first_shift, second_gain, second_shift, output_bias, down_bias], 1),
            project_bias.reshape(3, piece).T,
            up_bias.reshape(piece, fours),
            count_column[:, None].astype(single),
        ],
        1,
    )
    small = jnp.pad(small, ((0, 0), (0, 128 - small.shape[1])))
    spread = jnp.arange(devices, dtype=jnp.int32)
    bucket = jnp.sum(jnp.where(bucket_perm[None, :] == row_owner[:, None], spread[None, :], 0), -1)
    hot = (row_owner[:, None] == spread[None, :]).astype(bfloat)
    line = jnp.arange(rows, dtype=jnp.int32)
    before = (line[None, :] < line[:, None]).astype(bfloat)
    rank = jnp.sum(dot(before, hot) * hot.astype(single), -1).astype(jnp.int32)
    is_long = bucket < long_count
    short = bucket - long_count
    third = jnp.where(is_long, 0, short % 3)
    to_chip = jnp.where(is_long, 2 * bucket, 2 * (short // 3) + 1)
    held = jnp.where(is_long, 2 * share, share)
    to_core = rank // held
    place = (2 * to_chip + to_core) * room + third * share + rank % held
    slot = third * SHORT_TOK + row_slot
    spots = jnp.arange(devices * room, dtype=jnp.int32)
    slot_at = jnp.sum(
        jnp.where(place[None, :] == spots[:, None], slot[None, :] + 1, 0), -1
    ) - 1
    slot_code = jnp.concatenate([(slot_at + 1) // 256, (slot_at + 1) % 256])
    slot_code = slot_code.astype(single).reshape(piece, 2 * devices * room // piece)
    first_all = gather_all(
        jnp.concatenate([project_weight, output_weight, small, slot_code], 1).astype(bfloat)
    )
    lines = first_all[:, 4 * D : 4 * D + 16].astype(single).T
    project_add = lines[6:9].reshape(3, devices, piece).transpose(1, 0, 2).reshape(1, 3, 2, HW)
    project_add_half = lax.dynamic_index_in_dim(project_add, core, 2, keepdims=False).reshape(
        1, 3 * HW
    )
    up_add = lines[9:13].reshape(fours, 1, D)
    counts = lines[13].reshape(devices, piece)
    scale = lax.rsqrt(jnp.sum(counts[:, 0]) * 256.0 + jnp.sum(counts[:, 1]))

    sender = (place[None, :] == spots[:, None]).astype(bfloat)
    place_line = place[None]

    def swap_all(x):
        return lax.all_to_all(x, "dp", split_axis=0, concat_axis=0, tiled=True)

    def outgoing(x):
        return dot(sender, x).astype(bfloat).reshape(devices, room, D)

    def arrange(moved):
        return moved.reshape(devices, 3, share, D).transpose(1, 0, 2, 3).reshape(3, PART, D)

    def send_back(x):
        moved = x.reshape(3, devices, share, D).transpose(1, 0, 2, 3).reshape(devices, room, D)
        return swap_all(moved).reshape(devices * room, D)

    code = first_all[:, 4 * D + 128 :].reshape(devices, 2, chips, 2 * room)
    code = lax.dynamic_index_in_dim(code, chip, 2, keepdims=False).astype(jnp.int32)
    slot_recv = (code[:, 0] * 256 + code[:, 1] - 1).reshape(devices, 2, 3, share)
    slot_recv = slot_recv.transpose(1, 2, 0, 3).reshape(2, 3, PART)
    slot_recv = jnp.where(core == 0, slot_recv, slot_recv[::-1])
    places = slot_recv.reshape(6, 1, PART)

    self_long = chip % 2 == 0
    lengths = lax.dynamic_slice_in_dim(short_lengths, 3 * (chip // 2), 3, 0)
    ends = jnp.cumsum(lengths, -1)
    at = jnp.arange(TOTAL, dtype=jnp.int32).reshape(3, SHORT_TOK)
    inside = jnp.arange(SHORT_TOK, dtype=jnp.int32)
    begun = jnp.max(
        jnp.where(ends[:, None, :] <= inside[None, :, None], ends[:, None, :], 0), -1
    )
    start = jnp.where(self_long, 0, begun + at - inside[None, :]).reshape(TOTAL)
    position = jnp.arange(TOTAL, dtype=jnp.int32) - start
    blocks = jnp.arange(TOTAL // BLK, dtype=jnp.int32)
    low_start = start[::BLK] // BLK
    high_start = (start[BLK - 1 :: BLK] + BLK - 1) // BLK
    zero = jnp.zeros_like(blocks)
    meta = jnp.stack(
        [
            low_start,
            jnp.minimum(blocks, jnp.maximum(low_start, high_start)),
            jnp.where(self_long & (blocks >= LONG // BLK), 0, 1),
            jnp.where(self_long, 0, blocks // (SHORT_TOK // BLK)),
            jnp.where(self_long, 2, 1) + zero,
            jnp.where(self_long, 0, 2 * (blocks % 3)),
            jnp.where(self_long, jnp.where(blocks % 3 == 2, 0, 4), 2 * (blocks % 3) + 2),
            core + zero,
            jnp.where(self_long, LONG // BLK, BLOCKS) - 1 + zero,
        ]
    ).astype(jnp.int32)
    lane = jnp.arange(128, dtype=jnp.int32) % HEAD_DIM
    freq = 10000.0 ** (-2.0 * (lane % (ROT // 2)).astype(single) / ROT)
    phase = position.astype(single)[:, None] * freq[None, :]
    turning = (lane < ROT)[None, :]
    cosine = jnp.where(turning, jnp.cos(phase), 1.0)
    sine = jnp.where(turning, jnp.sin(phase) * jnp.where(lane < ROT // 2, -1.0, 1.0)[None, :], 0.0)
    starts = start.reshape(1, TOTAL)

    tangent = cotangent * loss_mask.astype(bfloat)[:, None]
    tokens_out = outgoing(tokens)
    tangent_out = outgoing(tangent)
    tokens_out, late_up, late_down = lax.optimization_barrier((tokens_out, up_weight, down_weight))
    up_mixed = late_up.astype(bfloat).reshape(piece, D, fours).transpose(0, 2, 1)
    down_mixed = late_down.astype(bfloat).reshape(piece, fours, D)
    feed_weights = gather_all(
        jnp.concatenate([up_mixed.reshape(piece, FF), down_mixed.reshape(piece, FF)], 1)
    )
    tokens_in = swap_all(tokens_out)
    tokens_in, places, meta, cosine, sine, starts, tangent_out = lax.optimization_barrier(
        (tokens_in, places, meta, cosine, sine, starts, tangent_out)
    )
    own = arrange(tokens_in)
    other = exchange(own)
    kept, q, k, kt, v, context, logsum, context_mine, context_theirs = forward(
        meta,
        places,
        own,
        other,
        lines,
        first_all,
        project_add_half,
        cosine,
        sine,
        starts,
    )

    tangent_in = swap_all(after(tangent_out, context_mine))

    mine, theirs = context_mine, exchange(context_theirs)
    context_out = jnp.concatenate(
        [jnp.where(core == 0, mine, theirs), jnp.where(core == 0, theirs, mine)], -1
    )
    feed, lower_two, wide, up_add_grad, sums = feed_forward(
        after(tokens, context_out), tangent, lines, feed_weights, up_add
    )
    wide_sum = lax.psum_scatter(wide, "dp", scatter_dimension=0, tiled=True).astype(single)

    context_moved = send_back(context_out)

    upper_own = arrange(after(tangent_in, feed))
    upper_other = exchange(upper_own)
    lower_mine, lower_theirs, *project_parts = backward(
        meta,
        places,
        upper_own,
        upper_other,
        q,
        k,
        kt,
        v,
        starts,
        context,
        logsum,
        kept,
        lines,
        first_all,
        cosine,
        sine,
    )
    lower_sum = (
        lower_mine.astype(single) + exchange(lower_theirs).astype(single)
    ).astype(bfloat)
    upper_moved = send_back(lower_sum)
    output_half_grad, project_grad_half, project_add_half_grad, gain_one_grad, shift_one_grad = (
        project_parts
    )

    block_out = close(
        place_line, after(context_moved, lower_sum), first_all, lines, tokens, feed
    )

    def pair_up(one, two):
        return jnp.where(
            core == 0, jnp.concatenate([one, two], -1), jnp.concatenate([two, one], -1)
        )

    add_half = project_add_half_grad.reshape(3, HW)
    project_add_grad = pair_up(add_half, jnp.zeros_like(add_half)).reshape(devices, 3, piece)
    vectors = jnp.concatenate(
        [
            gain_one_grad,
            shift_one_grad,
            sums[:3],
            project_add_grad.transpose(1, 0, 2).reshape(3, D),
            up_add_grad.reshape(fours, D),
            jnp.zeros((4, D), single),
        ],
        0,
    )
    def over_chips(x):
        return x.reshape((4, across, across) + x.shape[1:])

    extra = vectors.reshape(16, devices, piece).transpose(1, 0, 2).reshape(devices, 1, 16 * piece)
    extra = jnp.pad(extra, ((0, 0), (0, 7), (0, D - 16 * piece))).astype(bfloat)
    empty = jnp.zeros_like(output_half_grad)
    output_grad = jnp.where(
        core == 0,
        jnp.concatenate([output_half_grad, empty], 0),
        jnp.concatenate([empty, output_half_grad], 0),
    )
    output_part = jnp.concatenate([output_grad.reshape(devices, piece, D), extra], 1)
    output_half = reduce_along(output_part.reshape(chips, 2, piece + 8, D), "core", 1)
    by_core = project_grad_half.reshape(3, chips, 2, piece, HW)
    for_me = lax.dynamic_index_in_dim(by_core, core, 2, keepdims=False)
    for_other = lax.dynamic_index_in_dim(by_core, 1 - core, 2, keepdims=False)
    projects = pair_up(for_me, exchange(for_other))
    narrow = over_chips(
        jnp.concatenate([projects[0], projects[1], projects[2], output_half], 1)
    )
    cut = narrow.shape[3] // 16 * 8
    one = reduce_along(narrow[..., :cut, :], "x", 2, late=block_out)
    two = reduce_along(narrow[..., cut:, :], "y", 1, late=block_out)
    one = reduce_along(one, "y", 1)
    two = reduce_along(two, "x", 1)
    wide_sum = wide_sum.reshape(piece, fours, 2, D)
    up_sum = wide_sum[:, :, 0].transpose(0, 2, 1).reshape(piece, FF)
    down_sum = wide_sum[:, :, 1].reshape(fours * piece, D)
    upper_moved, up_sum, down_sum = lax.optimization_barrier(
        (upper_moved, up_sum * scale, down_sum * scale)
    )
    tokens_grad = finish(place_line, upper_moved, lines, tokens, lower_two)
    narrow = reduce_along(jnp.concatenate([one, two], 1), "z", 0, single, tokens_grad) * scale
    project_sum = narrow[: 3 * piece].reshape(3, piece, D).transpose(1, 0, 2).reshape(piece, 3 * D)
    output_sum = narrow[3 * piece : 4 * piece]
    vector_sum = narrow[4 * piece, : 16 * piece].reshape(16, piece)
    return (
        block_out,
        tokens_grad,
        vector_sum[0],
        vector_sum[1],
        vector_sum[2],
        vector_sum[3],
        project_sum,
        vector_sum[5:8].reshape(3 * piece),
        output_sum,
        vector_sum[4],
        up_sum,
        vector_sum[8:12].T.reshape(fours * piece),
        down_sum,
        vector_sum[4],
    )


def solution(mesh):
    tall, flat = P("dp", None), P("dp")
    return jax.shard_map(
        body,
        mesh=mesh,
        in_specs=(
            tall,
            tall,
            flat,
            P(),
            P(),
            flat,
            flat,
            flat,
            flat,
            flat,
            flat,
            tall,
            flat,
            tall,
            flat,
            tall,
            flat,
            tall,
            flat,
        ),
        out_specs=(
            tall,
            tall,
            flat,
            flat,
            flat,
            flat,
            tall,
            flat,
            tall,
            flat,
            tall,
            flat,
            tall,
            flat,
        ),
        check_vma=False,
    )
```

```python
import functools
import math

import jax
import jax.numpy as jnp
from jax import lax
from jax.experimental import pallas as pl
from jax.experimental.pallas import tpu as pltpu
from jax.sharding import PartitionSpec as P

D = 768
HEADS = 12
HEAD_DIM = 64
ROT = 16
FF = 3072
LONG = 2048
SHORT_TOK = 1024
TOTAL = 3 * SHORT_TOK
BLK = 256
BLOCKS = TOTAL // BLK
WIDE = 512
STEPS = TOTAL // WIDE
NH = HEADS // 2
HW = NH * HEAD_DIM
PART = SHORT_TOK // 2
MIB = 2**20

epsilon = 1e-05
bfloat = jnp.bfloat16
single = jnp.float32


def dot(left, right):
    return jnp.dot(left, right, preferred_element_type=single)


def over_rows(left, right):
    return lax.dot_general(left, right, (((0,), (0,)), ((), ())), preferred_element_type=single)


def against(left, right):
    return lax.dot_general(left, right, (((1,), (1,)), ((), ())), preferred_element_type=single)


def norm_stats(values):
    mean = jnp.mean(values, -1, keepdims=True)
    centred = values - mean
    spread = jnp.mean(centred * centred, -1, keepdims=True)
    factor = lax.rsqrt(spread + epsilon)
    return (centred * factor, factor)


def lower_norm(upper, scaled, factor, gain):
    inner = upper * gain
    return factor * (
        inner
        - jnp.mean(inner, -1, keepdims=True)
        - scaled * jnp.mean(inner * scaled, -1, keepdims=True)
    )


def params(mib):
    return pltpu.CompilerParams(vmem_limit_bytes=mib * MIB)


def whole(shape):
    return pl.BlockSpec(shape, lambda *_: (0,) * len(shape))


def feed_kernel(
    tok, tan, lines, up, up_add, down, feed, lower, grad, g_up_add, sums, normed, act, slope
):
    step = pl.program_id(0)
    rows = tok.shape[0]
    chunk = rows // 2
    root = 1.0 / math.sqrt(2.0)
    dens = 1.0 / math.sqrt(2.0 * math.pi)

    @pl.when(step == 0)
    def _():
        def one(i, carry):
            r = pl.ds(pl.multiple_of(i * BLK, BLK), BLK)
            scaled, _ = norm_stats(tok[r, :].astype(single))
            normed[r, :] = (scaled * lines[2:3, :] + lines[3:4, :]).astype(bfloat)
            return carry

        lax.fori_loop(0, rows // BLK, one, 0)

    bias_sum = jnp.zeros((1, D), single)
    for i in range(2):
        r = pl.ds(i * chunk, chunk)
        hidden = dot(normed[r, :], up[...]) + up_add[0]
        above = against(tan[r, :], down[...])
        phi = 0.5 * (1.0 + lax.erf(hidden * root))
        active = (hidden * phi).astype(bfloat)
        sl = (above * (phi + hidden * (dens * jnp.exp(-0.5 * hidden * hidden)))).astype(bfloat)
        act[r, :] = active
        slope[r, :] = sl
        bias_sum = bias_sum + jnp.sum(sl.astype(single), 0, keepdims=True)
        part_feed = dot(active, down[...])
        part_lower = against(sl, up[...])

        feed[r, :] = jnp.where(step > 0, feed[r, :], 0.0) + part_feed
        lower[r, :] = jnp.where(step > 0, lower[r, :], 0.0) + part_lower

    g_up_add[0] = bias_sum
    grad[:, :D] = over_rows(normed[...], slope[...]).astype(bfloat)
    grad[:, D:] = over_rows(act[...], tan[...]).astype(bfloat)

    @pl.when(step == pl.num_programs(0) - 1)
    def _():
        def one(i, carry):
            r = pl.ds(pl.multiple_of(i * BLK, BLK), BLK)
            scaled, _ = norm_stats(tok[r, :].astype(single))
            upper, wide = lower[r, :], tan[r, :].astype(single)
            terms = (upper * scaled, upper, wide)
            return tuple(c + jnp.sum(t, 0, keepdims=True) for c, t in zip(carry, terms))

        parts = lax.fori_loop(0, rows // BLK, one, (jnp.zeros((1, D), single),) * 3)
        sums[...] = jnp.zeros_like(sums)
        for i in range(3):
            sums[i : i + 1, :] = parts[i]


def feed_forward(tok, tan, lines, weights, up_add):
    rows, count = tok.shape[0], FF // D
    wide = lambda where: pl.BlockSpec((D, D), lambda j: (0, where + j))
    one = lambda shape: pl.BlockSpec(shape, lambda j: (0, 0), pipeline_mode=pl.Buffered(1))
    line = pl.BlockSpec((1, 1, D), lambda j: (j, 0, 0))
    pair = pl.BlockSpec((D, 2 * D), lambda j: (0, j))
    return pl.pallas_call(
        feed_kernel,
        grid=(count,),
        in_specs=[one((rows, D)), one((rows, D)), one((16, D)), wide(0), line, wide(count)],
        out_specs=[one((rows, D)), one((rows, D)), pair, line, one((8, D))],
        out_shape=[
            jax.ShapeDtypeStruct((rows, D), single),
            jax.ShapeDtypeStruct((rows, D), single),
            jax.ShapeDtypeStruct((D, 2 * count * D), bfloat),
            jax.ShapeDtypeStruct((count, 1, D), single),
            jax.ShapeDtypeStruct((8, D), single),
        ],
        scratch_shapes=[
            pltpu.VMEM((rows, D), bfloat),
            pltpu.VMEM((rows, D), bfloat),
            pltpu.VMEM((rows, D), bfloat),
        ],
        compiler_params=params(60),
        cost_estimate=pl.CostEstimate(
            flops=12 * rows * D * D * count, bytes_accessed=count * 12 * MIB, transcendentals=2 * rows * D * count
        ),
        name="feed_forward",
    )(tok, tan, lines, weights, up_add, weights)


def gather_rows(meta, i, places, own, other, rows):
    spot = lax.broadcasted_iota(jnp.int32, (BLK, PART), 0) + i * BLK

    def part(k):
        mine = jnp.where(places[k] == spot, 1.0, 0.0).astype(bfloat)
        theirs = jnp.where(places[k + 3] == spot, 1.0, 0.0).astype(bfloat)
        return dot(mine, own[k]) + dot(theirs, other[k])

    low = meta[3, i]
    rows[...] = part(low)

    @pl.when(meta[4, i] > 1)
    def _():
        rows[...] += part(low + 1)


def column(line):
    return jnp.broadcast_to(line, (128, line.shape[1])).T[:, 0:1]


def return_rows(meta, at, places, values, mine, theirs, acc):
    b = lax.rem(at + 3, 6)
    acc[...] = jnp.zeros_like(acc)
    lane = lax.broadcasted_iota(jnp.int32, (PART, PART), 1)
    spots = column(places[b])

    def one(c, carry):
        hot = jnp.where(spots == lane + c * PART, 1.0, 0.0).astype(bfloat)
        r = pl.ds(pl.multiple_of(c * PART, PART), PART)
        acc[...] += dot(hot, values[r, :])
        return carry

    lax.fori_loop(meta[5, b], meta[6, b], one, 0)

    @pl.when(at < 3)
    def _():
        theirs[0] = acc[...].astype(bfloat)

    @pl.when(at >= 3)
    def _():
        mine[0] = acc[...].astype(bfloat)


def turn_lanes(values, cosine, sine):
    lane = lax.broadcasted_iota(jnp.int32, values.shape, 1)
    swapped = jnp.where(
        (lane & (ROT - 1)) < ROT // 2, pltpu.roll(values, 128 - ROT // 2, 1), pltpu.roll(values, ROT // 2, 1)
    )
    return values * cosine + swapped * sine


def of_head(values, h):
    lane = lax.broadcasted_iota(jnp.int32, values.shape, 1)
    return jnp.where((lane < HEAD_DIM) == (h % 2 == 0), values, jnp.zeros_like(values))


def lanes_of(h):
    return slice((h // 2) * 128, (h // 2) * 128 + 128)


def rows_of(h):
    return slice(h * HEAD_DIM, (h + 1) * HEAD_DIM)


def block_of(j):
    return pl.ds(pl.multiple_of(j * BLK, BLK), BLK)


def allowed_of(start, j, diagonal):
    row = lax.broadcasted_iota(jnp.int32, (BLK, BLK), 0)
    allowed = row + j * BLK >= start[...]
    if diagonal:
        allowed &= row <= lax.broadcasted_iota(jnp.int32, (BLK, BLK), 1)
    return allowed


def over_blocks(meta, i, step):
    def masked(j, carry):
        step(j, True, False)
        return carry

    def plain(j, carry):
        step(j, False, False)
        return carry

    lax.fori_loop(meta[0, i], meta[1, i], masked, 0)
    lax.fori_loop(meta[1, i], i, plain, 0)
    step(i, True, True)


def forward_kernel(
    meta,
    places,
    own,
    other,
    lines,
    weight_q,
    weight_k,
    weight_v,
    add,
    cosine,
    sine,
    start,
    kept,
    q,
    k,
    kt,
    v,
    context,
    logsum,
    mine,
    theirs,
    rows,
    keys,
    values,
    score,
    peak,
    total,
    acc,
    done,
    back_acc,
):
    step_at = pl.program_id(0)
    i = jnp.minimum(step_at, BLOCKS - 1)
    here = block_of(i)
    live = (step_at < BLOCKS) & (meta[2, i] > 0)

    @pl.when(live)
    def _():
        gather_rows(meta, i, places, own, other, rows)
        scaled, _ = norm_stats(rows[...])
        n = (scaled * lines[0:1, :] + lines[1:2, :]).astype(bfloat)
        kept[...] = rows[...].astype(bfloat)
        for s, weight in enumerate((weight_q, weight_k, weight_v)):
            mixed = dot(n, weight[...]) + add[:, s * HW : (s + 1) * HW]
            if s < 2:
                mixed = jnp.concatenate(
                    [
                        turn_lanes(mixed[:, p : p + 128], cosine[...], sine[...])
                        for p in range(0, HW, 128)
                    ],
                    1,
                )
            narrow = mixed.astype(bfloat)
            if s == 0:
                q[...] = narrow * HEAD_DIM ** (-0.5)
            elif s == 1:
                k[...] = narrow
                keys[here, :] = narrow
                kt[...] = narrow.T
            else:
                v[...] = narrow
                values[:, here] = narrow.T

        first = meta[0, i]
        queries = [of_head(q[:, lanes_of(h)], h) for h in range(NH)]
        peak[...] = jnp.full(peak.shape, -jnp.inf, single)

        def step(j, masked, diagonal):
            if masked:
                allowed = allowed_of(start, j, diagonal)
            for h in range(NH):
                s = against(keys[block_of(j), lanes_of(h)], queries[h])
                if masked:
                    s = jnp.where(allowed, s, -jnp.inf)
                score[h, block_of(j - first), :] = s
                peak[h] = jnp.maximum(peak[h], jnp.max(s.reshape(BLK // 8, 8, BLK), 0))

        over_blocks(meta, i, step)
        tops = [jnp.max(peak[h], 0, keepdims=True) for h in range(NH)]
        total[...] = jnp.zeros_like(total)
        acc[...] = jnp.zeros_like(acc)

        def gain(j, carry):
            for h in range(NH):
                p = jnp.exp(score[h, block_of(j - first), :] - tops[h])
                total[h] += jnp.sum(p.reshape(BLK // 8, 8, BLK), 0)
                acc[rows_of(h), :] += dot(values[rows_of(h), block_of(j)], p.astype(bfloat))
            return carry

        lax.fori_loop(first, i + 1, gain, 0)
        for h in range(NH):
            whole_sum = jnp.sum(total[h], 0, keepdims=True)
            acc[rows_of(h), :] = acc[rows_of(h), :] / whole_sum
            logsum[h : h + 1, :] = tops[h] + jnp.log(whole_sum)
        turned = acc[...].T
        context[...] = turned
        done[here, :] = turned.astype(bfloat)

    @pl.when(step_at >= BLOCKS)
    def _():
        return_rows(meta, jnp.maximum(step_at - BLOCKS, 0), places, done, mine, theirs, back_acc)


def columns():
    return [
        pl.BlockSpec((D, HW), lambda i, m, s=s: (0, 2 * s + m[7, 0]), pipeline_mode=pl.Buffered(1))
        for s in range(3)
    ]


def held(*shape):
    return pl.BlockSpec(shape, lambda i, m: (0,) * len(shape), pipeline_mode=pl.Buffered(1))


def tall_at(width):
    return pl.BlockSpec((BLK, width), lambda i, m: (jnp.minimum(i, m[8, 0]), 0))


def flat_at(height):
    return pl.BlockSpec((height, BLK), lambda i, m: (0, jnp.minimum(i, m[8, 0])))


def wide_at(width):
    return pl.BlockSpec((WIDE, width), lambda i, m: (jnp.clip(i - BLOCKS, 0, m[8, 0] // 2), 0))


def parts_at(first, width):
    return [
        pl.BlockSpec((1, PART, width), lambda i, m, f=f: (jnp.clip(i - f, 0, 2), 0, 0))
        for f in (first + 3, first)
    ]


def forward(meta, places, own, other, lines, weight, add, cosine, sine, start):
    out = lambda *shape: jax.ShapeDtypeStruct(shape, bfloat)
    return pl.pallas_call(
        forward_kernel,
        grid_spec=pltpu.PrefetchScalarGridSpec(
            num_scalar_prefetch=1,
            grid=(BLOCKS + 6,),
            in_specs=[
                held(6, 1, PART),
                held(3, PART, D),
                held(3, PART, D),
                held(16, D),
                *columns(),
                held(1, 3 * HW),
                tall_at(128),
                tall_at(128),
                flat_at(1),
            ],
            out_specs=[
                tall_at(D),
                tall_at(HW),
                tall_at(HW),
                flat_at(HW),
                tall_at(HW),
                tall_at(HW),
                flat_at(8),
                *parts_at(BLOCKS, HW),
            ],
            scratch_shapes=[
                pltpu.VMEM((BLK, D), single),
                pltpu.VMEM((TOTAL, HW), bfloat),
                pltpu.VMEM((HW, TOTAL), bfloat),
                pltpu.VMEM((NH, LONG, BLK), single),
                pltpu.VMEM((NH, 8, BLK), single),
                pltpu.VMEM((NH, 8, BLK), single),
                pltpu.VMEM((HW, BLK), single),
                pltpu.VMEM((TOTAL, HW), bfloat),
                pltpu.VMEM((PART, HW), single),
            ],
        ),
        out_shape=[
            out(TOTAL, D),
            out(TOTAL, HW),
            out(TOTAL, HW),
            out(HW, TOTAL),
            out(TOTAL, HW),
            jax.ShapeDtypeStruct((TOTAL, HW), single),
            jax.ShapeDtypeStruct((8, TOTAL), single),
            out(3, PART, HW),
            out(3, PART, HW),
        ],
        compiler_params=params(60),
        cost_estimate=pl.CostEstimate(
            flops=75 * 10**9, bytes_accessed=40 * MIB, transcendentals=NH * LONG * LONG // 2
        ),
        name="forward",
    )(meta, places, own, other, lines, weight, weight, weight, add, cosine, sine, start)


def backward_kernel(
    meta,
    places,
    own,
    other,
    weight_out,
    q,
    k,
    kt,
    v,
    start,
    context,
    logsum,
    kept,
    lines,
    weight_q,
    weight_k,
    weight_v,
    cosine,
    sine,
    mine,
    theirs,
    g_out,
    g_weight,
    g_add,
    g_gain,
    g_shift,
    rows,
    upper,
    dq,
    dk,
    dv,
    dqt,
    probs,
    slopes,
    out_acc,
    g_acc,
    lower,
    back_acc,
):
    step_at = pl.program_id(0)
    i = jnp.minimum(step_at, BLOCKS - 1)
    b = jnp.clip(step_at - BLOCKS, 0, STEPS - 1)

    @pl.when(step_at == 0)
    def _():
        for ref in (out_acc, g_acc, g_add, g_gain, g_shift):
            ref[...] = jnp.zeros_like(ref)

    @pl.when((step_at < BLOCKS) & (meta[2, i] > 0))
    def _():
        gather_rows(meta, i, places, own, other, rows)
        tangent = rows[...].astype(bfloat)
        upper[...] = against(tangent, weight_out[...]).astype(bfloat)
        out_acc[...] += over_rows(context[...].astype(bfloat), tangent)
        queries = [of_head(q[:, lanes_of(h)], h) for h in range(NH)]
        uppers = [of_head(upper[:, lanes_of(h)], h) for h in range(NH)]
        both = (upper[...].astype(single) * context[...]).T
        delta = [jnp.sum(both[rows_of(h), :], 0, keepdims=True) for h in range(NH)]
        dqt[...] = jnp.zeros_like(dqt)

        def step(j, masked, diagonal):
            r = block_of(j)
            if masked:
                allowed = allowed_of(start, j, diagonal)
            for h in range(NH):
                s = against(k[r, lanes_of(h)], queries[h])
                p = jnp.exp(s - logsum[h : h + 1, :])
                if masked:
                    p = jnp.where(allowed, p, 0.0)
                dp = against(v[r, lanes_of(h)], uppers[h])
                c = slice((h % 2) * BLK, (h % 2) * BLK + BLK)
                probs[h // 2, :, c] = p.astype(bfloat)
                slopes[h // 2, :, c] = (p * (dp - delta[h])).astype(bfloat)
            for g in range(NH // 2):
                c = slice(g * 128, g * 128 + 128)
                part_v = dot(probs[g], jnp.concatenate(uppers[2 * g : 2 * g + 2], 0))
                part_k = dot(slopes[g], jnp.concatenate(queries[2 * g : 2 * g + 2], 0))
                if diagonal:
                    dv[r, c] = part_v
                    dk[r, c] = part_k
                else:
                    dv[r, c] += part_v
                    dk[r, c] += part_k
                for h in (2 * g, 2 * g + 1):
                    e = slice((h % 2) * BLK, (h % 2) * BLK + BLK)
                    dqt[rows_of(h), :] += dot(kt[rows_of(h), r], slopes[g, :, e])

        over_blocks(meta, i, step)
        dq[block_of(i), :] = dqt[...].T * HEAD_DIM ** (-0.5)

    @pl.when((step_at >= BLOCKS) & (step_at < BLOCKS + STEPS) & (meta[2, 2 * b] > 0))
    def _():
        r = pl.ds(pl.multiple_of(b * WIDE, WIDE), WIDE)
        turned = []
        for ref in (dq, dk):
            for p in range(0, HW, 128):
                turned.append(turn_lanes(ref[r, p : p + 128], cosine[...], -sine[...]))
        turned.append(dv[r, :])
        mixed = jnp.concatenate(turned, 1).astype(bfloat)
        g_add[...] += jnp.sum(mixed.astype(single), 0, keepdims=True)
        up = (
            against(mixed[:, :HW], weight_q[...])
            + against(mixed[:, HW : 2 * HW], weight_k[...])
            + against(mixed[:, 2 * HW :], weight_v[...])
        )
        lower[r, :] = up.astype(bfloat)
        scaled, _ = norm_stats(kept[...].astype(single))
        g_gain[...] += jnp.sum(up * scaled, 0, keepdims=True)
        g_shift[...] += jnp.sum(up, 0, keepdims=True)
        normed = (scaled * lines[0:1, :] + lines[1:2, :]).astype(bfloat)
        g_acc[...] += over_rows(normed, mixed)

    @pl.when(step_at == BLOCKS + STEPS)
    def _():
        g_out[...] = out_acc[...].astype(bfloat)
        for s in range(3):
            g_weight[s] = g_acc[:, s * HW : (s + 1) * HW].astype(bfloat)

    @pl.when(step_at >= BLOCKS + STEPS)
    def _():
        return_rows(
            meta, jnp.maximum(step_at - BLOCKS - STEPS, 0), places, lower, mine, theirs, back_acc
        )


def backward(
    meta, places, own, other, q, k, kt, v, start, context, logsum, kept, lines, weight, cosine, sine
):
    return pl.pallas_call(
        backward_kernel,
        grid_spec=pltpu.PrefetchScalarGridSpec(
            num_scalar_prefetch=1,
            grid=(BLOCKS + STEPS + 6,),
            in_specs=[
                held(6, 1, PART),
                held(3, PART, D),
                held(3, PART, D),
                pl.BlockSpec((HW, D), lambda i, m: (m[7, 0], 3), pipeline_mode=pl.Buffered(1)),
                tall_at(HW),
                held(TOTAL, HW),
                held(HW, TOTAL),
                held(TOTAL, HW),
                flat_at(1),
                tall_at(HW),
                flat_at(8),
                wide_at(D),
                held(16, D),
                *columns(),
                wide_at(128),
                wide_at(128),
            ],
            out_specs=[
                *parts_at(BLOCKS + STEPS, D),
                held(HW, D),
                held(3, D, HW),
                held(1, 3 * HW),
                held(1, D),
                held(1, D),
            ],
            scratch_shapes=[
                pltpu.VMEM((BLK, D), single),
                pltpu.VMEM((BLK, HW), bfloat),
                pltpu.VMEM((TOTAL, HW), single),
                pltpu.VMEM((TOTAL, HW), single),
                pltpu.VMEM((TOTAL, HW), single),
                pltpu.VMEM((HW, BLK), single),
                pltpu.VMEM((NH // 2, BLK, 2 * BLK), bfloat),
                pltpu.VMEM((NH // 2, BLK, 2 * BLK), bfloat),
                pltpu.VMEM((HW, D), single),
                pltpu.VMEM((D, 3 * HW), single),
                pltpu.VMEM((TOTAL, D), bfloat),
                pltpu.VMEM((PART, D), single),
            ],
        ),
        out_shape=[
            jax.ShapeDtypeStruct((3, PART, D), bfloat),
            jax.ShapeDtypeStruct((3, PART, D), bfloat),
            jax.ShapeDtypeStruct((HW, D), bfloat),
            jax.ShapeDtypeStruct((3, D, HW), bfloat),
            jax.ShapeDtypeStruct((1, 3 * HW), single),
            jax.ShapeDtypeStruct((1, D), single),
            jax.ShapeDtypeStruct((1, D), single),
        ],
        compiler_params=params(60),
        cost_estimate=pl.CostEstimate(
            flops=90 * 10**9, bytes_accessed=40 * MIB, transcendentals=NH * LONG * LONG // 2
        ),
        name="backward",
    )(
        meta,
        places,
        own,
        other,
        weight,
        q,
        k,
        kt,
        v,
        start,
        context,
        logsum,
        kept,
        lines,
        weight,
        weight,
        weight,
        cosine,
        sine,
    )


def placed_rows(place, moved):
    lane = lax.broadcasted_iota(jnp.int32, (BLK, moved.shape[0]), 1)
    return dot(jnp.where(column(place[...]) == lane, 1.0, 0.0).astype(bfloat), moved[...])


def close_kernel(place, moved, weight, lines, tok, tan, feed, feed_back, out, lower):
    context = placed_rows(place, moved).astype(bfloat)
    attended = dot(context, weight[...]) + lines[4:5, :]
    rows = tok[...].astype(single)
    out[...] = (rows + attended + (feed[...] + lines[5:6, :])).astype(bfloat)
    scaled, factor = norm_stats(rows)
    second = lower_norm(feed_back[...], scaled, factor, lines[2:3, :])
    lower[...] = tan[...].astype(single) + second


def close(place, moved, weights, lines, tok, tan, feed, feed_back):
    rows = tok.shape[0]
    tall = lambda width: pl.BlockSpec((BLK, width), lambda i: (i, 0))
    return pl.pallas_call(
        close_kernel,
        grid=(rows // BLK,),
        in_specs=[
            pl.BlockSpec((1, BLK), lambda i: (0, i)),
            whole(moved.shape),
            pl.BlockSpec((D, D), lambda i: (0, 3)),
            whole((16, D)),
            tall(D),
            tall(D),
            tall(D),
            tall(D),
        ],
        out_specs=[tall(D), tall(D)],
        out_shape=[
            jax.ShapeDtypeStruct((rows, D), bfloat),
            jax.ShapeDtypeStruct((rows, D), single),
        ],
        compiler_params=params(60),
        cost_estimate=pl.CostEstimate(
            flops=12 * 10**9, bytes_accessed=12 * MIB, transcendentals=0
        ),
        name="close",
    )(place, moved, weights, lines, tok, tan, feed, feed_back)


def finish_kernel(place, moved, lines, tok, lower, out):
    scaled, factor = norm_stats(tok[...].astype(single))
    upper = placed_rows(place, moved)
    out[...] = (lower[...] + lower_norm(upper, scaled, factor, lines[0:1, :])).astype(bfloat)


def finish(place, moved, lines, tok, lower):
    rows = tok.shape[0]
    tall = lambda width: pl.BlockSpec((BLK, width), lambda i: (i, 0))
    return pl.pallas_call(
        finish_kernel,
        grid=(rows // BLK,),
        in_specs=[
            pl.BlockSpec((1, BLK), lambda i: (0, i)),
            whole(moved.shape),
            whole((16, D)),
            tall(D),
            tall(D),
        ],
        out_specs=tall(D),
        out_shape=jax.ShapeDtypeStruct((rows, D), bfloat),
        compiler_params=params(60),
        cost_estimate=pl.CostEstimate(
            flops=2 * rows * D * moved.shape[0], bytes_accessed=12 * MIB, transcendentals=0
        ),
        name="finish",
    )(place, moved, lines, tok, lower)


def gather_all(x):
    return lax.all_gather(x, "dp", axis=0, tiled=True)


def body(
    tokens,
    cotangent,
    loss_mask,
    bucket_perm,
    short_lengths,
    row_owner,
    row_slot,
    first_gain,
    first_shift,
    second_gain,
    second_shift,
    project_weight,
    project_bias,
    output_weight,
    output_bias,
    up_weight,
    up_bias,
    down_weight,
    down_bias,
):
    devices = lax.axis_size("dp")
    me = lax.axis_index("dp")
    core = me % 2
    chip = me // 2
    rows = tokens.shape[0]
    share = LONG // devices // 4
    room = 3 * share
    long_count = devices // 4
    swap = [(i, i ^ 1) for i in range(devices)]

    def exchange(x):
        return lax.ppermute(x, "dp", swap)

    chips = devices // 2
    across = math.isqrt(chips // 4)
    sizes = {"core": 2, "x": across, "y": across, "z": 4}
    strides = {"core": 1, "x": 2, "y": 2 * across, "z": 2 * across * across}

    def shifted(x, name, shift):
        n, stride = sizes[name], strides[name]
        hop = []
        for d in range(devices):
            c = (d // stride) % n
            hop.append((d, d + ((c + shift) % n - c) * stride))
        return lax.ppermute(x, "dp", hop)

    def after(x, *others):
        return lax.optimization_barrier((x, *others))[0]

    def reduce_along(x, name, dim, kind=bfloat, late=None):
        n = sizes[name]
        at = (me // strides[name]) % n
        total = lax.dynamic_index_in_dim(x, at, dim, keepdims=False).astype(single)
        for shift in range(1, n):
            sent = lax.dynamic_index_in_dim(x, (at + shift) % n, dim, keepdims=False)
            got = shifted(sent, name, shift)
            total = total + (got if late is None else after(got, late)).astype(single)
        return total.astype(kind)

    piece = D // devices
    fours = FF // D
    count = jnp.sum(loss_mask)
    count_column = jnp.where(
        jnp.arange(piece) == 0, count // 256, jnp.where(jnp.arange(piece) == 1, count % 256, 0)
    )
    small = jnp.concatenate(
        [
            jnp.stack([first_gain, first_shift, second_gain, second_shift, output_bias, down_bias], 1),
            project_bias.reshape(3, piece).T,
            up_bias.reshape(piece, fours),
            count_column[:, None].astype(single),
        ],
        1,
    )
    small = jnp.pad(small, ((0, 0), (0, 128 - small.shape[1])))
    spread = jnp.arange(devices, dtype=jnp.int32)
    bucket = jnp.sum(jnp.where(bucket_perm[None, :] == row_owner[:, None], spread[None, :], 0), -1)
    hot = (row_owner[:, None] == spread[None, :]).astype(bfloat)
    line = jnp.arange(rows, dtype=jnp.int32)
    before = (line[None, :] < line[:, None]).astype(bfloat)
    rank = jnp.sum(dot(before, hot) * hot.astype(single), -1).astype(jnp.int32)
    is_long = bucket < long_count
    short = bucket - long_count
    third = jnp.where(is_long, 0, short % 3)
    to_chip = jnp.where(is_long, 2 * bucket, 2 * (short // 3) + 1)
    held = jnp.where(is_long, 2 * share, share)
    to_core = rank // held
    place = (2 * to_chip + to_core) * room + third * share + rank % held
    slot = third * SHORT_TOK + row_slot
    spots = jnp.arange(devices * room, dtype=jnp.int32)
    slot_at = jnp.sum(
        jnp.where(place[None, :] == spots[:, None], slot[None, :] + 1, 0), -1
    ) - 1
    slot_code = jnp.concatenate([(slot_at + 1) // 256, (slot_at + 1) % 256])
    slot_code = slot_code.astype(single).reshape(piece, 2 * devices * room // piece)
    first_all = gather_all(
        jnp.concatenate([project_weight, output_weight, small, slot_code], 1).astype(bfloat)
    )
    lines = first_all[:, 4 * D : 4 * D + 16].astype(single).T
    project_add = lines[6:9].reshape(3, devices, piece).transpose(1, 0, 2).reshape(1, 3, 2, HW)
    project_add_half = lax.dynamic_index_in_dim(project_add, core, 2, keepdims=False).reshape(
        1, 3 * HW
    )
    up_add = lines[9:13].reshape(fours, 1, D)
    counts = lines[13].reshape(devices, piece)
    scale = lax.rsqrt(jnp.sum(counts[:, 0]) * 256.0 + jnp.sum(counts[:, 1]))

    sender = (place[None, :] == spots[:, None]).astype(bfloat)
    place_line = place[None]

    def swap_all(x):
        return lax.all_to_all(x, "dp", split_axis=0, concat_axis=0, tiled=True)

    def outgoing(x):
        return dot(sender, x).astype(bfloat).reshape(devices, room, D)

    def arrange(moved):
        return moved.reshape(devices, 3, share, D).transpose(1, 0, 2, 3).reshape(3, PART, D)

    def send_back(x):
        moved = x.reshape(3, devices, share, D).transpose(1, 0, 2, 3).reshape(devices, room, D)
        return swap_all(moved).reshape(devices * room, D)

    code = first_all[:, 4 * D + 128 :].reshape(devices, 2, chips, 2 * room)
    code = lax.dynamic_index_in_dim(code, chip, 2, keepdims=False).astype(jnp.int32)
    slot_recv = (code[:, 0] * 256 + code[:, 1] - 1).reshape(devices, 2, 3, share)
    slot_recv = slot_recv.transpose(1, 2, 0, 3).reshape(2, 3, PART)
    slot_recv = jnp.where(core == 0, slot_recv, slot_recv[::-1])
    places = slot_recv.reshape(6, 1, PART)

    self_long = chip % 2 == 0
    lengths = lax.dynamic_slice_in_dim(short_lengths, 3 * (chip // 2), 3, 0)
    ends = jnp.cumsum(lengths, -1)
    at = jnp.arange(TOTAL, dtype=jnp.int32).reshape(3, SHORT_TOK)
    inside = jnp.arange(SHORT_TOK, dtype=jnp.int32)
    begun = jnp.max(
        jnp.where(ends[:, None, :] <= inside[None, :, None], ends[:, None, :], 0), -1
    )
    start = jnp.where(self_long, 0, begun + at - inside[None, :]).reshape(TOTAL)
    position = jnp.arange(TOTAL, dtype=jnp.int32) - start
    blocks = jnp.arange(TOTAL // BLK, dtype=jnp.int32)
    low_start = start[::BLK] // BLK
    high_start = (start[BLK - 1 :: BLK] + BLK - 1) // BLK
    zero = jnp.zeros_like(blocks)
    meta = jnp.stack(
        [
            low_start,
            jnp.minimum(blocks, jnp.maximum(low_start, high_start)),
            jnp.where(self_long & (blocks >= LONG // BLK), 0, 1),
            jnp.where(self_long, 0, blocks // (SHORT_TOK // BLK)),
            jnp.where(self_long, 2, 1) + zero,
            jnp.where(self_long, 0, 2 * (blocks % 3)),
            jnp.where(self_long, jnp.where(blocks % 3 == 2, 0, 4), 2 * (blocks % 3) + 2),
            core + zero,
            jnp.where(self_long, LONG // BLK, BLOCKS) - 1 + zero,
        ]
    ).astype(jnp.int32)
    lane = jnp.arange(128, dtype=jnp.int32) % HEAD_DIM
    freq = 10000.0 ** (-2.0 * (lane % (ROT // 2)).astype(single) / ROT)
    phase = position.astype(single)[:, None] * freq[None, :]
    turning = (lane < ROT)[None, :]
    cosine = jnp.where(turning, jnp.cos(phase), 1.0)
    sine = jnp.where(turning, jnp.sin(phase) * jnp.where(lane < ROT // 2, -1.0, 1.0)[None, :], 0.0)
    starts = start.reshape(1, TOTAL)

    tangent = cotangent * loss_mask.astype(bfloat)[:, None]
    tokens_out = outgoing(tokens)
    tangent_out = outgoing(tangent)
    tokens_out, late_up, late_down = lax.optimization_barrier((tokens_out, up_weight, down_weight))
    up_mixed = late_up.astype(bfloat).reshape(piece, D, fours).transpose(0, 2, 1)
    down_mixed = late_down.astype(bfloat).reshape(piece, fours, D)
    feed_weights = gather_all(
        jnp.concatenate([up_mixed.reshape(piece, FF), down_mixed.reshape(piece, FF)], 1)
    )
    tokens_in = swap_all(tokens_out)
    tokens_in, places, meta, cosine, sine, starts, tangent_out = lax.optimization_barrier(
        (tokens_in, places, meta, cosine, sine, starts, tangent_out)
    )
    own = arrange(tokens_in)
    other = exchange(own)
    kept, q, k, kt, v, context, logsum, context_mine, context_theirs = forward(
        meta,
        places,
        own,
        other,
        lines,
        first_all,
        project_add_half,
        cosine,
        sine,
        starts,
    )

    tangent_in = swap_all(after(tangent_out, context_mine))

    mine, theirs = context_mine, exchange(context_theirs)
    context_out = jnp.concatenate(
        [jnp.where(core == 0, mine, theirs), jnp.where(core == 0, theirs, mine)], -1
    )
    feed, feed_back, wide, up_add_grad, sums = feed_forward(
        after(tokens, context_out), tangent, lines, feed_weights, up_add
    )
    wide_sum = lax.psum_scatter(wide, "dp", scatter_dimension=0, tiled=True).astype(single)

    context_moved = send_back(context_out)

    upper_own = arrange(after(tangent_in, feed))
    upper_other = exchange(upper_own)
    lower_mine, lower_theirs, *project_parts = backward(
        meta,
        places,
        upper_own,
        upper_other,
        q,
        k,
        kt,
        v,
        starts,
        context,
        logsum,
        kept,
        lines,
        first_all,
        cosine,
        sine,
    )
    lower_sum = (
        lower_mine.astype(single) + exchange(lower_theirs).astype(single)
    ).astype(bfloat)
    upper_moved = send_back(lower_sum)
    output_half_grad, project_grad_half, project_add_half_grad, gain_one_grad, shift_one_grad = (
        project_parts
    )

    block_out, lower_two = close(
        place_line,
        after(context_moved, lower_sum),
        first_all,
        lines,
        tokens,
        tangent,
        feed,
        feed_back,
    )

    def pair_up(one, two):
        return jnp.where(
            core == 0, jnp.concatenate([one, two], -1), jnp.concatenate([two, one], -1)
        )

    add_half = project_add_half_grad.reshape(3, HW)
    project_add_grad = pair_up(add_half, jnp.zeros_like(add_half)).reshape(devices, 3, piece)
    vectors = jnp.concatenate(
        [
            gain_one_grad,
            shift_one_grad,
            sums[:3],
            project_add_grad.transpose(1, 0, 2).reshape(3, D),
            up_add_grad.reshape(fours, D),
            jnp.zeros((4, D), single),
        ],
        0,
    )
    def over_chips(x):
        return x.reshape((4, across, across) + x.shape[1:])

    extra = vectors.reshape(16, devices, piece).transpose(1, 0, 2).reshape(devices, 1, 16 * piece)
    extra = jnp.pad(extra, ((0, 0), (0, 7), (0, D - 16 * piece))).astype(bfloat)
    empty = jnp.zeros_like(output_half_grad)
    output_grad = jnp.where(
        core == 0,
        jnp.concatenate([output_half_grad, empty], 0),
        jnp.concatenate([empty, output_half_grad], 0),
    )
    output_part = jnp.concatenate([output_grad.reshape(devices, piece, D), extra], 1)
    output_half = reduce_along(output_part.reshape(chips, 2, piece + 8, D), "core", 1)
    by_core = project_grad_half.reshape(3, chips, 2, piece, HW)
    for_me = lax.dynamic_index_in_dim(by_core, core, 2, keepdims=False)
    for_other = lax.dynamic_index_in_dim(by_core, 1 - core, 2, keepdims=False)
    projects = pair_up(for_me, exchange(for_other))
    narrow = over_chips(
        jnp.concatenate([projects[0], projects[1], projects[2], output_half], 1)
    )
    cut = narrow.shape[3] // 16 * 8
    one = reduce_along(narrow[..., :cut, :], "x", 2, late=block_out)
    two = reduce_along(narrow[..., cut:, :], "y", 1, late=block_out)
    one = reduce_along(one, "y", 1)
    two = reduce_along(two, "x", 1)
    wide_sum = wide_sum.reshape(piece, fours, 2, D)
    up_sum = wide_sum[:, :, 0].transpose(0, 2, 1).reshape(piece, FF)
    down_sum = wide_sum[:, :, 1].reshape(fours * piece, D)
    upper_moved, up_sum, down_sum = lax.optimization_barrier(
        (upper_moved, up_sum * scale, down_sum * scale)
    )
    tokens_grad = finish(place_line, upper_moved, lines, tokens, lower_two)
    narrow = reduce_along(jnp.concatenate([one, two], 1), "z", 0, single, tokens_grad) * scale
    project_sum = narrow[: 3 * piece].reshape(3, piece, D).transpose(1, 0, 2).reshape(piece, 3 * D)
    output_sum = narrow[3 * piece : 4 * piece]
    vector_sum = narrow[4 * piece, : 16 * piece].reshape(16, piece)
    return (
        block_out,
        tokens_grad,
        vector_sum[0],
        vector_sum[1],
        vector_sum[2],
        vector_sum[3],
        project_sum,
        vector_sum[5:8].reshape(3 * piece),
        output_sum,
        vector_sum[4],
        up_sum,
        vector_sum[8:12].T.reshape(fours * piece),
        down_sum,
        vector_sum[4],
    )


def solution(mesh):
    tall, flat = P("dp", None), P("dp")
    return jax.shard_map(
        body,
        mesh=mesh,
        in_specs=(
            tall,
            tall,
            flat,
            P(),
            P(),
            flat,
            flat,
            flat,
            flat,
            flat,
            flat,
            tall,
            flat,
            tall,
            flat,
            tall,
            flat,
            tall,
            flat,
        ),
        out_specs=(
            tall,
            tall,
            flat,
            flat,
            flat,
            flat,
            tall,
            flat,
            tall,
            flat,
            tall,
            flat,
            tall,
            flat,
        ),
        check_vma=False,
    )
```
